512 devices in a mesh: dp: 32 (over x, y, core), tensor: 16 (over z).
Axes of the slice: x: 4, y: 4, z: 16, core: 2. Of those that a mesh axis runs over, the one named last changes fastest.
Arguments:
- queries: bfloat16 [1024, 64, 128], P('dp', 'tensor'), parts along dimension 0, may hold values from -80 to 80
- new_key: bfloat16 [1024, 8, 128], P('dp'), parts along dimension 0, may hold values from -4 to 4
- new_value: bfloat16 [1024, 8, 128], P('dp'), parts along dimension 0, may hold values from -6 to 6
- key_codes: int32 [1024, 16, 2048], P('dp', 'tensor'), parts along dimension 0, may hold values from 0 to 65280
- key_scales: int32 [1024, 16, 64], P('dp', 'tensor'), parts along dimension 0, may hold values from 16 to 127
- value_codes: int32 [1024, 16, 2048], P('dp', 'tensor'), parts along dimension 0, may hold values from 0 to 65280
- value_scales: int32 [1024, 16, 64], P('dp', 'tensor'), parts along dimension 0, may hold values from 16 to 127
- lengths: int32 [1024], P('dp'), parts along dimension 0, may hold values from 1 to 128, 2048 in all
- out_codes: int32 [2048, 8192], P(None, 'tensor'), may hold values from 0 to 65280
- out_scales: int32 [64, 8192], P(None, 'tensor'), may hold values from 16 to 127
Outputs:
- projected: bfloat16 [1024, 8192], P('dp', 'tensor'), parts along dimension 0
The draws below stay inside these ranges and needn't reach their ends.
There are 32 independent parts, one for each index of `dp`. The reference program is written for one: setup_inputs(seed, part) draws one part's arguments, and reference() takes and returns one part's arrays. A program takes and returns all parts, laid end to end along the dimension named above; an argument that names none is the same for every part. Nothing has to cross between parts.
Inputs may be any that keep to these rules, and one draw needn't show every extreme that they name: Each row attends to its cached tokens 0 to lengths - 1 and to its new token, which stands at position lengths; the largest length is 128 in every draw. The sum of the lengths is 2048 within each decode group's 32 rows, not over the whole array of all groups.
All inputs are finite; a program needn't handle non-finite values.
Results may differ from the reference program's by a relative error of at most 0.012.
Values may be sent and summed in bfloat16 or wider, within the bound.
No kernel may reach another device: no remote copies, remote signals or barrier semaphores. Data moves between devices by JAX's collectives and lax.ppermute only.
A program may use at most 128 MiB of HBM per device.

```python
import math
import jax
import jax.numpy as jnp
import numpy as np
from jax import lax

D = 8192
H = 64
KVH = 8
HD = 128
G = 128
CTX = 128
ROWS = 32


def common_key(key):
    return jnp.clip(jax.random.normal(key, (ROWS, KVH, HD), jnp.float32), -4.0, 4.0)


def draw_new_key(key, part):
    shared = common_key(key)
    return shared.astype(jnp.bfloat16)


def draw_queries(key, part):
    key = jax.random.fold_in(key, 12)
    drawn = jnp.clip(jax.random.normal(key, (ROWS, H, HD), jnp.float32), -6.0, 6.0)
    return drawn.astype(jnp.bfloat16)


def touch_ends(values, key, smallest, largest):
    longest = values.shape.index(max(values.shape))
    spots = []
    for shift in (0, 1):
        where = [jax.random.randint(jax.random.fold_in(key, axis), (), 0, length) for axis, length in enumerate(values.shape)]
        where[longest] = (where[longest] + shift) % values.shape[longest]
        spots.append(tuple(where))
    return values.at[spots[0]].set(smallest).at[spots[1]].set(largest)


def length_profile(number_of, total, bound, lean):
    loads = [(1 << 20) // math.isqrt(rank ** lean) + 1 for rank in range(2, number_of + 1)]
    surplus, holding = total - bound - (number_of - 1), [1] * (number_of - 1)
    while surplus > 0:
        movable = [i for i in range(number_of - 1) if holding[i] < bound]
        pool, budget = sum([loads[i] for i in movable]), surplus
        for i in movable:
            addition = min(bound - holding[i], max(1, budget * loads[i] // pool), surplus)
            holding[i] = holding[i] + addition
            surplus = surplus - addition
    return np.array([bound] + holding)


def ragged_sizes(own_key, amount, total, bound, lean):
    if amount == 2:
        one = jax.random.randint(own_key, (), max(1, total - bound), min(bound, total - 1) + 1)
        return jnp.stack([one, total - one])
    sizes = jnp.asarray(length_profile(amount, total, bound, lean), jnp.int32)
    pairs = (amount - 1) // 2
    source_of, receiver = sizes[1:1 + 2 * pairs:2], sizes[2:2 + 2 * pairs:2]
    room = jnp.minimum(source_of - 1, bound - receiver)
    moved = jax.random.randint(jax.random.fold_in(own_key, 1), (pairs,), 0, 1 << 20) % (room + 1)
    sizes = sizes.at[1:1 + 2 * pairs:2].set(source_of - moved).at[2:2 + 2 * pairs:2].set(receiver + moved)
    return sizes[jax.random.permutation(jax.random.fold_in(own_key, 2), amount)]


def centred(key, extent, width, limit, kind=jnp.bfloat16):
    values = jax.random.normal(key, extent, jnp.float32) * width
    return jnp.minimum(jnp.maximum(values, -limit), limit).astype(kind)


def setup_inputs(seed: int = 0, part: int = 0) -> dict:
    key_of = jax.random.split(jax.random.key(seed), 11)
    part_splits = jax.random.split(jax.random.fold_in(key_of[10], part), 11)
    return {
        "queries": draw_queries(jax.random.fold_in(jax.random.fold_in(key_of[10], part), 71), part),
        "new_key": draw_new_key(jax.random.fold_in(jax.random.fold_in(key_of[10], part), 71), part),
        "new_value": centred(part_splits[2], (ROWS, KVH, HD), 1.0, 6.0),
        "key_codes": touch_ends(jax.random.randint(part_splits[3], (ROWS, 2 * KVH, CTX * HD // 8), 0, 65281), jax.random.fold_in(part_splits[3], 1), 0, 65280).astype(jnp.int32),
        "key_scales": touch_ends(jax.random.randint(part_splits[4], (ROWS, 2 * KVH, CTX // 2), 16, 128), jax.random.fold_in(part_splits[4], 1), 16, 127).astype(jnp.int32),
        "value_codes": touch_ends(jax.random.randint(part_splits[5], (ROWS, 2 * KVH, CTX * HD // 8), 0, 65281), jax.random.fold_in(part_splits[5], 1), 0, 65280).astype(jnp.int32),
        "value_scales": touch_ends(jax.random.randint(part_splits[6], (ROWS, 2 * KVH, CTX // 2), 16, 128), jax.random.fold_in(part_splits[6], 1), 16, 127).astype(jnp.int32),
        "lengths": ragged_sizes(part_splits[7], ROWS, ROWS * CTX // 2, CTX, 2).astype(jnp.int32),
        "out_codes": touch_ends(jax.random.randint(key_of[8], (D // 4, D), 0, 65281), jax.random.fold_in(key_of[8], 1), 0, 65280).astype(jnp.int32),
        "out_scales": touch_ends(jax.random.randint(key_of[9], (D // G, D), 16, 128), jax.random.fold_in(key_of[9], 1), 16, 127).astype(jnp.int32),
    }


rope_base = 10000.0
neg_floor = -1.0e30
code_offset = 7.5
cache_step = 256.0
weight_step = 8192.0


def unpack_codes(code_words):
    shifts = 4 * jnp.arange(4, dtype=jnp.int32)
    nibbles = jnp.bitwise_and(jnp.right_shift(code_words[..., None], shifts), 15)
    return nibbles.reshape(code_words.shape[:-1] + (code_words.shape[-1] * 4,)).astype(jnp.float32) - code_offset


def unpack_rows(code_words, scale_rows):
    shifts = 4 * jnp.arange(4, dtype=jnp.int32)
    nibbles = jnp.bitwise_and(jnp.right_shift(code_words[:, None, :], shifts[None, :, None]), 15)
    row_total = code_words.shape[0] * 4
    columns = code_words.shape[1]
    levels = nibbles.reshape(row_total, columns).astype(jnp.float32) - code_offset
    group_rows = row_total // scale_rows.shape[0]
    spread = jnp.broadcast_to(scale_rows.astype(jnp.float32)[:, None, :], (scale_rows.shape[0], group_rows, columns)).reshape(row_total, columns)
    return (levels * spread / weight_step).astype(jnp.bfloat16)


def rope_tables(positions, head_width):
    half_width = head_width // 2
    frequency = rope_base ** (-(jnp.arange(half_width, dtype=jnp.float32) * 2.0 / head_width))
    angles = positions.astype(jnp.float32)[..., None] * frequency
    return jnp.cos(angles), jnp.sin(angles)


def rotate(vectors, cosine_table, sine_table):
    half_width = vectors.shape[-1] // 2
    first_half = vectors[..., :half_width]
    second_half = vectors[..., half_width:]
    return jnp.concatenate([first_half * cosine_table - second_half * sine_table, second_half * cosine_table + first_half * sine_table], axis=-1)


def sylvester(table_order):
    entries = jnp.arange(table_order, dtype=jnp.int32)
    intersection = jnp.bitwise_and(entries[:, None], entries[None, :])
    parity = jnp.zeros((table_order, table_order), jnp.int32)
    for bit_index in range(max(table_order.bit_length() - 1, 0)):
        parity = parity + jnp.bitwise_and(jnp.right_shift(intersection, bit_index), 1)
    return 1.0 - 2.0 * jnp.bitwise_and(parity, 1).astype(jnp.float32)


def half_partial(query_block, code_words, scale_block, value_words, value_scale, lengths, half_index, key_new, value_new, include):
    row_count, token_count = scale_block.shape
    head_width = query_block.shape[-1]
    key_levels = unpack_codes(code_words.reshape(row_count, token_count, head_width // 4))
    positions = half_index * token_count + jnp.arange(token_count, dtype=jnp.int32)
    cosine_table, sine_table = rope_tables(positions, head_width)
    key_block = rotate(key_levels * scale_block.astype(jnp.float32)[..., None] / cache_step, cosine_table[None], sine_table[None]).astype(jnp.bfloat16)
    value_levels = unpack_codes(value_words.reshape(row_count, token_count, head_width // 4))
    value_block = (value_levels * value_scale.astype(jnp.float32)[..., None] / cache_step).astype(jnp.bfloat16)
    factor = head_width ** -0.5
    scores = jnp.einsum("rqd,rkd->rqk", query_block.astype(jnp.float32), key_block.astype(jnp.float32)) * factor
    new_score = jnp.einsum("rqd,rd->rq", query_block.astype(jnp.float32), key_new.astype(jnp.float32)) * factor
    live_mask = (positions[None, :] < lengths[:, None])[:, None, :]
    scores = jnp.where(live_mask, scores, neg_floor)
    row_top = jnp.maximum(jnp.max(scores, axis=-1), jnp.where(include, new_score, neg_floor))
    weights = jnp.where(live_mask, jnp.exp(scores - row_top[..., None]), 0.0).astype(jnp.bfloat16)
    new_weight = jnp.where(include, jnp.exp(new_score - row_top), 0.0).astype(jnp.bfloat16)
    weight_sum = jnp.sum(weights.astype(jnp.float32), axis=-1) + new_weight.astype(jnp.float32)
    weighted = jnp.einsum("rqk,rkd->rqd", weights.astype(jnp.float32), value_block.astype(jnp.float32))
    weighted = weighted + new_weight.astype(jnp.float32)[..., None] * value_new.astype(jnp.float32)[:, None, :]
    return row_top, weight_sum, weighted


def combine(first, second):
    joint_top = jnp.maximum(first[0], second[0])
    first_factor = jnp.exp(first[0] - joint_top)
    second_factor = jnp.exp(second[0] - joint_top)
    numerator = first[2] * first_factor[..., None] + second[2] * second_factor[..., None]
    denominator = first[1] * first_factor + second[1] * second_factor
    return (numerator / denominator[..., None]).astype(jnp.bfloat16)


def reference(queries, new_key, new_value, key_codes, key_scales, value_codes, value_scales, lengths, out_codes, out_scales):
    row_count, head_count, head_width = queries.shape
    kv_count = new_key.shape[1]
    group_size = head_count // kv_count
    query_cos, query_sin = rope_tables(lengths, head_width)
    query_rot = rotate(queries.astype(jnp.float32), query_cos[:, None, :], query_sin[:, None, :]).astype(jnp.bfloat16)
    key_now = rotate(new_key.astype(jnp.float32), query_cos[:, None, :], query_sin[:, None, :]).astype(jnp.bfloat16)
    blocks = []
    for kv_index in range(kv_count):
        query_block = query_rot[:, kv_index * group_size:(kv_index + 1) * group_size]
        lower = half_partial(query_block, key_codes[:, 2 * kv_index], key_scales[:, 2 * kv_index], value_codes[:, 2 * kv_index], value_scales[:, 2 * kv_index], lengths, 0, key_now[:, kv_index], new_value[:, kv_index], True)
        upper = half_partial(query_block, key_codes[:, 2 * kv_index + 1], key_scales[:, 2 * kv_index + 1], value_codes[:, 2 * kv_index + 1], value_scales[:, 2 * kv_index + 1], lengths, 1, key_now[:, kv_index], new_value[:, kv_index], False)
        blocks.append(combine(lower, upper))
    attended = jnp.concatenate(blocks, axis=1)
    within_head = jnp.einsum("rhe,de->rhd", attended.astype(jnp.float32), sylvester(head_width), precision=lax.Precision.HIGHEST)
    across_head = jnp.einsum("gh,rhd->rgd", sylvester(head_count), within_head, precision=lax.Precision.HIGHEST)
    rotated = (across_head * (head_count * head_width) ** -0.5).astype(jnp.bfloat16)
    weight = unpack_rows(out_codes, out_scales)
    flat_rows = rotated.reshape(row_count, head_count * head_width)
    return jnp.dot(flat_rows, weight, preferred_element_type=jnp.float32).astype(jnp.bfloat16)
```

```python
import functools

import jax
import jax.numpy as jnp
import numpy as np
from jax import lax
from jax.experimental import pallas as pl
from jax.experimental.pallas import tpu as pltpu
from jax.sharding import PartitionSpec as P

rope_base = 10000.0
neg_floor = -1e30
code_offset = 7.5
cache_step = 256.0
weight_step = 8192.0

rows = 32
head_width = 128
local_heads = 4
half_tokens = 64
chunk = 8
nt = (((1,), (1,)), ((), ()))


def rope_angles(positions):
    frequency = rope_base ** (-(np.arange(64) * 2.0 / head_width))
    return np.asarray(positions, np.float64)[..., None] * frequency


def key_tables():
    lane = np.arange(512)
    plane, low, word = lane // 128, lane % 128 // 32, lane % 32
    entry = 4 * word + plane
    position = 4 * np.arange(16)[:, None] + low[None, :]
    out = []
    for half in range(2):
        angle = rope_angles(np.arange(128))[half * half_tokens + position, (entry % 64)[None, :]]
        sign = np.where(entry < 64, -1.0, 1.0)
        scale = head_width**-0.5 / cache_step
        out.append(np.stack([np.cos(angle) * scale, np.sin(angle) * sign * scale]))
    return np.stack(out).astype(np.float32)


def query_table():
    angle = rope_angles(np.arange(136))
    return np.concatenate([np.cos(angle), np.cos(angle), -np.sin(angle), np.sin(angle)], -1).astype(
        np.float32
    )


def selector():
    lane = np.arange(512)
    entry = 4 * (lane % 32) + lane // 128
    return (np.arange(128)[:, None] == entry[None, :]).astype(np.float32)


def swap_words():
    lane = np.arange(128)
    return (lane[:, None] == (lane ^ 16)[None, :]).astype(np.float32)


def token_spread():
    return (np.arange(64)[:, None] % 4 == np.arange(128)[None, :] // 32).astype(np.float32)


def hadamard_pair():
    column = np.arange(256)
    target = (column // 32 % 2) * 128 + 4 * (column % 32) + column // 64
    both = np.arange(256)[:, None] & target[None, :]
    parity = np.zeros_like(both)
    for bit in range(8):
        parity ^= both >> bit & 1
    return (1.0 - 2.0 * parity).astype(np.float32)


def iota(shape, dim):
    return lax.broadcasted_iota(jnp.int32, shape, dim)


def unpack_planes(codes):
    return [
        jnp.bitwise_and(jnp.right_shift(codes, 4 * j), 15).astype(jnp.float32) - code_offset
        for j in range(4)
    ]


def spread_scales(scales_ref, spread_ref):
    one_hot = (iota((512, rows), 0) // 16 == iota((512, rows), 1)).astype(jnp.bfloat16)
    by_row = jnp.dot(
        one_hot,
        scales_ref[...].astype(jnp.float32).astype(jnp.bfloat16),
        preferred_element_type=jnp.float32,
    )
    mine = iota((512, half_tokens), 1) // 4 == iota((512, half_tokens), 0) % 16
    kept = jnp.where(mine, by_row, 0.0).astype(jnp.bfloat16)
    return jnp.dot(kept, spread_ref[...], preferred_element_type=jnp.float32)


def rotate_rows(vectors, cosine, sine):
    return vectors * cosine + pltpu.roll(vectors, 64, 1) * sine


def attend(
    half,
    lengths_ref,
    q_ref,
    q_scratch,
    cosine,
    sine,
    key_now,
    value_now,
    select_ref,
    key_ref,
    value_ref,
    store,
):
    q_scratch[...] = q_ref[...].astype(jnp.float32)
    by_head = [
        rotate_rows(q_scratch[pl.ds(h, rows, stride=local_heads), :], cosine, sine)
        for h in range(local_heads)
    ]
    q_rot = jnp.concatenate(by_head, axis=0).astype(jnp.bfloat16)
    spread = jnp.dot(q_rot, select_ref[...], preferred_element_type=jnp.float32)
    new_all = lax.dot_general(
        q_rot, key_now, nt, preferred_element_type=jnp.float32
    ) * np.float32(head_width**-0.5)
    lane_low = iota((1, 512), 1) % 128 // 32
    size = local_heads * chunk
    row = iota((4 * size, 128), 0)
    lane = iota((4 * size, 128), 1)
    position = jnp.where(
        row % chunk == lane // 16,
        half * half_tokens + 4 * (lane % 16) + row // size,
        1 << 20,
    )
    for b in range(rows // chunk):
        pick = lambda a: jnp.concatenate(
            [a[h * rows + b * chunk : h * rows + (b + 1) * chunk] for h in range(local_heads)], 0
        )
        q_block = pick(spread)
        left = jnp.concatenate(
            [jnp.where(lane_low == low, q_block, 0.0) for low in range(4)], axis=0
        ).astype(jnp.bfloat16)
        cache = pl.ds(b * 128, 128)
        scores = lax.dot_general(left, key_ref[cache, :], nt, preferred_element_type=jnp.float32)
        length_row = jnp.full((1, 128), lengths_ref[b * chunk], jnp.int32)
        for i in range(1, chunk):
            length_row = jnp.where(
                iota((1, 128), 1) // 16 >= i, lengths_ref[b * chunk + i], length_row
            )
        live = position < length_row
        scores = jnp.where(live, scores, neg_floor)
        new_block = pick(new_all)
        mine = jnp.logical_and(
            iota((size, rows), 1) == b * chunk + iota((size, rows), 0) % chunk, half == 0
        )
        new_block = jnp.where(mine, new_block, neg_floor)
        parts = [scores[low * size : (low + 1) * size] for low in range(4)]
        top = jnp.maximum(
            jnp.max(
                jnp.maximum(jnp.maximum(parts[0], parts[1]), jnp.maximum(parts[2], parts[3])),
                axis=1,
                keepdims=True,
            ),
            jnp.max(new_block, axis=1, keepdims=True),
        )
        weights = jnp.where(
            live, jnp.exp(scores - jnp.concatenate([top] * 4, axis=0)), 0.0
        ).astype(jnp.bfloat16)
        new_weight = jnp.where(mine, jnp.exp(new_block - top), 0.0).astype(jnp.bfloat16)
        wide = weights.astype(jnp.float32)
        total = jnp.sum(
            wide[:size] + wide[size : 2 * size] + wide[2 * size : 3 * size] + wide[3 * size :],
            axis=1,
            keepdims=True,
        ) + jnp.sum(new_weight.astype(jnp.float32), axis=1, keepdims=True)
        crossed = jnp.dot(weights, value_ref[cache, :], preferred_element_type=jnp.float32)
        mixed = jnp.where(lane_low == 0, crossed[:size], 0.0)
        for low in range(1, 4):
            mixed = jnp.where(lane_low == low, crossed[low * size : (low + 1) * size], mixed)
        high = mixed.astype(jnp.bfloat16)
        rest = (mixed - high.astype(jnp.float32)).astype(jnp.bfloat16)
        weighted = (
            lax.dot_general(high, select_ref[...], nt, preferred_element_type=jnp.float32)
            + lax.dot_general(rest, select_ref[...], nt, preferred_element_type=jnp.float32)
            + jnp.dot(new_weight, value_now, preferred_element_type=jnp.float32)
        )
        some = total > 0.0
        floor_total = jnp.where(some, total, 1.0)
        logsum = jnp.where(some, top + jnp.log(floor_total), neg_floor)
        result = weighted / floor_total
        for h in range(local_heads):
            part = slice(h * chunk, (h + 1) * chunk)
            store(b, h, result[part], logsum[part])


def position_tables(lengths_ref, table_ref, table_scratch):
    for r in range(rows):
        table_scratch[pl.ds(r, 1), :] = table_ref[pl.ds(lengths_ref[r], 1), :]
    return table_scratch[:, :128], table_scratch[:, 128:]


def pick_head(array_ref, index):
    wide = array_ref[...].astype(jnp.float32)
    return jnp.sum(jnp.where(iota(wide.shape, 1) == index, wide, 0.0), axis=1)


def own_kernel(
    lengths_ref,
    q_ref,
    new_key_ref,
    new_value_ref,
    key_codes_ref,
    key_scales_ref,
    value_codes_ref,
    value_scales_ref,
    key_table_ref,
    query_table_ref,
    select_ref,
    swap_ref,
    spread_ref,
    key_ref,
    value_ref,
    table_ref,
    now_ref,
    own_ref,
    own_log_ref,
    q_scratch,
):
    rank = lax.axis_index("tensor")
    half = lax.rem(rank, 2)
    head = lax.div(rank, 2)
    cosine, sine = position_tables(lengths_ref, query_table_ref, table_ref)
    key_now = rotate_rows(pick_head(new_key_ref, head), cosine, sine).astype(jnp.bfloat16)
    value_now = pick_head(new_value_ref, head).astype(jnp.bfloat16)
    now_ref[0] = key_now
    now_ref[1] = value_now
    scales = spread_scales(key_scales_ref, spread_ref)
    swap = swap_ref[...]
    for j, plane in enumerate(unpack_planes(key_codes_ref[...])):
        partner = jnp.dot(plane.astype(jnp.bfloat16), swap, preferred_element_type=jnp.float32)
        lanes = slice(j * 128, (j + 1) * 128)
        shape = (rows, 16, 128)
        turned = (
            plane.reshape(shape) * key_table_ref[half, 0, :, lanes][None]
            + partner.reshape(shape) * key_table_ref[half, 1, :, lanes][None]
        ).reshape(512, 128)
        key_ref[:, lanes] = (turned * scales).astype(jnp.bfloat16)
    scales = spread_scales(value_scales_ref, spread_ref) * np.float32(1.0 / cache_step)
    for j, plane in enumerate(unpack_planes(value_codes_ref[...])):
        value_ref[:, j * 128 : (j + 1) * 128] = (plane * scales).astype(jnp.bfloat16)

    lane_head = iota((chunk, 128), 1) // 32

    def store(b, h, result, logsum):
        block = pl.ds(b * chunk, chunk)
        own_ref[block, h * 128 : (h + 1) * 128] = result
        spread_log = jnp.broadcast_to(logsum, (chunk, 128))
        own_log_ref[block, :] = (
            spread_log if h == 0 else jnp.where(lane_head == h, spread_log, own_log_ref[block, :])
        )

    attend(
        half, lengths_ref, q_ref, q_scratch, cosine, sine, key_now, value_now,
        select_ref, key_ref, value_ref, store,
    )


def partner_kernel(
    lengths_ref,
    q_ref,
    table_ref,
    now_ref,
    key_ref,
    value_ref,
    select_ref,
    out_ref,
    q_scratch,
    out_scratch,
):
    half = lax.rem(lax.axis_index("tensor"), 2)
    lane = iota((chunk, 128), 1)
    lane_head = lane // 32

    def store(b, h, result, logsum):
        block = pl.ds(b * chunk, chunk)
        out_scratch[block, h * 128 : (h + 1) * 128] = result
        whole = jnp.broadcast_to(logsum, (chunk, 128))
        first = whole.astype(jnp.bfloat16).astype(jnp.float32)
        second = (whole - first).astype(jnp.bfloat16).astype(jnp.float32)
        third = whole - first - second
        which = lane % 32
        pieces = jnp.where(
            which == 0, first, jnp.where(which == 1, second, jnp.where(which == 2, third, 0.0))
        )
        tail = slice(512, 640)
        out_scratch[block, tail] = (
            pieces if h == 0 else jnp.where(lane_head == h, pieces, out_scratch[block, tail])
        )

    attend(
        half, lengths_ref, q_ref, q_scratch, table_ref[:, :128], table_ref[:, 128:],
        now_ref[0], now_ref[1], select_ref, key_ref, value_ref, store,
    )
    out_ref[...] = out_scratch[...].astype(jnp.bfloat16)


def combine_kernel(own_ref, own_log_ref, other_ref, out_ref):
    lane_head = iota((rows, 128), 1) // 32
    other_log = other_ref[:, 512:640].astype(jnp.float32)
    for h in range(local_heads):
        lanes = slice(h * 128, (h + 1) * 128)
        theirs = jnp.sum(jnp.where(lane_head == h, other_log, 0.0), axis=1, keepdims=True)
        mine = own_log_ref[:, h * 32 : h * 32 + 1]
        joint = jnp.maximum(mine, theirs)
        mine_factor = jnp.exp(mine - joint)
        their_factor = jnp.exp(theirs - joint)
        scale = 1.0 / (mine_factor + their_factor)
        out_ref[:, lanes] = (
            own_ref[:, lanes] * (mine_factor * scale)
            + other_ref[:, lanes].astype(jnp.float32) * (their_factor * scale)
        ).astype(jnp.bfloat16)


def weight_kernel(codes_ref, scales_ref, out_ref):
    for b in range(codes_ref.shape[0] // 64):
        words = codes_ref[b * 64 : (b + 1) * 64, :]
        first = pl.program_id(0) * (codes_ref.shape[0] // 32) + 2 * b
        scale = [
            (scales_ref[pl.ds(first + n, 1), :].astype(jnp.float32) / weight_step) for n in range(2)
        ]
        for k in range(4):
            plane = (
                jnp.bitwise_and(jnp.right_shift(words, 4 * k), 15).astype(jnp.float32) - code_offset
            )
            out_ref[b * 256 + k * 64 : b * 256 + (k + 1) * 64, :] = jnp.concatenate(
                [plane[:32] * scale[0], plane[32:] * scale[1]], axis=0
            ).astype(jnp.bfloat16)


def project_kernel(gathered_ref, hadamard_ref, weight_ref, out_ref):
    hadamard = hadamard_ref[...]
    left = jnp.dot(gathered_ref[:, :256], hadamard, preferred_element_type=jnp.float32)
    right = jnp.dot(gathered_ref[:, 256:], hadamard, preferred_element_type=jnp.float32)
    factor = np.float32(8192.0**-0.5)
    total = jnp.zeros((rows, 512), jnp.float32)
    for p, mixed in enumerate((left + right, left - right)):
        blocks = [mixed[z * rows : (z + 1) * rows] for z in range(16)]
        for bit in range(4):
            step = 1 << bit
            blocks = [
                blocks[z] + blocks[z ^ step] if z & step == 0 else blocks[z ^ step] - blocks[z]
                for z in range(16)
            ]
        for z in range(16):
            start = (2 * z + p) * 256
            total = total + jnp.dot(
                (blocks[z] * factor).astype(jnp.bfloat16),
                weight_ref[start : start + 256, :],
                preferred_element_type=jnp.float32,
            )
    out_ref[...] = total.astype(jnp.bfloat16)


vmem = pl.BlockSpec(memory_space=pltpu.VMEM)
smem = pl.BlockSpec(memory_space=pltpu.SMEM)
params = pltpu.CompilerParams(vmem_limit_bytes=40 * 1024 * 1024)


def per_device(
    queries,
    new_key,
    new_value,
    key_codes,
    key_scales,
    value_codes,
    value_scales,
    lengths,
    out_codes,
    out_scales,
):
    pairs = [(i, i ^ 1) for i in range(16)]
    f32, bf16 = jnp.float32, jnp.bfloat16
    shape = jax.ShapeDtypeStruct
    other_queries = lax.ppermute(queries, "tensor", pairs)
    select = jnp.asarray(selector(), bf16)
    keys, values, table, now, own, own_log = pl.pallas_call(
        own_kernel,
        out_shape=(
            shape((512, 512), bf16),
            shape((512, 512), bf16),
            shape((rows, 256), f32),
            shape((2, rows, 128), bf16),
            shape((rows, 512), f32),
            shape((rows, 128), f32),
        ),
        in_specs=[smem] + [vmem] * 12,
        out_specs=(vmem,) * 6,
        scratch_shapes=[pltpu.VMEM((128, 128), f32)],
        compiler_params=params,
        cost_estimate=pl.CostEstimate(flops=400_000_000, bytes_accessed=2_000_000, transcendentals=65536),
        name="own_heads",
    )(
        lengths,
        queries.reshape(128, 128),
        new_key,
        new_value,
        key_codes.reshape(512, 128),
        key_scales.reshape(rows, half_tokens),
        value_codes.reshape(512, 128),
        value_scales.reshape(rows, half_tokens),
        jnp.asarray(key_tables()),
        jnp.asarray(query_table()),
        select,
        jnp.asarray(swap_words(), bf16),
        jnp.asarray(token_spread(), bf16),
    )
    sending = pl.pallas_call(
        partner_kernel,
        out_shape=shape((rows, 640), bf16),
        in_specs=[smem] + [vmem] * 6,
        out_specs=vmem,
        scratch_shapes=[pltpu.VMEM((128, 128), f32), pltpu.VMEM((rows, 640), f32)],
        compiler_params=params,
        name="other_heads",
    )(lengths, other_queries.reshape(128, 128), table, now, keys, values, select)
    received = lax.ppermute(sending, "tensor", pairs)
    out_codes, _ = lax.optimization_barrier((out_codes, sending))
    steps = 8
    weight = pl.pallas_call(
        weight_kernel,
        grid=(steps,),
        out_shape=shape((8192, 512), bf16),
        in_specs=[
            pl.BlockSpec((2048 // steps, 512), lambda i: (i, 0)),
            pl.BlockSpec((64, 512), lambda i: (0, 0)),
        ],
        out_specs=pl.BlockSpec((8192 // steps, 512), lambda i: (i, 0)),
        compiler_params=params,
        cost_estimate=pl.CostEstimate(flops=20_000_000, bytes_accessed=12_000_000, transcendentals=0),
        name="unpack_weight",
    )(out_codes, out_scales)
    attended = pl.pallas_call(
        combine_kernel,
        out_shape=shape((rows, 512), bf16),
        in_specs=[vmem] * 3,
        out_specs=vmem,
        compiler_params=params,
        name="combine_halves",
    )(own, own_log, received)
    gathered = lax.all_gather(attended, "tensor", axis=0, tiled=True)
    return pl.pallas_call(
        project_kernel,
        out_shape=shape((rows, 512), bf16),
        in_specs=[vmem] * 3,
        out_specs=vmem,
        compiler_params=params,
        name="project",
    )(gathered, jnp.asarray(hadamard_pair(), bf16), weight)


def solution(mesh):
    return jax.shard_map(
        per_device,
        mesh=mesh,
        in_specs=(
            P("dp", "tensor", None),
            P("dp", None, None),
            P("dp", None, None),
            P("dp", "tensor", None),
            P("dp", "tensor", None),
            P("dp", "tensor", None),
            P("dp", "tensor", None),
            P("dp"),
            P(None, "tensor"),
            P(None, "tensor"),
        ),
        out_specs=P("dp", "tensor"),
        check_vma=False,
    )
```

```python
import functools

import jax
import jax.numpy as jnp
import numpy as np
from jax import lax
from jax.experimental import pallas as pl
from jax.experimental.pallas import tpu as pltpu
from jax.sharding import PartitionSpec as P

rope_base = 10000.0
neg_floor = -1e30
code_offset = 7.5
cache_step = 256.0
weight_step = 8192.0

rows = 32
head_width = 128
local_heads = 4
half_tokens = 64
chunk = 8
nt = (((1,), (1,)), ((), ()))


def rope_angles(positions):
    frequency = rope_base ** (-(np.arange(64) * 2.0 / head_width))
    return np.asarray(positions, np.float64)[..., None] * frequency


def key_tables():
    lane = np.arange(512)
    plane, low, word = lane // 128, lane % 128 // 32, lane % 32
    entry = 4 * word + plane
    position = 4 * np.arange(16)[:, None] + low[None, :]
    out = []
    for half in range(2):
        angle = rope_angles(np.arange(128))[half * half_tokens + position, (entry % 64)[None, :]]
        sign = np.where(entry < 64, -1.0, 1.0)
        scale = head_width**-0.5 / cache_step
        out.append(np.stack([np.cos(angle) * scale, np.sin(angle) * sign * scale]))
    return np.stack(out).astype(np.float32)


def query_table():
    angle = rope_angles(np.arange(136))
    return np.concatenate([np.cos(angle), np.cos(angle), -np.sin(angle), np.sin(angle)], -1).astype(
        np.float32
    )


def iota(shape, dim):
    return lax.broadcasted_iota(jnp.int32, shape, dim)


def one_hot(condition):
    return jnp.where(condition, 1.0, 0.0).astype(jnp.bfloat16)


def selector():
    shape = (128, 512)
    lane = iota(shape, 1)
    return one_hot(iota(shape, 0) == 4 * (lane % 32) + lane // 128)


def swap_words():
    shape = (128, 128)
    return one_hot(iota(shape, 0) == jnp.bitwise_xor(iota(shape, 1), 16))


def token_spread():
    return one_hot(iota((64, 128), 0) % 4 == iota((64, 128), 1) // 32)


def hadamard_pair():
    shape = (256, 256)
    column = iota(shape, 1)
    target = column // 32 % 2 * 128 + 4 * (column % 32) + column // 64
    both = jnp.bitwise_and(iota(shape, 0), target)
    for shift in (4, 2, 1):
        both = jnp.bitwise_xor(both, jnp.right_shift(both, shift))
    return (1.0 - 2.0 * jnp.bitwise_and(both, 1).astype(jnp.float32)).astype(jnp.bfloat16)


def unpack_planes(codes):
    return [
        jnp.bitwise_and(jnp.right_shift(codes, 4 * j), 15).astype(jnp.float32) - code_offset
        for j in range(4)
    ]


def spread_scales(scales):
    by_row = jnp.dot(
        one_hot(iota((512, rows), 0) // 16 == iota((512, rows), 1)),
        scales.astype(jnp.float32).astype(jnp.bfloat16),
        preferred_element_type=jnp.float32,
    )
    mine = iota((512, half_tokens), 1) // 4 == iota((512, half_tokens), 0) % 16
    kept = jnp.where(mine, by_row, 0.0).astype(jnp.bfloat16)
    return jnp.dot(kept, token_spread(), preferred_element_type=jnp.float32)


def rotate_rows(vectors, cosine, sine):
    return vectors * cosine + pltpu.roll(vectors, 64, 1) * sine


def rotate_queries(q, scratch, table_ref):
    scratch[...] = q.astype(jnp.float32)
    return jnp.concatenate(
        [
            rotate_rows(
                scratch[pl.ds(h, rows, stride=local_heads), :], table_ref[:, :128], table_ref[:, 128:]
            )
            for h in range(local_heads)
        ],
        axis=0,
    ).astype(jnp.bfloat16)


def attend(
    half, length_ref, q_rot, key_now, value_now, select_ref, key_ref, value_ref, store
):
    spread = jnp.dot(q_rot, select_ref[...], preferred_element_type=jnp.float32)
    new_all = lax.dot_general(
        q_rot, key_now, nt, preferred_element_type=jnp.float32
    ) * np.float32(head_width**-0.5)
    lane_low = iota((1, 512), 1) % 128 // 32
    size = local_heads * chunk
    row = iota((4 * size, 128), 0)
    lane = iota((4 * size, 128), 1)
    position = jnp.where(
        row % chunk == lane // 16,
        half * half_tokens + 4 * (lane % 16) + row // size,
        1 << 20,
    )
    for b in range(rows // chunk):
        pick = lambda a: jnp.concatenate(
            [a[h * rows + b * chunk : h * rows + (b + 1) * chunk] for h in range(local_heads)], 0
        )
        q_block = pick(spread)
        left = jnp.concatenate(
            [jnp.where(lane_low == low, q_block, 0.0) for low in range(4)], axis=0
        ).astype(jnp.bfloat16)
        cache = pl.ds(b * 128, 128)
        scores = lax.dot_general(left, key_ref[cache, :], nt, preferred_element_type=jnp.float32)
        length_row = length_ref[pl.ds(b, 1), :]
        live = position < length_row
        scores = jnp.where(live, scores, neg_floor)
        new_block = pick(new_all)
        mine = jnp.logical_and(
            iota((size, rows), 1) == b * chunk + iota((size, rows), 0) % chunk, half == 0
        )
        new_block = jnp.where(mine, new_block, neg_floor)
        parts = [scores[low * size : (low + 1) * size] for low in range(4)]
        top = jnp.maximum(
            jnp.max(
                jnp.maximum(jnp.maximum(parts[0], parts[1]), jnp.maximum(parts[2], parts[3])),
                axis=1,
                keepdims=True,
            ),
            jnp.max(new_block, axis=1, keepdims=True),
        )
        weights = jnp.where(
            live, jnp.exp(scores - jnp.concatenate([top] * 4, axis=0)), 0.0
        ).astype(jnp.bfloat16)
        new_weight = jnp.where(mine, jnp.exp(new_block - top), 0.0).astype(jnp.bfloat16)
        wide = weights.astype(jnp.float32)
        total = jnp.sum(
            wide[:size] + wide[size : 2 * size] + wide[2 * size : 3 * size] + wide[3 * size :],
            axis=1,
            keepdims=True,
        ) + jnp.sum(new_weight.astype(jnp.float32), axis=1, keepdims=True)
        crossed = jnp.dot(weights, value_ref[cache, :], preferred_element_type=jnp.float32)
        mixed = jnp.where(lane_low == 0, crossed[:size], 0.0)
        for low in range(1, 4):
            mixed = jnp.where(lane_low == low, crossed[low * size : (low + 1) * size], mixed)
        high = mixed.astype(jnp.bfloat16)
        rest = (mixed - high.astype(jnp.float32)).astype(jnp.bfloat16)
        weighted = (
            lax.dot_general(high, select_ref[...], nt, preferred_element_type=jnp.float32)
            + lax.dot_general(rest, select_ref[...], nt, preferred_element_type=jnp.float32)
            + jnp.dot(new_weight, value_now, preferred_element_type=jnp.float32)
        )
        some = total > 0.0
        floor_total = jnp.where(some, total, 1.0)
        logsum = jnp.where(some, top + jnp.log(floor_total), neg_floor)
        result = weighted / floor_total
        for h in range(local_heads):
            part = slice(h * chunk, (h + 1) * chunk)
            store(b, h, result[part], logsum[part])


def pick_head(array, index):
    wide = array.astype(jnp.float32)
    return jnp.sum(jnp.where(iota(wide.shape, 1) == index, wide, 0.0), axis=1)


code_chunks = 8


def prepare_kernel(
    lengths_hbm,
    queries_hbm,
    new_key_hbm,
    new_value_hbm,
    key_codes_hbm,
    key_scales_hbm,
    value_codes_hbm,
    value_scales_hbm,
    key_table_hbm,
    query_table_hbm,
    out_codes_hbm,
    out_scales_hbm,
    key_ref,
    value_ref,
    table_ref,
    now_ref,
    query_ref,
    length_ref,
    select_ref,
    hadamard_ref,
    weight_ref,
    lengths,
    queries,
    new_key,
    new_value,
    key_codes,
    key_scales,
    value_codes,
    value_scales,
    key_table,
    query_table,
    out_codes,
    out_scales,
    q_scratch,
    scale_scratch,
    sems,
    code_sems,
):
    rank = lax.axis_index("tensor")
    half = lax.rem(rank, 2)
    head = lax.div(rank, 2)
    pairs = [
        (key_codes_hbm, key_codes),
        (key_scales_hbm, key_scales),
        (key_table_hbm.at[half], key_table),
        (value_codes_hbm, value_codes),
        (value_scales_hbm, value_scales),
        (lengths_hbm, lengths),
        (query_table_hbm, query_table),
        (new_key_hbm, new_key),
        (new_value_hbm, new_value),
        (queries_hbm, queries),
        (out_scales_hbm, out_scales),
    ]
    copies = [
        pltpu.make_async_copy(source, target, sems.at[i]) for i, (source, target) in enumerate(pairs)
    ]
    for copy in copies:
        copy.start()
    size = out_codes_hbm.shape[0] // code_chunks

    def code_copy(i):
        part = pl.ds(i * size, size)
        return pltpu.make_async_copy(out_codes_hbm.at[part, :], out_codes.at[part, :], code_sems.at[i])

    for i in range(code_chunks):
        code_copy(i).start()
    select_ref[...] = selector()
    hadamard_ref[...] = hadamard_pair()
    swap = swap_words()
    for copy in copies[:3]:
        copy.wait()
    scales = spread_scales(key_scales[...])
    for j, plane in enumerate(unpack_planes(key_codes[...])):
        partner = jnp.dot(plane.astype(jnp.bfloat16), swap, preferred_element_type=jnp.float32)
        lanes = slice(j * 128, (j + 1) * 128)
        shape = (rows, 16, 128)
        turned = (
            plane.reshape(shape) * key_table[0, :, lanes][None]
            + partner.reshape(shape) * key_table[1, :, lanes][None]
        ).reshape(512, 128)
        key_ref[:, lanes] = (turned * scales).astype(jnp.bfloat16)
    for copy in copies[3:5]:
        copy.wait()
    scales = spread_scales(value_scales[...]) * np.float32(1.0 / cache_step)
    for j, plane in enumerate(unpack_planes(value_codes[...])):
        value_ref[:, j * 128 : (j + 1) * 128] = (plane * scales).astype(jnp.bfloat16)
    for copy in copies[5:]:
        copy.wait()
    for r in range(rows):
        table_ref[pl.ds(r, 1), :] = query_table[pl.ds(lengths[r], 1), :]
    cosine, sine = table_ref[:, :128], table_ref[:, 128:]
    now_ref[0] = rotate_rows(pick_head(new_key[...], head), cosine, sine).astype(jnp.bfloat16)
    now_ref[1] = pick_head(new_value[...], head).astype(jnp.bfloat16)
    query_ref[...] = rotate_queries(queries[...], q_scratch, table_ref)
    lane_row = iota((1, 128), 1) // 16
    for b in range(rows // chunk):
        line = jnp.full((1, 128), lengths[b * chunk], jnp.int32)
        for i in range(1, chunk):
            line = jnp.where(lane_row >= i, lengths[b * chunk + i], line)
        length_ref[pl.ds(b, 1), :] = line
    scale_scratch[...] = out_scales[...].astype(jnp.float32) * np.float32(1.0 / weight_step)

    @pl.loop(0, code_chunks)
    def _(i):
        code_copy(i).wait()
        for b in range(size // 32):
            words = out_codes[pl.ds(i * size + b * 32, 32), :]
            group = i * (size // 32) + b
            scale = jnp.broadcast_to(scale_scratch[pl.ds(group, 1), :], (16, 512)).astype(jnp.bfloat16)
            for k in range(4):
                power = 16.0**k
                plane = (
                    jnp.bitwise_and(words, 15 << 4 * k).astype(jnp.float32).astype(jnp.bfloat16)
                    - jnp.bfloat16(code_offset * power)
                )
                scaled = scale * jnp.bfloat16(1.0 / power)
                for part in range(2):
                    start = i * size * 4 + (b // 2) * 256 + k * 64 + (b % 2) * 32 + part * 16
                    weight_ref[pl.ds(start, 16), :] = plane[part * 16 : (part + 1) * 16] * scaled


def own_kernel(
    q_ref, now_ref, length_ref, select_ref, key_ref, value_ref, own_ref, own_log_ref
):
    half = lax.rem(lax.axis_index("tensor"), 2)
    lane_head = iota((chunk, 128), 1) // 32

    def store(b, h, result, logsum):
        block = pl.ds(b * chunk, chunk)
        own_ref[block, h * 128 : (h + 1) * 128] = result
        spread_log = jnp.broadcast_to(logsum, (chunk, 128))
        own_log_ref[block, :] = (
            spread_log if h == 0 else jnp.where(lane_head == h, spread_log, own_log_ref[block, :])
        )

    attend(
        half, length_ref, q_ref[...], now_ref[0], now_ref[1], select_ref, key_ref, value_ref, store
    )


def partner_kernel(
    q_ref, table_ref, now_ref, length_ref, select_ref, key_ref, value_ref, out_ref, q_scratch, out_scratch
):
    half = lax.rem(lax.axis_index("tensor"), 2)
    lane = iota((chunk, 128), 1)
    lane_head = lane // 32

    def store(b, h, result, logsum):
        block = pl.ds(b * chunk, chunk)
        out_scratch[block, h * 128 : (h + 1) * 128] = result
        whole = jnp.broadcast_to(logsum, (chunk, 128))
        first = whole.astype(jnp.bfloat16).astype(jnp.float32)
        second = (whole - first).astype(jnp.bfloat16).astype(jnp.float32)
        third = whole - first - second
        which = lane % 32
        pieces = jnp.where(
            which == 0, first, jnp.where(which == 1, second, jnp.where(which == 2, third, 0.0))
        )
        tail = slice(512, 640)
        out_scratch[block, tail] = (
            pieces if h == 0 else jnp.where(lane_head == h, pieces, out_scratch[block, tail])
        )

    attend(
        half,
        length_ref,
        rotate_queries(q_ref[...], q_scratch, table_ref),
        now_ref[0],
        now_ref[1],
        select_ref,
        key_ref,
        value_ref,
        store,
    )
    out_ref[...] = out_scratch[...].astype(jnp.bfloat16)


def combine_kernel(own_ref, own_log_ref, other_ref, out_ref):
    lane_head = iota((rows, 128), 1) // 32
    other_log = other_ref[:, 512:640].astype(jnp.float32)
    for h in range(local_heads):
        lanes = slice(h * 128, (h + 1) * 128)
        theirs = jnp.sum(jnp.where(lane_head == h, other_log, 0.0), axis=1, keepdims=True)
        mine = own_log_ref[:, h * 32 : h * 32 + 1]
        joint = jnp.maximum(mine, theirs)
        mine_factor = jnp.exp(mine - joint)
        their_factor = jnp.exp(theirs - joint)
        scale = 1.0 / (mine_factor + their_factor)
        out_ref[:, lanes] = (
            own_ref[:, lanes] * (mine_factor * scale)
            + other_ref[:, lanes].astype(jnp.float32) * (their_factor * scale)
        ).astype(jnp.bfloat16)


def project_kernel(gathered_ref, hadamard_ref, weight_ref, out_ref):
    hadamard = hadamard_ref[...]
    left = jnp.dot(gathered_ref[:, :256], hadamard, preferred_element_type=jnp.float32)
    right = jnp.dot(gathered_ref[:, 256:], hadamard, preferred_element_type=jnp.float32)
    factor = np.float32(8192.0**-0.5)
    total = jnp.zeros((rows, 512), jnp.float32)
    for p, mixed in enumerate((left + right, left - right)):
        blocks = [mixed[z * rows : (z + 1) * rows] for z in range(16)]
        for bit in range(4):
            step = 1 << bit
            blocks = [
                blocks[z] + blocks[z ^ step] if z & step == 0 else blocks[z ^ step] - blocks[z]
                for z in range(16)
            ]
        for z in range(16):
            start = (2 * z + p) * 256
            total = total + jnp.dot(
                (blocks[z] * factor).astype(jnp.bfloat16),
                weight_ref[start : start + 256, :],
                preferred_element_type=jnp.float32,
            )
    out_ref[...] = total.astype(jnp.bfloat16)


vmem = pl.BlockSpec(memory_space=pltpu.VMEM)
hbm = pl.BlockSpec(memory_space=pltpu.HBM)
params = pltpu.CompilerParams(vmem_limit_bytes=20 * 1024 * 1024)


def per_device(
    queries,
    new_key,
    new_value,
    key_codes,
    key_scales,
    value_codes,
    value_scales,
    lengths,
    out_codes,
    out_scales,
):
    pairs = [(i, i ^ 1) for i in range(16)]
    f32, bf16, i32 = jnp.float32, jnp.bfloat16, jnp.int32
    shape = jax.ShapeDtypeStruct
    other_queries = lax.ppermute(queries, "tensor", pairs)
    keys, values, table, now, query, length, select, hadamard, weight = pl.pallas_call(
        prepare_kernel,
        out_shape=(
            shape((512, 512), bf16),
            shape((512, 512), bf16),
            shape((rows, 256), f32),
            shape((2, rows, 128), bf16),
            shape((128, 128), bf16),
            shape((8, 128), i32),
            shape((128, 512), bf16),
            shape((256, 256), bf16),
            shape((8192, 512), bf16),
        ),
        in_specs=[hbm] * 12,
        out_specs=(vmem,) * 9,
        scratch_shapes=[
            pltpu.SMEM((rows,), i32),
            pltpu.VMEM((128, 128), bf16),
            pltpu.VMEM((rows, 8, 128), bf16),
            pltpu.VMEM((rows, 8, 128), bf16),
            pltpu.VMEM((512, 128), i32),
            pltpu.VMEM((rows, half_tokens), i32),
            pltpu.VMEM((512, 128), i32),
            pltpu.VMEM((rows, half_tokens), i32),
            pltpu.VMEM((2, 16, 512), f32),
            pltpu.VMEM((136, 256), f32),
            pltpu.VMEM((2048, 512), i32),
            pltpu.VMEM((64, 512), i32),
            pltpu.VMEM((128, 128), f32),
            pltpu.VMEM((64, 512), f32),
            pltpu.SemaphoreType.DMA((11,)),
            pltpu.SemaphoreType.DMA((code_chunks,)),
        ],
        compiler_params=params,
        cost_estimate=pl.CostEstimate(flops=100_000_000, bytes_accessed=14_000_000, transcendentals=0),
        name="prepare",
    )(
        *[
            pltpu.with_memory_space_constraint(array, pltpu.HBM)
            for array in (
                lengths,
                queries.reshape(128, 128),
                new_key,
                new_value,
                key_codes.reshape(512, 128),
                key_scales.reshape(rows, half_tokens),
                value_codes.reshape(512, 128),
                value_scales.reshape(rows, half_tokens),
                jnp.asarray(key_tables()),
                jnp.asarray(query_table()),
                out_codes,
                out_scales,
            )
        ]
    )
    sending = pl.pallas_call(
        partner_kernel,
        out_shape=shape((rows, 640), bf16),
        in_specs=[vmem] * 7,
        out_specs=vmem,
        scratch_shapes=[pltpu.VMEM((128, 128), f32), pltpu.VMEM((rows, 640), f32)],
        compiler_params=params,
        name="other_heads",
    )(other_queries.reshape(128, 128), table, now, length, select, keys, values)
    received = lax.ppermute(sending, "tensor", pairs)
    query, _ = lax.optimization_barrier((query, sending))
    own, own_log = pl.pallas_call(
        own_kernel,
        out_shape=(shape((rows, 512), f32), shape((rows, 128), f32)),
        in_specs=[vmem] * 6,
        out_specs=(vmem,) * 2,
        compiler_params=params,
        cost_estimate=pl.CostEstimate(flops=300_000_000, bytes_accessed=2_000_000, transcendentals=65536),
        name="own_heads",
    )(query, now, length, select, keys, values)
    attended = pl.pallas_call(
        combine_kernel,
        out_shape=shape((rows, 512), bf16),
        in_specs=[vmem] * 3,
        out_specs=vmem,
        compiler_params=params,
        name="combine_halves",
    )(own, own_log, received)
    gathered = lax.all_gather(attended, "tensor", axis=0, tiled=True)
    return pl.pallas_call(
        project_kernel,
        out_shape=shape((rows, 512), bf16),
        in_specs=[vmem] * 3,
        out_specs=vmem,
        compiler_params=params,
        name="project",
    )(gathered, hadamard, weight)


def solution(mesh):
    return jax.shard_map(
        per_device,
        mesh=mesh,
        in_specs=(
            P("dp", "tensor", None),
            P("dp", None, None),
            P("dp", None, None),
            P("dp", "tensor", None),
            P("dp", "tensor", None),
            P("dp", "tensor", None),
            P("dp", "tensor", None),
            P("dp"),
            P(None, "tensor"),
            P(None, "tensor"),
        ),
        out_specs=P("dp", "tensor"),
        check_vma=False,
    )
```

```python
import functools

import jax
import jax.numpy as jnp
import numpy as np
from jax import lax
from jax.experimental import pallas as pl
from jax.experimental.pallas import tpu as pltpu
from jax.sharding import PartitionSpec as P

rope_base = 10000.0
neg_floor = -1e30
code_offset = 7.5
cache_step = 256.0
weight_step = 8192.0

rows = 32
head_width = 128
local_heads = 4
half_tokens = 64
chunk = 8
nt = (((1,), (1,)), ((), ()))


def rope_angles(positions):
    frequency = rope_base ** (-(np.arange(64) * 2.0 / head_width))
    return np.asarray(positions, np.float64)[..., None] * frequency


def key_tables():
    lane = np.arange(512)
    plane, low, word = lane // 128, lane % 128 // 32, lane % 32
    entry = 4 * word + plane
    position = 4 * np.arange(16)[:, None] + low[None, :]
    out = []
    for half in range(2):
        angle = rope_angles(np.arange(128))[half * half_tokens + position, (entry % 64)[None, :]]
        sign = np.where(entry < 64, -1.0, 1.0)
        scale = head_width**-0.5 / cache_step
        out.append(np.stack([np.cos(angle) * scale, np.sin(angle) * sign * scale]))
    return np.stack(out).astype(np.float32)


def query_table():
    angle = rope_angles(np.arange(136))
    return np.concatenate([np.cos(angle), np.cos(angle), -np.sin(angle), np.sin(angle)], -1).astype(
        np.float32
    )


def iota(shape, dim):
    return lax.broadcasted_iota(jnp.int32, shape, dim)


def one_hot(condition):
    return jnp.where(condition, 1.0, 0.0).astype(jnp.bfloat16)


def selector():
    shape = (128, 512)
    lane = iota(shape, 1)
    return one_hot(iota(shape, 0) == 4 * (lane % 32) + lane // 128)


def swap_words():
    shape = (128, 128)
    return one_hot(iota(shape, 0) == jnp.bitwise_xor(iota(shape, 1), 16))


def token_spread():
    return one_hot(iota((64, 128), 0) % 4 == iota((64, 128), 1) // 32)


def hadamard_pair():
    shape = (256, 256)
    column = iota(shape, 1)
    target = column // 32 % 2 * 128 + 4 * (column % 32) + column // 64
    both = jnp.bitwise_and(iota(shape, 0), target)
    for shift in (4, 2, 1):
        both = jnp.bitwise_xor(both, jnp.right_shift(both, shift))
    return (1.0 - 2.0 * jnp.bitwise_and(both, 1).astype(jnp.float32)).astype(jnp.bfloat16)


def unpack_planes(codes):
    return [
        jnp.bitwise_and(jnp.right_shift(codes, 4 * j), 15).astype(jnp.float32) - code_offset
        for j in range(4)
    ]


def spread_scales(scales):
    by_row = jnp.dot(
        one_hot(iota((512, rows), 0) // 16 == iota((512, rows), 1)),
        scales.astype(jnp.float32).astype(jnp.bfloat16),
        preferred_element_type=jnp.float32,
    )
    mine = iota((512, half_tokens), 1) // 4 == iota((512, half_tokens), 0) % 16
    kept = jnp.where(mine, by_row, 0.0).astype(jnp.bfloat16)
    return jnp.dot(kept, token_spread(), preferred_element_type=jnp.float32)


def rotate_rows(vectors, cosine, sine):
    return vectors * cosine + pltpu.roll(vectors, 64, 1) * sine


def rotate_queries(q, scratch, table_ref):
    scratch[...] = q.astype(jnp.float32)
    return jnp.concatenate(
        [
            rotate_rows(
                scratch[pl.ds(h, rows, stride=local_heads), :], table_ref[:, :128], table_ref[:, 128:]
            )
            for h in range(local_heads)
        ],
        axis=0,
    ).astype(jnp.bfloat16)


def attend(
    half, length_ref, q_rot, key_now, value_now, select_ref, key_ref, value_ref, store
):
    spread = jnp.dot(q_rot, select_ref[...], preferred_element_type=jnp.float32)
    new_all = lax.dot_general(
        q_rot, key_now, nt, preferred_element_type=jnp.float32
    ) * np.float32(head_width**-0.5)
    lane_low = iota((1, 512), 1) % 128 // 32
    size = local_heads * chunk
    row = iota((4 * size, 128), 0)
    lane = iota((4 * size, 128), 1)
    position = jnp.where(
        row % chunk == lane // 16,
        half * half_tokens + 4 * (lane % 16) + row // size,
        1 << 20,
    )
    for b in range(rows // chunk):
        pick = lambda a: jnp.concatenate(
            [a[h * rows + b * chunk : h * rows + (b + 1) * chunk] for h in range(local_heads)], 0
        )
        q_block = pick(spread)
        left = jnp.concatenate(
            [jnp.where(lane_low == low, q_block, 0.0) for low in range(4)], axis=0
        ).astype(jnp.bfloat16)
        cache = pl.ds(b * 128, 128)
        scores = lax.dot_general(left, key_ref[cache, :], nt, preferred_element_type=jnp.float32)
        length_row = length_ref[pl.ds(b, 1), :]
        live = position < length_row
        scores = jnp.where(live, scores, neg_floor)
        new_block = pick(new_all)
        mine = jnp.logical_and(
            iota((size, rows), 1) == b * chunk + iota((size, rows), 0) % chunk, half == 0
        )
        new_block = jnp.where(mine, new_block, neg_floor)
        parts = [scores[low * size : (low + 1) * size] for low in range(4)]
        top = jnp.maximum(
            jnp.max(
                jnp.maximum(jnp.maximum(parts[0], parts[1]), jnp.maximum(parts[2], parts[3])),
                axis=1,
                keepdims=True,
            ),
            jnp.max(new_block, axis=1, keepdims=True),
        )
        weights = jnp.where(
            live, jnp.exp(scores - jnp.concatenate([top] * 4, axis=0)), 0.0
        ).astype(jnp.bfloat16)
        new_weight = jnp.where(mine, jnp.exp(new_block - top), 0.0).astype(jnp.bfloat16)
        wide = weights.astype(jnp.float32)
        total = jnp.sum(
            wide[:size] + wide[size : 2 * size] + wide[2 * size : 3 * size] + wide[3 * size :],
            axis=1,
            keepdims=True,
        ) + jnp.sum(new_weight.astype(jnp.float32), axis=1, keepdims=True)
        crossed = jnp.dot(weights, value_ref[cache, :], preferred_element_type=jnp.float32)
        mixed = jnp.where(lane_low == 0, crossed[:size], 0.0)
        for low in range(1, 4):
            mixed = jnp.where(lane_low == low, crossed[low * size : (low + 1) * size], mixed)
        high = mixed.astype(jnp.bfloat16)
        rest = (mixed - high.astype(jnp.float32)).astype(jnp.bfloat16)
        weighted = (
            lax.dot_general(high, select_ref[...], nt, preferred_element_type=jnp.float32)
            + lax.dot_general(rest, select_ref[...], nt, preferred_element_type=jnp.float32)
            + jnp.dot(new_weight, value_now, preferred_element_type=jnp.float32)
        )
        some = total > 0.0
        floor_total = jnp.where(some, total, 1.0)
        logsum = jnp.where(some, top + jnp.log(floor_total), neg_floor)
        result = weighted / floor_total
        for h in range(local_heads):
            part = slice(h * chunk, (h + 1) * chunk)
            store(b, h, result[part], logsum[part])


def pick_head(array, index):
    wide = array.astype(jnp.float32)
    return jnp.sum(jnp.where(iota(wide.shape, 1) == index, wide, 0.0), axis=1)


code_chunks = 8


def stats_of(logsum):
    which = iota((chunk, 128), 1) % 32
    whole = jnp.broadcast_to(logsum, (chunk, 128))
    first = whole.astype(jnp.bfloat16).astype(jnp.float32)
    second = (whole - first).astype(jnp.bfloat16).astype(jnp.float32)
    third = whole - first - second
    return jnp.where(
        which == 0, first, jnp.where(which == 1, second, jnp.where(which == 2, third, 0.0))
    )


def storing(target):
    lane_head = iota((chunk, 128), 1) // 32
    tail = slice(512, 640)

    def store(b, h, result, logsum):
        block = pl.ds(b * chunk, chunk)
        target[block, h * 128 : (h + 1) * 128] = result
        pieces = stats_of(logsum)
        target[block, tail] = (
            pieces if h == 0 else jnp.where(lane_head == h, pieces, target[block, tail])
        )

    return store


def own_kernel(
    lengths_hbm,
    queries_hbm,
    new_key_hbm,
    new_value_hbm,
    key_codes_hbm,
    key_scales_hbm,
    value_codes_hbm,
    value_scales_hbm,
    key_table_hbm,
    query_table_hbm,
    key_ref,
    value_ref,
    table_ref,
    now_ref,
    length_ref,
    select_ref,
    hadamard_ref,
    own_ref,
    lengths,
    queries,
    new_key,
    new_value,
    key_codes,
    key_scales,
    value_codes,
    value_scales,
    key_table,
    query_table,
    q_scratch,
    sems,
):
    rank = lax.axis_index("tensor")
    half = lax.rem(rank, 2)
    head = lax.div(rank, 2)
    pairs = [
        (key_codes_hbm, key_codes),
        (key_scales_hbm, key_scales),
        (key_table_hbm.at[half], key_table),
        (value_codes_hbm, value_codes),
        (value_scales_hbm, value_scales),
        (lengths_hbm, lengths),
        (query_table_hbm, query_table),
        (new_key_hbm, new_key),
        (new_value_hbm, new_value),
        (queries_hbm, queries),
    ]
    copies = [
        pltpu.make_async_copy(source, target, sems.at[i]) for i, (source, target) in enumerate(pairs)
    ]
    for copy in copies:
        copy.start()
    select_ref[...] = selector()
    hadamard_ref[...] = hadamard_pair()
    swap = swap_words()
    for copy in copies[:3]:
        copy.wait()
    scales = spread_scales(key_scales[...])
    for j, plane in enumerate(unpack_planes(key_codes[...])):
        partner = jnp.dot(plane.astype(jnp.bfloat16), swap, preferred_element_type=jnp.float32)
        lanes = slice(j * 128, (j + 1) * 128)
        shape = (rows, 16, 128)
        turned = (
            plane.reshape(shape) * key_table[0, :, lanes][None]
            + partner.reshape(shape) * key_table[1, :, lanes][None]
        ).reshape(512, 128)
        key_ref[:, lanes] = (turned * scales).astype(jnp.bfloat16)
    for copy in copies[3:5]:
        copy.wait()
    scales = spread_scales(value_scales[...]) * np.float32(1.0 / cache_step)
    for j, plane in enumerate(unpack_planes(value_codes[...])):
        value_ref[:, j * 128 : (j + 1) * 128] = (plane * scales).astype(jnp.bfloat16)
    for copy in copies[5:]:
        copy.wait()
    for r in range(rows):
        table_ref[pl.ds(r, 1), :] = query_table[pl.ds(lengths[r], 1), :]
    cosine, sine = table_ref[:, :128], table_ref[:, 128:]
    key_now = rotate_rows(pick_head(new_key[...], head), cosine, sine).astype(jnp.bfloat16)
    value_now = pick_head(new_value[...], head).astype(jnp.bfloat16)
    now_ref[0] = key_now
    now_ref[1] = value_now
    lane_row = iota((1, 128), 1) // 16
    for b in range(rows // chunk):
        line = jnp.full((1, 128), lengths[b * chunk], jnp.int32)
        for i in range(1, chunk):
            line = jnp.where(lane_row >= i, lengths[b * chunk + i], line)
        length_ref[pl.ds(b, 1), :] = line
    attend(
        half,
        length_ref,
        rotate_queries(queries[...], q_scratch, table_ref),
        key_now,
        value_now,
        select_ref,
        key_ref,
        value_ref,
        storing(own_ref),
    )


def partner_kernel(
    q_ref,
    table_ref,
    now_ref,
    length_ref,
    select_ref,
    key_ref,
    value_ref,
    own_ref,
    out_ref,
    q_scratch,
    out_scratch,
):
    attend(
        lax.rem(lax.axis_index("tensor"), 2),
        length_ref,
        rotate_queries(q_ref[...], q_scratch, table_ref),
        now_ref[0],
        now_ref[1],
        select_ref,
        key_ref,
        value_ref,
        storing(out_scratch),
    )
    out_ref[:, :640] = own_ref[...].astype(jnp.bfloat16)
    out_ref[:, 640:] = out_scratch[...].astype(jnp.bfloat16)


def combine_kernel(mine_ref, theirs_ref, out_ref, scratch):
    half = lax.rem(lax.axis_index("tensor"), 2)
    lane_head = iota((rows, 128), 1) // 32
    for own in range(2):
        at, other = own * 640, 640 - own * 640
        logs = [mine_ref[:, at + 512 : at + 640], theirs_ref[:, other + 512 : other + 640]]
        logs = [log.astype(jnp.float32) for log in logs]
        for h in range(local_heads):
            mine, theirs = [
                jnp.sum(jnp.where(lane_head == h, log, 0.0), axis=1, keepdims=True) for log in logs
            ]
            joint = jnp.maximum(mine, theirs)
            mine_factor = jnp.exp(mine - joint)
            their_factor = jnp.exp(theirs - joint)
            scale = 1.0 / (mine_factor + their_factor)
            block = mine_ref[:, at + h * 128 : at + (h + 1) * 128].astype(jnp.float32)
            other_block = theirs_ref[:, other + h * 128 : other + (h + 1) * 128].astype(jnp.float32)
            scratch[own, :, h * 128 : (h + 1) * 128] = block * (
                mine_factor * scale
            ) + other_block * (their_factor * scale)
    first = scratch[half].astype(jnp.bfloat16)
    second = scratch[1 - half].astype(jnp.bfloat16)
    for k in range(out_ref.shape[0]):
        out_ref[k, :, :512] = first
        out_ref[k, :, 512:] = second


def weight_kernel(codes_hbm, scales_hbm, weight_ref, codes, scales, scale_scratch, sem, code_sems):
    size = codes_hbm.shape[0] // code_chunks

    def code_copy(i):
        part = pl.ds(i * size, size)
        return pltpu.make_async_copy(codes_hbm.at[part, :], codes.at[part, :], code_sems.at[i])

    scale_copy = pltpu.make_async_copy(scales_hbm, scales, sem)
    scale_copy.start()
    for i in range(code_chunks):
        code_copy(i).start()
    scale_copy.wait()
    scale_scratch[...] = scales[...].astype(jnp.float32) * np.float32(1.0 / weight_step)

    @pl.loop(0, code_chunks)
    def _(i):
        code_copy(i).wait()
        for b in range(size // 32):
            words = codes[pl.ds(i * size + b * 32, 32), :]
            group = i * (size // 32) + b
            scale = jnp.broadcast_to(scale_scratch[pl.ds(group, 1), :], (16, 512)).astype(jnp.bfloat16)
            for k in range(4):
                power = 16.0**k
                plane = (
                    jnp.bitwise_and(words, 15 << 4 * k).astype(jnp.float32).astype(jnp.bfloat16)
                    - jnp.bfloat16(code_offset * power)
                )
                scaled = scale * jnp.bfloat16(1.0 / power)
                for part in range(2):
                    start = i * size * 4 + (b // 2) * 256 + k * 64 + (b % 2) * 32 + part * 16
                    weight_ref[pl.ds(start, 16), :] = plane[part * 16 : (part + 1) * 16] * scaled


def project_kernel(gathered_ref, hadamard_ref, weight_ref, out_ref):
    hadamard = hadamard_ref[...]
    factor = np.float32(8192.0**-0.5)
    turned = [
        jnp.dot(
            gathered_ref[:, q * 256 : (q + 1) * 256], hadamard, preferred_element_type=jnp.float32
        )
        for q in range(4)
    ]
    start = [((i // 4) % 2 * 4 + i // 8) * rows for i in range(32)]
    blocks = [turned[i % 4][start[i] : start[i] + rows] for i in range(32)]
    for bit in range(5):
        step = 1 << bit
        blocks = [
            blocks[i] + blocks[i ^ step] if i & step == 0 else blocks[i ^ step] - blocks[i]
            for i in range(32)
        ]
    total = jnp.zeros((rows, 512), jnp.float32)
    for i in range(32):
        total = total + jnp.dot(
            (blocks[i] * factor).astype(jnp.bfloat16),
            weight_ref[i * 256 : (i + 1) * 256, :],
            preferred_element_type=jnp.float32,
        )
    out_ref[...] = total.astype(jnp.bfloat16)


vmem = pl.BlockSpec(memory_space=pltpu.VMEM)
hbm = pl.BlockSpec(memory_space=pltpu.HBM)
params = pltpu.CompilerParams(vmem_limit_bytes=20 * 1024 * 1024)


def in_hbm(*arrays):
    return [pltpu.with_memory_space_constraint(array, pltpu.HBM) for array in arrays]


def per_device(
    queries,
    new_key,
    new_value,
    key_codes,
    key_scales,
    value_codes,
    value_scales,
    lengths,
    out_codes,
    out_scales,
):
    pairs = [(i, i ^ 1) for i in range(16)]
    f32, bf16, i32 = jnp.float32, jnp.bfloat16, jnp.int32
    shape = jax.ShapeDtypeStruct
    other_queries = lax.ppermute(queries, "tensor", pairs)
    keys, values, table, now, length, select, hadamard, own = pl.pallas_call(
        own_kernel,
        out_shape=(
            shape((512, 512), bf16),
            shape((512, 512), bf16),
            shape((rows, 256), f32),
            shape((2, rows, 128), bf16),
            shape((8, 128), i32),
            shape((128, 512), bf16),
            shape((256, 256), bf16),
            shape((rows, 640), f32),
        ),
        in_specs=[hbm] * 10,
        out_specs=(vmem,) * 8,
        scratch_shapes=[
            pltpu.SMEM((rows,), i32),
            pltpu.VMEM((128, 128), bf16),
            pltpu.VMEM((rows, 8, 128), bf16),
            pltpu.VMEM((rows, 8, 128), bf16),
            pltpu.VMEM((512, 128), i32),
            pltpu.VMEM((rows, half_tokens), i32),
            pltpu.VMEM((512, 128), i32),
            pltpu.VMEM((rows, half_tokens), i32),
            pltpu.VMEM((2, 16, 512), f32),
            pltpu.VMEM((136, 256), f32),
            pltpu.VMEM((128, 128), f32),
            pltpu.SemaphoreType.DMA((10,)),
        ],
        compiler_params=params,
        cost_estimate=pl.CostEstimate(flops=400_000_000, bytes_accessed=14_000_000, transcendentals=0),
        name="own_heads",
    )(
        *in_hbm(
            lengths,
            queries.reshape(128, 128),
            new_key,
            new_value,
            key_codes.reshape(512, 128),
            key_scales.reshape(rows, half_tokens),
            value_codes.reshape(512, 128),
            value_scales.reshape(rows, half_tokens),
            jnp.asarray(key_tables()),
            jnp.asarray(query_table()),
        )
    )
    sending = pl.pallas_call(
        partner_kernel,
        out_shape=shape((rows, 1280), bf16),
        in_specs=[vmem] * 8,
        out_specs=vmem,
        scratch_shapes=[pltpu.VMEM((128, 128), f32), pltpu.VMEM((rows, 640), f32)],
        compiler_params=params,
        name="other_heads",
    )(other_queries.reshape(128, 128), table, now, length, select, keys, values, own)
    received = lax.ppermute(sending, "tensor", pairs)
    out_scales, _ = lax.optimization_barrier((out_scales, sending))
    weight = pl.pallas_call(
        weight_kernel,
        out_shape=shape((8192, 512), bf16),
        in_specs=[hbm] * 2,
        out_specs=vmem,
        scratch_shapes=[
            pltpu.VMEM((2048, 512), i32),
            pltpu.VMEM((64, 512), i32),
            pltpu.VMEM((64, 512), f32),
            pltpu.SemaphoreType.DMA,
            pltpu.SemaphoreType.DMA((code_chunks,)),
        ],
        compiler_params=params,
        cost_estimate=pl.CostEstimate(flops=20_000_000, bytes_accessed=12_000_000, transcendentals=0),
        name="unpack_weight",
    )(*in_hbm(out_codes, out_scales))
    received, weight = lax.optimization_barrier((received, weight))
    attended = pl.pallas_call(
        combine_kernel,
        out_shape=shape((1, rows, 1024), bf16),
        in_specs=[vmem] * 2,
        out_specs=vmem,
        scratch_shapes=[pltpu.VMEM((2, rows, 512), f32)],
        compiler_params=params,
        name="combine_halves",
    )(sending, received)
    groups = [list(range(parity, 16, 2)) for parity in range(2)]
    strided = [[4 * k + i for k in range(4)] for i in range(4)]
    edges = [[2 * a + 1, (2 * a + 2) % 16] for a in range(8)]
    edges = [edge if a % 2 == 0 else edge[::-1] for a, edge in enumerate(edges)]
    gathered = lax.all_gather(attended[0], "tensor", axis=0, tiled=True, axis_index_groups=strided)
    gathered = lax.all_gather(gathered, "tensor", axis=0, tiled=True, axis_index_groups=edges)
    return pl.pallas_call(
        project_kernel,
        out_shape=shape((rows, 512), bf16),
        in_specs=[vmem] * 3,
        out_specs=vmem,
        compiler_params=params,
        name="project",
    )(gathered.reshape(256, 1024), hadamard, weight)


def solution(mesh):
    return jax.shard_map(
        per_device,
        mesh=mesh,
        in_specs=(
            P("dp", "tensor", None),
            P("dp", None, None),
            P("dp", None, None),
            P("dp", "tensor", None),
            P("dp", "tensor", None),
            P("dp", "tensor", None),
            P("dp", "tensor", None),
            P("dp"),
            P(None, "tensor"),
            P(None, "tensor"),
        ),
        out_specs=P("dp", "tensor"),
        check_vma=False,
    )
```

```python
import functools

import jax
import jax.numpy as jnp
import numpy as np
from jax import lax
from jax.experimental import pallas as pl
from jax.experimental.pallas import tpu as pltpu
from jax.sharding import PartitionSpec as P

rope_base = 10000.0
neg_floor = -1e30
code_offset = 7.5
cache_step = 256.0
weight_step = 8192.0

rows = 32
head_width = 128
local_heads = 4
half_tokens = 64
chunk = 8
nt = (((1,), (1,)), ((), ()))


def rope_angles(positions):
    frequency = rope_base ** (-(np.arange(64) * 2.0 / head_width))
    return np.asarray(positions, np.float64)[..., None] * frequency


def key_tables():
    lane = np.arange(512)
    plane, low, word = lane // 128, lane % 128 // 32, lane % 32
    entry = 4 * word + plane
    position = 4 * np.arange(16)[:, None] + low[None, :]
    out = []
    for half in range(2):
        angle = rope_angles(np.arange(128))[half * half_tokens + position, (entry % 64)[None, :]]
        sign = np.where(entry < 64, -1.0, 1.0)
        scale = head_width**-0.5 / cache_step
        out.append(np.stack([np.cos(angle) * scale, np.sin(angle) * sign * scale]))
    return np.stack(out).astype(np.float32)


def query_table():
    angle = rope_angles(np.arange(136))
    return np.concatenate([np.cos(angle), np.cos(angle), -np.sin(angle), np.sin(angle)], -1).astype(
        np.float32
    )


def iota(shape, dim):
    return lax.broadcasted_iota(jnp.int32, shape, dim)


def one_hot(condition):
    return jnp.where(condition, 1.0, 0.0).astype(jnp.bfloat16)


def selector():
    shape = (128, 512)
    lane = iota(shape, 1)
    return one_hot(iota(shape, 0) == 4 * (lane % 32) + lane // 128)


def swap_words():
    shape = (128, 128)
    return one_hot(iota(shape, 0) == jnp.bitwise_xor(iota(shape, 1), 16))


def token_spread():
    return one_hot(iota((64, 128), 0) % 4 == iota((64, 128), 1) // 32)


def hadamard_pair():
    shape = (256, 256)
    column = iota(shape, 1)
    target = column // 32 % 2 * 128 + 4 * (column % 32) + column // 64
    both = jnp.bitwise_and(iota(shape, 0), target)
    for shift in (4, 2, 1):
        both = jnp.bitwise_xor(both, jnp.right_shift(both, shift))
    return (1.0 - 2.0 * jnp.bitwise_and(both, 1).astype(jnp.float32)).astype(jnp.bfloat16)


def unpack_planes(codes):
    return [
        jnp.bitwise_and(jnp.right_shift(codes, 4 * j), 15).astype(jnp.float32) - code_offset
        for j in range(4)
    ]


def spread_scales(scales):
    by_row = jnp.dot(
        one_hot(iota((512, rows), 0) // 16 == iota((512, rows), 1)),
        scales.astype(jnp.float32).astype(jnp.bfloat16),
        preferred_element_type=jnp.float32,
    )
    mine = iota((512, half_tokens), 1) // 4 == iota((512, half_tokens), 0) % 16
    kept = jnp.where(mine, by_row, 0.0).astype(jnp.bfloat16)
    return jnp.dot(kept, token_spread(), preferred_element_type=jnp.float32)


def rotate_rows(vectors, cosine, sine):
    return vectors * cosine + pltpu.roll(vectors, 64, 1) * sine


def rotate_queries(q, scratch, table_ref):
    scratch[...] = q.astype(jnp.float32)
    heads = [
        rotate_rows(
            scratch[pl.ds(h, rows, stride=local_heads), :], table_ref[:, :128], table_ref[:, 128:]
        )
        for h in range(local_heads)
    ]
    return jnp.concatenate(
        [
            heads[h][b * chunk : (b + 1) * chunk]
            for b in range(rows // chunk)
            for h in range(local_heads)
        ],
        axis=0,
    ).astype(jnp.bfloat16)


def attend(
    half, length_ref, q_rot, key_now, value_now, select_ref, key_ref, value_ref, target
):
    size = local_heads * chunk
    blocks = range(rows // chunk)
    select = select_ref[...]
    spread = jnp.dot(q_rot, select, preferred_element_type=jnp.float32)
    new_scores = lax.dot_general(
        q_rot, key_now, nt, preferred_element_type=jnp.float32
    ) * np.float32(head_width**-0.5)
    row = iota((128, rows), 0)
    mine = jnp.logical_and(iota((128, rows), 1) == row // size * chunk + row % chunk, half == 0)
    new_scores = jnp.where(mine, new_scores, neg_floor)
    lane_low = iota((1, 512), 1) % 128 // 32
    row = iota((4 * size, 128), 0)
    lane = iota((4 * size, 128), 1)
    position = jnp.where(
        row % chunk == lane // 16,
        half * half_tokens + 4 * (lane % 16) + row // size,
        1 << 20,
    )
    scores, live = [], []
    for b in blocks:
        part = spread[b * size : (b + 1) * size]
        left = jnp.concatenate(
            [jnp.where(lane_low == low, part, 0.0) for low in range(4)], axis=0
        ).astype(jnp.bfloat16)
        scores.append(
            lax.dot_general(
                left, key_ref[pl.ds(b * 128, 128), :], nt, preferred_element_type=jnp.float32
            )
        )
    for b in blocks:
        live.append(position < length_ref[pl.ds(b, 1), :])
        scores[b] = jnp.where(live[b], scores[b], neg_floor)
    quarter = lambda a, low: a[low * size : (low + 1) * size]
    widest = [
        jnp.maximum(
            jnp.maximum(quarter(a, 0), quarter(a, 1)), jnp.maximum(quarter(a, 2), quarter(a, 3))
        )
        for a in scores
    ]
    top = jnp.maximum(
        jnp.max(jnp.concatenate(widest, axis=0), axis=1, keepdims=True),
        jnp.max(new_scores, axis=1, keepdims=True),
    )
    weights = []
    for b in blocks:
        shift = jnp.broadcast_to(top[b * size : (b + 1) * size], (size, 128))
        shift = jnp.concatenate([shift] * 4, axis=0)
        weights.append(jnp.where(live[b], jnp.exp(scores[b] - shift), 0.0).astype(jnp.bfloat16))
    new_weight = jnp.where(mine, jnp.exp(new_scores - top), 0.0).astype(jnp.bfloat16)
    mixed = []
    for b in blocks:
        crossed = jnp.dot(
            weights[b], value_ref[pl.ds(b * 128, 128), :], preferred_element_type=jnp.float32
        )
        kept = quarter(crossed, 0)
        for low in range(1, 4):
            kept = jnp.where(lane_low == low, quarter(crossed, low), kept)
        mixed.append(kept)
    sums = []
    for b in blocks:
        wide = weights[b].astype(jnp.float32)
        sums.append((quarter(wide, 0) + quarter(wide, 1)) + (quarter(wide, 2) + quarter(wide, 3)))
    total = jnp.sum(jnp.concatenate(sums, axis=0), axis=1, keepdims=True) + jnp.sum(
        new_weight.astype(jnp.float32), axis=1, keepdims=True
    )
    mixed = jnp.concatenate(mixed, axis=0)
    high = mixed.astype(jnp.bfloat16)
    rest = (mixed - high.astype(jnp.float32)).astype(jnp.bfloat16)
    weighted = (
        lax.dot_general(high, select, nt, preferred_element_type=jnp.float32)
        + lax.dot_general(rest, select, nt, preferred_element_type=jnp.float32)
        + jnp.dot(new_weight, value_now, preferred_element_type=jnp.float32)
    )
    some = total > 0.0
    floor_total = jnp.where(some, total, 1.0)
    logsum = jnp.where(some, top + jnp.log(floor_total), neg_floor)
    result = weighted / floor_total
    pieces = stats_of(logsum)
    lane_head = iota((chunk, 128), 1) // 32
    for b in blocks:
        at = pl.ds(b * chunk, chunk)
        tail = None
        for h in range(local_heads):
            start = b * size + h * chunk
            target[at, h * 128 : (h + 1) * 128] = result[start : start + chunk]
            stat = pieces[start : start + chunk]
            tail = stat if tail is None else jnp.where(lane_head == h, stat, tail)
        target[at, 512:640] = tail


def stats_of(logsum):
    which = iota((128, 128), 1) % 32
    whole = jnp.broadcast_to(logsum, (128, 128))
    first = whole.astype(jnp.bfloat16).astype(jnp.float32)
    second = (whole - first).astype(jnp.bfloat16).astype(jnp.float32)
    third = whole - first - second
    return jnp.where(
        which == 0, first, jnp.where(which == 1, second, jnp.where(which == 2, third, 0.0))
    )


def pick_head(array, index):
    wide = array.astype(jnp.float32)
    return jnp.sum(jnp.where(iota(wide.shape, 1) == index, wide, 0.0), axis=1)


def own_kernel(
    lengths_hbm,
    queries_hbm,
    new_key_hbm,
    new_value_hbm,
    key_codes_hbm,
    key_scales_hbm,
    value_codes_hbm,
    value_scales_hbm,
    key_table_hbm,
    query_table_hbm,
    out_codes_hbm,
    out_scales_hbm,
    key_ref,
    value_ref,
    table_ref,
    now_ref,
    length_ref,
    select_ref,
    hadamard_ref,
    own_ref,
    out_codes_ref,
    out_scales_ref,
    lengths,
    queries,
    new_key,
    new_value,
    key_codes,
    key_scales,
    value_codes,
    value_scales,
    key_table,
    query_table,
    q_scratch,
    sems,
):
    rank = lax.axis_index("tensor")
    half = lax.rem(rank, 2)
    head = lax.div(rank, 2)
    pairs = [
        (key_codes_hbm, key_codes),
        (key_scales_hbm, key_scales),
        (key_table_hbm.at[half], key_table),
        (value_codes_hbm, value_codes),
        (value_scales_hbm, value_scales),
        (lengths_hbm, lengths),
        (query_table_hbm, query_table),
        (new_key_hbm, new_key),
        (new_value_hbm, new_value),
        (queries_hbm, queries),
        (out_codes_hbm, out_codes_ref),
        (out_scales_hbm, out_scales_ref),
    ]
    copies = [
        pltpu.make_async_copy(source, target, sems.at[i]) for i, (source, target) in enumerate(pairs)
    ]
    for copy in copies:
        copy.start()
    select_ref[...] = selector()
    hadamard_ref[...] = hadamard_pair()
    swap = swap_words()
    for copy in copies[:3]:
        copy.wait()
    scales = spread_scales(key_scales[...])
    for j, plane in enumerate(unpack_planes(key_codes[...])):
        partner = jnp.dot(plane.astype(jnp.bfloat16), swap, preferred_element_type=jnp.float32)
        lanes = slice(j * 128, (j + 1) * 128)
        shape = (rows, 16, 128)
        turned = (
            plane.reshape(shape) * key_table[0, :, lanes][None]
            + partner.reshape(shape) * key_table[1, :, lanes][None]
        ).reshape(512, 128)
        key_ref[:, lanes] = (turned * scales).astype(jnp.bfloat16)
    for copy in copies[3:5]:
        copy.wait()
    scales = spread_scales(value_scales[...]) * np.float32(1.0 / cache_step)
    for j, plane in enumerate(unpack_planes(value_codes[...])):
        value_ref[:, j * 128 : (j + 1) * 128] = (plane * scales).astype(jnp.bfloat16)
    for copy in copies[5:10]:
        copy.wait()
    for r in range(rows):
        table_ref[pl.ds(r, 1), :] = query_table[pl.ds(lengths[r], 1), :]
    cosine, sine = table_ref[:, :128], table_ref[:, 128:]
    key_now = rotate_rows(pick_head(new_key[...], head), cosine, sine).astype(jnp.bfloat16)
    value_now = pick_head(new_value[...], head).astype(jnp.bfloat16)
    now_ref[0] = key_now
    now_ref[1] = value_now
    lane_row = iota((1, 128), 1) // 16
    for b in range(rows // chunk):
        line = jnp.full((1, 128), lengths[b * chunk], jnp.int32)
        for i in range(1, chunk):
            line = jnp.where(lane_row >= i, lengths[b * chunk + i], line)
        length_ref[pl.ds(b, 1), :] = line
    attend(
        half,
        length_ref,
        rotate_queries(queries[...], q_scratch, table_ref),
        key_now,
        value_now,
        select_ref,
        key_ref,
        value_ref,
        own_ref,
    )
    for copy in copies[10:]:
        copy.wait()


def partner_kernel(
    q_ref,
    table_ref,
    now_ref,
    length_ref,
    select_ref,
    key_ref,
    value_ref,
    own_ref,
    out_ref,
    q_scratch,
    out_scratch,
):
    attend(
        lax.rem(lax.axis_index("tensor"), 2),
        length_ref,
        rotate_queries(q_ref[...], q_scratch, table_ref),
        now_ref[0],
        now_ref[1],
        select_ref,
        key_ref,
        value_ref,
        out_scratch,
    )
    out_ref[:, :640] = own_ref[...].astype(jnp.bfloat16)
    out_ref[:, 640:] = out_scratch[...].astype(jnp.bfloat16)


def combine_kernel(mine_ref, theirs_ref, out_ref, scratch):
    half = lax.rem(lax.axis_index("tensor"), 2)
    lane_head = iota((rows, 128), 1) // 32
    for own in range(2):
        at, other = own * 640, 640 - own * 640
        logs = [mine_ref[:, at + 512 : at + 640], theirs_ref[:, other + 512 : other + 640]]
        logs = [log.astype(jnp.float32) for log in logs]
        for h in range(local_heads):
            mine, theirs = [
                jnp.sum(jnp.where(lane_head == h, log, 0.0), axis=1, keepdims=True) for log in logs
            ]
            joint = jnp.maximum(mine, theirs)
            mine_factor = jnp.exp(mine - joint)
            their_factor = jnp.exp(theirs - joint)
            scale = 1.0 / (mine_factor + their_factor)
            block = mine_ref[:, at + h * 128 : at + (h + 1) * 128].astype(jnp.float32)
            other_block = theirs_ref[:, other + h * 128 : other + (h + 1) * 128].astype(jnp.float32)
            scratch[own, :, h * 128 : (h + 1) * 128] = block * (
                mine_factor * scale
            ) + other_block * (their_factor * scale)
    first = scratch[half].astype(jnp.bfloat16)
    second = scratch[1 - half].astype(jnp.bfloat16)
    out_ref[:, :512] = first
    out_ref[:, 512:] = second


def weight_kernel(codes_ref, scales_ref, weight_ref, scale_scratch):
    scale_scratch[...] = scales_ref[...].astype(jnp.float32) * np.float32(1.0 / weight_step)

    @pl.loop(0, 4)
    def _(q):
        for b in range(8):
            words, scales = [], []
            for c in range(2):
                group = q * 16 + c * 8 + b
                words.append(codes_ref[pl.ds(group * 32, 32), :])
                scales.append(
                    jnp.broadcast_to(scale_scratch[pl.ds(group, 1), :], (32, 512)).astype(
                        jnp.bfloat16
                    )
                )
            for k in range(4):
                power = 16.0**k
                first, second = [
                    (
                        jnp.bitwise_and(word, 15 << 4 * k).astype(jnp.float32).astype(jnp.bfloat16)
                        - jnp.bfloat16(code_offset * power)
                    )
                    * (scale * jnp.bfloat16(1.0 / power))
                    for word, scale in zip(words, scales)
                ]
                start = q * 1024 + (b // 2) * 256 + k * 64 + (b % 2) * 32
                weight_ref[0, pl.ds(start, 32), :] = first + second
                weight_ref[1, pl.ds(start, 32), :] = first - second


def project_half(gathered_ref, hadamard_ref, weight_ref, pair_class):
    hadamard = hadamard_ref[...]
    factor = np.float32(8192.0**-0.5)
    turned = [
        jnp.dot(
            gathered_ref[:, q * 256 : (q + 1) * 256], hadamard, preferred_element_type=jnp.float32
        )
        for q in range(4)
    ]
    blocks = [turned[i % 4][i // 4 * rows : (i // 4 + 1) * rows] for i in range(16)]
    for bit in range(4):
        step = 1 << bit
        blocks = [
            blocks[i] + blocks[i ^ step] if i & step == 0 else blocks[i ^ step] - blocks[i]
            for i in range(16)
        ]
    total = None
    for i in range(16):
        term = jnp.dot(
            (blocks[i] * factor).astype(jnp.bfloat16),
            weight_ref[pair_class, i * 256 : (i + 1) * 256, :],
            preferred_element_type=jnp.float32,
        )
        total = term if total is None else total + term
    return total


def pair_class_here():
    return lax.rem(lax.div(lax.axis_index("tensor"), 2), 2)


def first_half_kernel(gathered_ref, hadamard_ref, weight_ref, out_ref):
    out_ref[...] = project_half(gathered_ref, hadamard_ref, weight_ref, pair_class_here())


def second_half_kernel(gathered_ref, hadamard_ref, weight_ref, first_ref, out_ref):
    second = project_half(gathered_ref, hadamard_ref, weight_ref, 1 - pair_class_here())
    out_ref[...] = (first_ref[...] + second).astype(jnp.bfloat16)


vmem = pl.BlockSpec(memory_space=pltpu.VMEM)
hbm = pl.BlockSpec(memory_space=pltpu.HBM)
params = pltpu.CompilerParams(vmem_limit_bytes=20 * 1024 * 1024)


def in_hbm(*arrays):
    return [pltpu.with_memory_space_constraint(array, pltpu.HBM) for array in arrays]


def per_device(
    queries,
    new_key,
    new_value,
    key_codes,
    key_scales,
    value_codes,
    value_scales,
    lengths,
    out_codes,
    out_scales,
):
    pairs = [(i, i ^ 1) for i in range(16)]
    f32, bf16, i32 = jnp.float32, jnp.bfloat16, jnp.int32
    shape = jax.ShapeDtypeStruct
    other_queries = lax.ppermute(queries, "tensor", pairs)
    outputs = pl.pallas_call(
        own_kernel,
        out_shape=(
            shape((512, 512), bf16),
            shape((512, 512), bf16),
            shape((rows, 256), f32),
            shape((2, rows, 128), bf16),
            shape((8, 128), i32),
            shape((128, 512), bf16),
            shape((256, 256), bf16),
            shape((rows, 640), f32),
            shape((2048, 512), i32),
            shape((64, 512), i32),
        ),
        in_specs=[hbm] * 12,
        out_specs=(vmem,) * 10,
        scratch_shapes=[
            pltpu.SMEM((rows,), i32),
            pltpu.VMEM((128, 128), bf16),
            pltpu.VMEM((rows, 8, 128), bf16),
            pltpu.VMEM((rows, 8, 128), bf16),
            pltpu.VMEM((512, 128), i32),
            pltpu.VMEM((rows, half_tokens), i32),
            pltpu.VMEM((512, 128), i32),
            pltpu.VMEM((rows, half_tokens), i32),
            pltpu.VMEM((2, 16, 512), f32),
            pltpu.VMEM((136, 256), f32),
            pltpu.VMEM((128, 128), f32),
            pltpu.SemaphoreType.DMA((12,)),
        ],
        compiler_params=params,
        cost_estimate=pl.CostEstimate(flops=400_000_000, bytes_accessed=14_000_000, transcendentals=0),
        name="own_heads",
    )(
        *in_hbm(
            lengths,
            queries.reshape(128, 128),
            new_key,
            new_value,
            key_codes.reshape(512, 128),
            key_scales.reshape(rows, half_tokens),
            value_codes.reshape(512, 128),
            value_scales.reshape(rows, half_tokens),
            jnp.asarray(key_tables()),
            jnp.asarray(query_table()),
            out_codes,
            out_scales,
        )
    )
    keys, values, table, now, length, select, hadamard, own, codes, scales = outputs
    sending = pl.pallas_call(
        partner_kernel,
        out_shape=shape((rows, 1280), bf16),
        in_specs=[vmem] * 8,
        out_specs=vmem,
        scratch_shapes=[pltpu.VMEM((128, 128), f32), pltpu.VMEM((rows, 640), f32)],
        compiler_params=params,
        name="other_heads",
    )(other_queries.reshape(128, 128), table, now, length, select, keys, values, own)
    received = lax.ppermute(sending, "tensor", pairs)
    scales, _ = lax.optimization_barrier((scales, sending))
    weight = pl.pallas_call(
        weight_kernel,
        out_shape=shape((2, 4096, 512), bf16),
        in_specs=[vmem] * 2,
        out_specs=vmem,
        scratch_shapes=[pltpu.VMEM((64, 512), f32)],
        compiler_params=params,
        cost_estimate=pl.CostEstimate(flops=20_000_000, bytes_accessed=12_000_000, transcendentals=0),
        name="unpack_weight",
    )(codes, scales)
    received, weight = lax.optimization_barrier((received, weight))
    attended = pl.pallas_call(
        combine_kernel,
        out_shape=shape((rows, 1024), bf16),
        in_specs=[vmem] * 2,
        out_specs=vmem,
        scratch_shapes=[pltpu.VMEM((2, rows, 512), f32)],
        compiler_params=params,
        name="combine_halves",
    )(sending, received)
    strided = [[4 * k + i for k in range(4)] for i in range(4)]
    gathered = lax.all_gather(attended, "tensor", axis=0, tiled=True, axis_index_groups=strided)
    edges = [(2 * a + 1, (2 * a + 2) % 16) for a in range(8)]
    other_class = lax.ppermute(gathered, "tensor", edges + [edge[::-1] for edge in edges])
    first = pl.pallas_call(
        first_half_kernel,
        out_shape=shape((rows, 512), f32),
        in_specs=[vmem] * 3,
        out_specs=vmem,
        compiler_params=params,
        cost_estimate=pl.CostEstimate(flops=300_000_000, bytes_accessed=5_000_000, transcendentals=0),
        name="project_first",
    )(gathered, hadamard, weight)
    return pl.pallas_call(
        second_half_kernel,
        out_shape=shape((rows, 512), bf16),
        in_specs=[vmem] * 4,
        out_specs=vmem,
        compiler_params=params,
        name="project_second",
    )(other_class, hadamard, weight, first)


def solution(mesh):
    return jax.shard_map(
        per_device,
        mesh=mesh,
        in_specs=(
            P("dp", "tensor", None),
            P("dp", None, None),
            P("dp", None, None),
            P("dp", "tensor", None),
            P("dp", "tensor", None),
            P("dp", "tensor", None),
            P("dp", "tensor", None),
            P("dp"),
            P(None, "tensor"),
            P(None, "tensor"),
        ),
        out_specs=P("dp", "tensor"),
        check_vma=False,
    )
```

```python
import functools

import jax
import jax.numpy as jnp
import numpy as np
from jax import lax
from jax.experimental import pallas as pl
from jax.experimental.pallas import tpu as pltpu
from jax.sharding import PartitionSpec as P

rope_base = 10000.0
neg_floor = -1e30
code_offset = 7.5
cache_step = 256.0
weight_step = 8192.0

rows = 32
head_width = 128
local_heads = 4
half_tokens = 64
chunk = 8
nt = (((1,), (1,)), ((), ()))


def rope_angles(positions):
    frequency = rope_base ** (-(np.arange(64) * 2.0 / head_width))
    return np.asarray(positions, np.float64)[..., None] * frequency


def key_tables():
    lane = np.arange(512)
    plane, low, word = lane // 128, lane % 128 // 32, lane % 32
    entry = 4 * word + plane
    position = 4 * np.arange(16)[:, None] + low[None, :]
    out = []
    for half in range(2):
        angle = rope_angles(np.arange(128))[half * half_tokens + position, (entry % 64)[None, :]]
        sign = np.where(entry < 64, -1.0, 1.0)
        scale = head_width**-0.5 / cache_step
        out.append(np.stack([np.cos(angle) * scale, np.sin(angle) * sign * scale]))
    return np.stack(out).astype(np.float32)


def query_table():
    angle = rope_angles(np.arange(136))
    return np.concatenate([np.cos(angle), np.cos(angle), -np.sin(angle), np.sin(angle)], -1).astype(
        np.float32
    )


def iota(shape, dim):
    return lax.broadcasted_iota(jnp.int32, shape, dim)


def one_hot(condition):
    return jnp.where(condition, 1.0, 0.0).astype(jnp.bfloat16)


def selector():
    shape = (128, 512)
    lane = iota(shape, 1)
    return one_hot(iota(shape, 0) == 4 * (lane % 32) + lane // 128)


def swap_words():
    shape = (128, 128)
    return one_hot(iota(shape, 0) == jnp.bitwise_xor(iota(shape, 1), 16))


def token_spread():
    return one_hot(iota((64, 128), 0) % 4 == iota((64, 128), 1) // 32)


def hadamard_pair():
    shape = (256, 256)
    column = iota(shape, 1)
    target = column // 32 % 2 * 128 + 4 * (column % 32) + column // 64
    both = jnp.bitwise_and(iota(shape, 0), target)
    for shift in (4, 2, 1):
        both = jnp.bitwise_xor(both, jnp.right_shift(both, shift))
    return (1.0 - 2.0 * jnp.bitwise_and(both, 1).astype(jnp.float32)).astype(jnp.bfloat16)


def unpack_planes(codes):
    return [
        jnp.bitwise_and(jnp.right_shift(codes, 4 * j), 15).astype(jnp.float32) - code_offset
        for j in range(4)
    ]


def spread_scales(scales):
    by_row = jnp.dot(
        one_hot(iota((512, rows), 0) // 16 == iota((512, rows), 1)),
        scales.astype(jnp.float32).astype(jnp.bfloat16),
        preferred_element_type=jnp.float32,
    )
    mine = iota((512, half_tokens), 1) // 4 == iota((512, half_tokens), 0) % 16
    kept = jnp.where(mine, by_row, 0.0).astype(jnp.bfloat16)
    return jnp.dot(kept, token_spread(), preferred_element_type=jnp.float32)


def rotate_rows(vectors, cosine, sine):
    return vectors * cosine + pltpu.roll(vectors, 64, 1) * sine


def rotate_queries(q, scratch, table_ref):
    scratch[...] = q.astype(jnp.float32)
    heads = [
        rotate_rows(
            scratch[pl.ds(h, rows, stride=local_heads), :], table_ref[:, :128], table_ref[:, 128:]
        )
        for h in range(local_heads)
    ]
    return jnp.concatenate(
        [
            heads[h][b * chunk : (b + 1) * chunk]
            for b in range(rows // chunk)
            for h in range(local_heads)
        ],
        axis=0,
    ).astype(jnp.bfloat16)


def attend(
    half, length_ref, q_rot, key_now, value_now, select_ref, key_ref, value_ref, target
):
    size = local_heads * chunk
    blocks = range(rows // chunk)
    select = select_ref[...]
    spread = jnp.dot(q_rot, select, preferred_element_type=jnp.float32)
    new_scores = lax.dot_general(
        q_rot, key_now, nt, preferred_element_type=jnp.float32
    ) * np.float32(head_width**-0.5)
    row = iota((128, rows), 0)
    mine = jnp.logical_and(iota((128, rows), 1) == row // size * chunk + row % chunk, half == 0)
    new_scores = jnp.where(mine, new_scores, neg_floor)
    lane_low = iota((1, 512), 1) % 128 // 32
    row = iota((4 * size, 128), 0)
    lane = iota((4 * size, 128), 1)
    position = jnp.where(
        row % chunk == lane // 16,
        half * half_tokens + 4 * (lane % 16) + row // size,
        1 << 20,
    )
    scores, live = [], []
    for b in blocks:
        part = spread[b * size : (b + 1) * size]
        left = jnp.concatenate(
            [jnp.where(lane_low == low, part, 0.0) for low in range(4)], axis=0
        ).astype(jnp.bfloat16)
        scores.append(
            lax.dot_general(
                left, key_ref[pl.ds(b * 128, 128), :], nt, preferred_element_type=jnp.float32
            )
        )
    for b in blocks:
        live.append(position < length_ref[pl.ds(b, 1), :])
        scores[b] = jnp.where(live[b], scores[b], neg_floor)
    quarter = lambda a, low: a[low * size : (low + 1) * size]
    widest = [
        jnp.maximum(
            jnp.maximum(quarter(a, 0), quarter(a, 1)), jnp.maximum(quarter(a, 2), quarter(a, 3))
        )
        for a in scores
    ]
    top = jnp.maximum(
        jnp.max(jnp.concatenate(widest, axis=0), axis=1, keepdims=True),
        jnp.max(new_scores, axis=1, keepdims=True),
    )
    weights = []
    for b in blocks:
        shift = jnp.broadcast_to(top[b * size : (b + 1) * size], (size, 128))
        shift = jnp.concatenate([shift] * 4, axis=0)
        weights.append(jnp.where(live[b], jnp.exp(scores[b] - shift), 0.0).astype(jnp.bfloat16))
    new_weight = jnp.where(mine, jnp.exp(new_scores - top), 0.0).astype(jnp.bfloat16)
    mixed = []
    for b in blocks:
        crossed = jnp.dot(
            weights[b], value_ref[pl.ds(b * 128, 128), :], preferred_element_type=jnp.float32
        )
        kept = quarter(crossed, 0)
        for low in range(1, 4):
            kept = jnp.where(lane_low == low, quarter(crossed, low), kept)
        mixed.append(kept)
    sums = []
    for b in blocks:
        wide = weights[b].astype(jnp.float32)
        sums.append((quarter(wide, 0) + quarter(wide, 1)) + (quarter(wide, 2) + quarter(wide, 3)))
    total = jnp.sum(jnp.concatenate(sums, axis=0), axis=1, keepdims=True) + jnp.sum(
        new_weight.astype(jnp.float32), axis=1, keepdims=True
    )
    mixed = jnp.concatenate(mixed, axis=0)
    high = mixed.astype(jnp.bfloat16)
    rest = (mixed - high.astype(jnp.float32)).astype(jnp.bfloat16)
    weighted = (
        lax.dot_general(high, select, nt, preferred_element_type=jnp.float32)
        + lax.dot_general(rest, select, nt, preferred_element_type=jnp.float32)
        + jnp.dot(new_weight, value_now, preferred_element_type=jnp.float32)
    )
    some = total > 0.0
    floor_total = jnp.where(some, total, 1.0)
    logsum = jnp.where(some, top + jnp.log(floor_total), neg_floor)
    result = weighted / floor_total
    pieces = stats_of(logsum)
    lane_head = iota((chunk, 128), 1) // 32
    for b in blocks:
        at = pl.ds(b * chunk, chunk)
        tail = None
        for h in range(local_heads):
            start = b * size + h * chunk
            target[at, h * 128 : (h + 1) * 128] = result[start : start + chunk]
            stat = pieces[start : start + chunk]
            tail = stat if tail is None else jnp.where(lane_head == h, stat, tail)
        target[at, 512:640] = tail


def stats_of(logsum):
    which = iota((128, 128), 1) % 32
    whole = jnp.broadcast_to(logsum, (128, 128))
    first = whole.astype(jnp.bfloat16).astype(jnp.float32)
    second = (whole - first).astype(jnp.bfloat16).astype(jnp.float32)
    third = whole - first - second
    return jnp.where(
        which == 0, first, jnp.where(which == 1, second, jnp.where(which == 2, third, 0.0))
    )


def pick_head(array, index):
    wide = array.astype(jnp.float32)
    return jnp.sum(jnp.where(iota(wide.shape, 1) == index, wide, 0.0), axis=1)


def own_kernel(
    lengths_hbm,
    queries_hbm,
    new_key_hbm,
    new_value_hbm,
    key_codes_hbm,
    key_scales_hbm,
    value_codes_hbm,
    value_scales_hbm,
    key_table_hbm,
    query_table_hbm,
    out_codes_hbm,
    out_scales_hbm,
    key_ref,
    value_ref,
    table_ref,
    now_ref,
    length_ref,
    select_ref,
    hadamard_ref,
    own_ref,
    out_codes_ref,
    out_scales_ref,
    lengths,
    queries,
    new_key,
    new_value,
    key_codes,
    key_scales,
    value_codes,
    value_scales,
    key_table,
    query_table,
    q_scratch,
    sems,
):
    rank = lax.axis_index("tensor")
    half = lax.rem(rank, 2)
    head = lax.div(rank, 2)
    pairs = [
        (key_codes_hbm, key_codes),
        (key_scales_hbm, key_scales),
        (key_table_hbm.at[half], key_table),
        (value_codes_hbm, value_codes),
        (value_scales_hbm, value_scales),
        (lengths_hbm, lengths),
        (query_table_hbm, query_table),
        (new_key_hbm, new_key),
        (new_value_hbm, new_value),
        (queries_hbm, queries),
        (out_codes_hbm, out_codes_ref),
        (out_scales_hbm, out_scales_ref),
    ]
    copies = [
        pltpu.make_async_copy(source, target, sems.at[i]) for i, (source, target) in enumerate(pairs)
    ]
    for copy in copies:
        copy.start()
    select_ref[...] = selector()
    hadamard_ref[...] = hadamard_pair()
    swap = swap_words()
    for copy in copies[:3]:
        copy.wait()
    scales = spread_scales(key_scales[...])
    for j, plane in enumerate(unpack_planes(key_codes[...])):
        partner = jnp.dot(plane.astype(jnp.bfloat16), swap, preferred_element_type=jnp.float32)
        lanes = slice(j * 128, (j + 1) * 128)
        shape = (rows, 16, 128)
        turned = (
            plane.reshape(shape) * key_table[0, :, lanes][None]
            + partner.reshape(shape) * key_table[1, :, lanes][None]
        ).reshape(512, 128)
        key_ref[:, lanes] = (turned * scales).astype(jnp.bfloat16)
    for copy in copies[3:5]:
        copy.wait()
    scales = spread_scales(value_scales[...]) * np.float32(1.0 / cache_step)
    for j, plane in enumerate(unpack_planes(value_codes[...])):
        value_ref[:, j * 128 : (j + 1) * 128] = (plane * scales).astype(jnp.bfloat16)
    for copy in copies[5:10]:
        copy.wait()
    for r in range(rows):
        table_ref[pl.ds(r, 1), :] = query_table[pl.ds(lengths[r], 1), :]
    cosine, sine = table_ref[:, :128], table_ref[:, 128:]
    key_now = rotate_rows(pick_head(new_key[...], head), cosine, sine).astype(jnp.bfloat16)
    value_now = pick_head(new_value[...], head).astype(jnp.bfloat16)
    now_ref[0] = key_now
    now_ref[1] = value_now
    lane_row = iota((1, 128), 1) // 16
    for b in range(rows // chunk):
        line = jnp.full((1, 128), lengths[b * chunk], jnp.int32)
        for i in range(1, chunk):
            line = jnp.where(lane_row >= i, lengths[b * chunk + i], line)
        length_ref[pl.ds(b, 1), :] = line
    attend(
        half,
        length_ref,
        rotate_queries(queries[...], q_scratch, table_ref),
        key_now,
        value_now,
        select_ref,
        key_ref,
        value_ref,
        own_ref,
    )
    for copy in copies[10:]:
        copy.wait()


def partner_kernel(
    q_ref,
    table_ref,
    now_ref,
    length_ref,
    select_ref,
    key_ref,
    value_ref,
    own_ref,
    out_ref,
    q_scratch,
    out_scratch,
):
    attend(
        lax.rem(lax.axis_index("tensor"), 2),
        length_ref,
        rotate_queries(q_ref[...], q_scratch, table_ref),
        now_ref[0],
        now_ref[1],
        select_ref,
        key_ref,
        value_ref,
        out_scratch,
    )
    out_ref[:, :640] = own_ref[...].astype(jnp.bfloat16)
    out_ref[:, 640:] = out_scratch[...].astype(jnp.bfloat16)


def combine_kernel(both_ref, out_ref, scratch):
    half = lax.rem(lax.axis_index("tensor"), 2)
    lane_head = iota((rows, 128), 1) // 32
    mine_ref, theirs_ref = both_ref.at[half], both_ref.at[1 - half]
    for own in range(2):
        at, other = own * 640, 640 - own * 640
        logs = [mine_ref[:, at + 512 : at + 640], theirs_ref[:, other + 512 : other + 640]]
        logs = [log.astype(jnp.float32) for log in logs]
        for h in range(local_heads):
            mine, theirs = [
                jnp.sum(jnp.where(lane_head == h, log, 0.0), axis=1, keepdims=True) for log in logs
            ]
            joint = jnp.maximum(mine, theirs)
            mine_factor = jnp.exp(mine - joint)
            their_factor = jnp.exp(theirs - joint)
            scale = 1.0 / (mine_factor + their_factor)
            block = mine_ref[:, at + h * 128 : at + (h + 1) * 128].astype(jnp.float32)
            other_block = theirs_ref[:, other + h * 128 : other + (h + 1) * 128].astype(jnp.float32)
            scratch[own, :, h * 128 : (h + 1) * 128] = block * (
                mine_factor * scale
            ) + other_block * (their_factor * scale)
    first = scratch[half].astype(jnp.bfloat16)
    second = scratch[1 - half].astype(jnp.bfloat16)
    out_ref[:, :512] = first
    out_ref[:, 512:] = second


def unpacks_early():
    return lax.axis_index("tensor") < 4


def unpack_weight(codes_ref, scales_ref, weight_ref, scale_scratch):
    scale_scratch[...] = scales_ref[...].astype(jnp.float32) * np.float32(1.0 / weight_step)

    @pl.loop(0, 8)
    def _(pair):
        for b in range(8):
            group = pair * 8 + b
            words = codes_ref[pl.ds(group * 32, 32), :]
            scale = jnp.broadcast_to(scale_scratch[pl.ds(group, 1), :], (32, 512)).astype(
                jnp.bfloat16
            )
            for k in range(4):
                power = 16.0**k
                plane = jnp.bitwise_and(words, 15 << 4 * k).astype(jnp.float32).astype(
                    jnp.bfloat16
                ) - jnp.bfloat16(code_offset * power)
                start = pair * 1024 + (b // 2) * 256 + k * 64 + (b % 2) * 32
                weight_ref[pl.ds(start, 32), :] = plane * (scale * jnp.bfloat16(1.0 / power))


def weight_kernel(codes_ref, scales_ref, weight_ref, scale_scratch):
    @pl.when(unpacks_early())
    def _():
        unpack_weight(codes_ref, scales_ref, weight_ref, scale_scratch)


def project(gathered_ref, hadamard_ref, weight_ref, out_ref):
    hadamard = hadamard_ref[...]
    turned = [
        jnp.dot(
            gathered_ref[:, q * 256 : (q + 1) * 256], hadamard, preferred_element_type=jnp.float32
        )
        for q in range(4)
    ]
    start = [(i // 4 % 2 * 4 + i // 8) * rows for i in range(32)]
    blocks = [turned[i % 4][start[i] : start[i] + rows] for i in range(32)]
    for bit in range(5):
        step = 1 << bit
        blocks = [
            blocks[i] + blocks[i ^ step] if i & step == 0 else blocks[i ^ step] - blocks[i]
            for i in range(32)
        ]
    total = None
    for i in range(32):
        term = jnp.dot(
            blocks[i].astype(jnp.bfloat16),
            weight_ref[i * 256 : (i + 1) * 256, :],
            preferred_element_type=jnp.float32,
        )
        total = term if total is None else total + term
    out_ref[...] = (total * np.float32(8192.0**-0.5)).astype(jnp.bfloat16)


def project_kernel(
    gathered_ref, hadamard_ref, weight_ref, codes_ref, scales_ref, out_ref, late_weight, scale_scratch
):
    early = unpacks_early()

    @pl.when(early)
    def _():
        project(gathered_ref, hadamard_ref, weight_ref, out_ref)

    @pl.when(jnp.logical_not(early))
    def _():
        unpack_weight(codes_ref, scales_ref, late_weight, scale_scratch)
        project(gathered_ref, hadamard_ref, late_weight, out_ref)


vmem = pl.BlockSpec(memory_space=pltpu.VMEM)
hbm = pl.BlockSpec(memory_space=pltpu.HBM)
params = pltpu.CompilerParams(vmem_limit_bytes=20 * 1024 * 1024)


def in_hbm(*arrays):
    return [pltpu.with_memory_space_constraint(array, pltpu.HBM) for array in arrays]


def per_device(
    queries,
    new_key,
    new_value,
    key_codes,
    key_scales,
    value_codes,
    value_scales,
    lengths,
    out_codes,
    out_scales,
):
    pairs = [(i, i ^ 1) for i in range(16)]
    f32, bf16, i32 = jnp.float32, jnp.bfloat16, jnp.int32
    shape = jax.ShapeDtypeStruct
    other_queries = lax.ppermute(queries, "tensor", pairs)
    outputs = pl.pallas_call(
        own_kernel,
        out_shape=(
            shape((512, 512), bf16),
            shape((512, 512), bf16),
            shape((rows, 256), f32),
            shape((2, rows, 128), bf16),
            shape((8, 128), i32),
            shape((128, 512), bf16),
            shape((256, 256), bf16),
            shape((rows, 640), f32),
            shape((2048, 512), i32),
            shape((64, 512), i32),
        ),
        in_specs=[hbm] * 12,
        out_specs=(vmem,) * 10,
        scratch_shapes=[
            pltpu.SMEM((rows,), i32),
            pltpu.VMEM((128, 128), bf16),
            pltpu.VMEM((rows, 8, 128), bf16),
            pltpu.VMEM((rows, 8, 128), bf16),
            pltpu.VMEM((512, 128), i32),
            pltpu.VMEM((rows, half_tokens), i32),
            pltpu.VMEM((512, 128), i32),
            pltpu.VMEM((rows, half_tokens), i32),
            pltpu.VMEM((2, 16, 512), f32),
            pltpu.VMEM((136, 256), f32),
            pltpu.VMEM((128, 128), f32),
            pltpu.SemaphoreType.DMA((12,)),
        ],
        compiler_params=params,
        cost_estimate=pl.CostEstimate(flops=400_000_000, bytes_accessed=14_000_000, transcendentals=0),
        name="own_heads",
    )(
        *in_hbm(
            lengths,
            queries.reshape(128, 128),
            new_key,
            new_value,
            key_codes.reshape(512, 128),
            key_scales.reshape(rows, half_tokens),
            value_codes.reshape(512, 128),
            value_scales.reshape(rows, half_tokens),
            jnp.asarray(key_tables()),
            jnp.asarray(query_table()),
            out_codes,
            out_scales,
        )
    )
    keys, values, table, now, length, select, hadamard, own, codes, scales = outputs
    sending = pl.pallas_call(
        partner_kernel,
        out_shape=shape((rows, 1280), bf16),
        in_specs=[vmem] * 8,
        out_specs=vmem,
        scratch_shapes=[pltpu.VMEM((128, 128), f32), pltpu.VMEM((rows, 640), f32)],
        compiler_params=params,
        name="other_heads",
    )(other_queries.reshape(128, 128), table, now, length, select, keys, values, own)
    both = lax.all_gather(
        sending, "tensor", axis=0, axis_index_groups=[[2 * a, 2 * a + 1] for a in range(8)]
    )
    scales, _ = lax.optimization_barrier((scales, both))
    weight = pl.pallas_call(
        weight_kernel,
        out_shape=shape((8192, 512), bf16),
        in_specs=[vmem] * 2,
        out_specs=vmem,
        scratch_shapes=[pltpu.VMEM((64, 512), f32)],
        compiler_params=params,
        cost_estimate=pl.CostEstimate(flops=20_000_000, bytes_accessed=12_000_000, transcendentals=0),
        name="unpack_weight",
    )(codes, scales)
    both, weight = lax.optimization_barrier((both, weight))
    attended = pl.pallas_call(
        combine_kernel,
        out_shape=shape((rows, 1024), bf16),
        in_specs=[vmem],
        out_specs=vmem,
        scratch_shapes=[pltpu.VMEM((2, rows, 512), f32)],
        compiler_params=params,
        name="combine_halves",
    )(both)
    strided = [[4 * k + i for k in range(4)] for i in range(4)]
    gathered = lax.all_gather(attended, "tensor", axis=0, tiled=True, axis_index_groups=strided)
    edges = [[2 * a + 1, (2 * a + 2) % 16] for a in range(8)]
    edges = [edge if a % 2 == 0 else edge[::-1] for a, edge in enumerate(edges)]
    gathered = lax.all_gather(gathered, "tensor", axis=0, tiled=True, axis_index_groups=edges)
    return pl.pallas_call(
        project_kernel,
        out_shape=shape((rows, 512), bf16),
        in_specs=[vmem] * 5,
        out_specs=vmem,
        scratch_shapes=[pltpu.VMEM((8192, 512), bf16), pltpu.VMEM((64, 512), f32)],
        compiler_params=params,
        name="project",
    )(gathered, hadamard, weight, codes, scales)


def solution(mesh):
    return jax.shard_map(
        per_device,
        mesh=mesh,
        in_specs=(
            P("dp", "tensor", None),
            P("dp", None, None),
            P("dp", None, None),
            P("dp", "tensor", None),
            P("dp", "tensor", None),
            P("dp", "tensor", None),
            P("dp", "tensor", None),
            P("dp"),
            P(None, "tensor"),
            P(None, "tensor"),
        ),
        out_specs=P("dp", "tensor"),
        check_vma=False,
    )
```

```python
import functools

import jax
import jax.numpy as jnp
import numpy as np
from jax import lax
from jax.experimental import pallas as pl
from jax.experimental.pallas import tpu as pltpu
from jax.sharding import PartitionSpec as P

rope_base = 10000.0
neg_floor = -1e30
code_offset = 7.5
cache_step = 256.0
weight_step = 8192.0

rows = 32
head_width = 128
local_heads = 4
half_tokens = 64
chunk = 8
nt = (((1,), (1,)), ((), ()))


def rope_angles(positions):
    frequency = rope_base ** (-(np.arange(64) * 2.0 / head_width))
    return np.asarray(positions, np.float64)[..., None] * frequency


def key_tables():
    lane = np.arange(512)
    plane, low, word = lane // 128, lane % 128 // 32, lane % 32
    entry = 4 * word + plane
    position = 4 * np.arange(16)[:, None] + low[None, :]
    out = []
    for half in range(2):
        angle = rope_angles(np.arange(128))[half * half_tokens + position, (entry % 64)[None, :]]
        sign = np.where(entry < 64, -1.0, 1.0)
        scale = head_width**-0.5 / cache_step
        out.append(np.stack([np.cos(angle) * scale, np.sin(angle) * sign * scale]))
    return np.stack(out).astype(np.float32)


def query_table():
    angle = rope_angles(np.arange(136))
    return np.concatenate([np.cos(angle), np.cos(angle), -np.sin(angle), np.sin(angle)], -1).astype(
        np.float32
    )


def iota(shape, dim):
    return lax.broadcasted_iota(jnp.int32, shape, dim)


def one_hot(condition):
    return jnp.where(condition, 1.0, 0.0).astype(jnp.bfloat16)


def selector():
    shape = (128, 512)
    lane = iota(shape, 1)
    return one_hot(iota(shape, 0) == 4 * (lane % 32) + lane // 128)


def swap_words():
    shape = (128, 128)
    return one_hot(iota(shape, 0) == jnp.bitwise_xor(iota(shape, 1), 16))


def token_spread():
    return one_hot(iota((64, 128), 0) % 4 == iota((64, 128), 1) // 32)


def hadamard_pair():
    shape = (256, 256)
    column = iota(shape, 1)
    target = column // 32 % 2 * 128 + 4 * (column % 32) + column // 64
    both = jnp.bitwise_and(iota(shape, 0), target)
    for shift in (4, 2, 1):
        both = jnp.bitwise_xor(both, jnp.right_shift(both, shift))
    return (1.0 - 2.0 * jnp.bitwise_and(both, 1).astype(jnp.float32)).astype(jnp.bfloat16)


def unpack_planes(codes):
    return [
        jnp.bitwise_and(jnp.right_shift(codes, 4 * j), 15).astype(jnp.float32) - code_offset
        for j in range(4)
    ]


def spread_scales(scales):
    by_row = jnp.dot(
        one_hot(iota((512, rows), 0) // 16 == iota((512, rows), 1)),
        scales.astype(jnp.float32).astype(jnp.bfloat16),
        preferred_element_type=jnp.float32,
    )
    mine = iota((512, half_tokens), 1) // 4 == iota((512, half_tokens), 0) % 16
    kept = jnp.where(mine, by_row, 0.0).astype(jnp.bfloat16)
    return jnp.dot(kept, token_spread(), preferred_element_type=jnp.float32)


def rotate_rows(vectors, cosine, sine):
    return vectors * cosine + pltpu.roll(vectors, 64, 1) * sine


def rotate_queries(q, scratch, table_ref):
    scratch[...] = q.astype(jnp.float32)
    heads = [
        rotate_rows(
            scratch[pl.ds(h, rows, stride=local_heads), :], table_ref[:, :128], table_ref[:, 128:]
        )
        for h in range(local_heads)
    ]
    return jnp.concatenate(
        [
            heads[h][b * chunk : (b + 1) * chunk]
            for b in range(rows // chunk)
            for h in range(local_heads)
        ],
        axis=0,
    ).astype(jnp.bfloat16)


def attend(
    half, length_ref, q_rot, key_now, value_now, select_ref, key_ref, value_ref, target
):
    size = local_heads * chunk
    blocks = range(rows // chunk)
    select = select_ref[...]
    spread = jnp.dot(q_rot, select, preferred_element_type=jnp.float32)
    new_scores = lax.dot_general(
        q_rot, key_now, nt, preferred_element_type=jnp.float32
    ) * np.float32(head_width**-0.5)
    row = iota((128, rows), 0)
    mine = jnp.logical_and(iota((128, rows), 1) == row // size * chunk + row % chunk, half == 0)
    new_scores = jnp.where(mine, new_scores, neg_floor)
    lane_low = iota((1, 512), 1) % 128 // 32
    row = iota((4 * size, 128), 0)
    lane = iota((4 * size, 128), 1)
    position = jnp.where(
        row % chunk == lane // 16,
        half * half_tokens + 4 * (lane % 16) + row // size,
        1 << 20,
    )
    scores, live = [], []
    for b in blocks:
        part = spread[b * size : (b + 1) * size]
        left = jnp.concatenate(
            [jnp.where(lane_low == low, part, 0.0) for low in range(4)], axis=0
        ).astype(jnp.bfloat16)
        scores.append(
            lax.dot_general(
                left, key_ref[pl.ds(b * 128, 128), :], nt, preferred_element_type=jnp.float32
            )
        )
    for b in blocks:
        live.append(position < length_ref[pl.ds(b, 1), :])
        scores[b] = jnp.where(live[b], scores[b], neg_floor)
    quarter = lambda a, low: a[low * size : (low + 1) * size]
    widest = [
        jnp.maximum(
            jnp.maximum(quarter(a, 0), quarter(a, 1)), jnp.maximum(quarter(a, 2), quarter(a, 3))
        )
        for a in scores
    ]
    top = jnp.maximum(
        jnp.max(jnp.concatenate(widest, axis=0), axis=1, keepdims=True),
        jnp.max(new_scores, axis=1, keepdims=True),
    )
    weights = []
    for b in blocks:
        shift = jnp.broadcast_to(top[b * size : (b + 1) * size], (size, 128))
        shift = jnp.concatenate([shift] * 4, axis=0)
        weights.append(jnp.where(live[b], jnp.exp(scores[b] - shift), 0.0).astype(jnp.bfloat16))
    new_weight = jnp.where(mine, jnp.exp(new_scores - top), 0.0).astype(jnp.bfloat16)
    mixed = []
    for b in blocks:
        crossed = jnp.dot(
            weights[b], value_ref[pl.ds(b * 128, 128), :], preferred_element_type=jnp.float32
        )
        kept = quarter(crossed, 0)
        for low in range(1, 4):
            kept = jnp.where(lane_low == low, quarter(crossed, low), kept)
        mixed.append(kept)
    sums = []
    for b in blocks:
        wide = weights[b].astype(jnp.float32)
        sums.append((quarter(wide, 0) + quarter(wide, 1)) + (quarter(wide, 2) + quarter(wide, 3)))
    total = jnp.sum(jnp.concatenate(sums, axis=0), axis=1, keepdims=True) + jnp.sum(
        new_weight.astype(jnp.float32), axis=1, keepdims=True
    )
    mixed = jnp.concatenate(mixed, axis=0)
    high = mixed.astype(jnp.bfloat16)
    rest = (mixed - high.astype(jnp.float32)).astype(jnp.bfloat16)
    weighted = (
        lax.dot_general(high, select, nt, preferred_element_type=jnp.float32)
        + lax.dot_general(rest, select, nt, preferred_element_type=jnp.float32)
        + jnp.dot(new_weight, value_now, preferred_element_type=jnp.float32)
    )
    some = total > 0.0
    floor_total = jnp.where(some, total, 1.0)
    logsum = jnp.where(some, top + jnp.log(floor_total), neg_floor)
    result = weighted / floor_total
    pieces = stats_of(logsum)
    lane_head = iota((chunk, 128), 1) // 32
    for b in blocks:
        at = pl.ds(b * chunk, chunk)
        tail = None
        for h in range(local_heads):
            start = b * size + h * chunk
            target[at, h * 128 : (h + 1) * 128] = result[start : start + chunk]
            stat = pieces[start : start + chunk]
            tail = stat if tail is None else jnp.where(lane_head == h, stat, tail)
        target[at, 512:640] = tail


def stats_of(logsum):
    which = iota((128, 128), 1) % 32
    whole = jnp.broadcast_to(logsum, (128, 128))
    first = whole.astype(jnp.bfloat16).astype(jnp.float32)
    second = (whole - first).astype(jnp.bfloat16).astype(jnp.float32)
    third = whole - first - second
    return jnp.where(
        which == 0, first, jnp.where(which == 1, second, jnp.where(which == 2, third, 0.0))
    )


def pick_head(array, index):
    wide = array.astype(jnp.float32)
    return jnp.sum(jnp.where(iota(wide.shape, 1) == index, wide, 0.0), axis=1)


def own_kernel(
    lengths_hbm,
    queries_hbm,
    new_key_hbm,
    new_value_hbm,
    key_codes_hbm,
    key_scales_hbm,
    value_codes_hbm,
    value_scales_hbm,
    key_table_hbm,
    query_table_hbm,
    out_codes_hbm,
    out_scales_hbm,
    key_ref,
    value_ref,
    table_ref,
    now_ref,
    length_ref,
    select_ref,
    hadamard_ref,
    own_ref,
    out_codes_ref,
    out_scales_ref,
    lengths,
    queries,
    new_key,
    new_value,
    key_codes,
    key_scales,
    value_codes,
    value_scales,
    key_table,
    query_table,
    q_scratch,
    sems,
):
    rank = lax.axis_index("tensor")
    half = lax.rem(rank, 2)
    head = lax.div(rank, 2)
    pairs = [
        (key_codes_hbm, key_codes),
        (key_scales_hbm, key_scales),
        (key_table_hbm.at[half], key_table),
        (value_codes_hbm, value_codes),
        (value_scales_hbm, value_scales),
        (lengths_hbm, lengths),
        (query_table_hbm, query_table),
        (new_key_hbm, new_key),
        (new_value_hbm, new_value),
        (queries_hbm, queries),
        (out_codes_hbm, out_codes_ref),
        (out_scales_hbm, out_scales_ref),
    ]
    copies = [
        pltpu.make_async_copy(source, target, sems.at[i]) for i, (source, target) in enumerate(pairs)
    ]
    for copy in copies:
        copy.start()
    select_ref[...] = selector()
    hadamard_ref[...] = hadamard_pair()
    swap = swap_words()
    for copy in copies[:3]:
        copy.wait()
    scales = spread_scales(key_scales[...])
    for j, plane in enumerate(unpack_planes(key_codes[...])):
        partner = jnp.dot(plane.astype(jnp.bfloat16), swap, preferred_element_type=jnp.float32)
        lanes = slice(j * 128, (j + 1) * 128)
        shape = (rows, 16, 128)
        turned = (
            plane.reshape(shape) * key_table[0, :, lanes][None]
            + partner.reshape(shape) * key_table[1, :, lanes][None]
        ).reshape(512, 128)
        key_ref[:, lanes] = (turned * scales).astype(jnp.bfloat16)
    for copy in copies[3:5]:
        copy.wait()
    scales = spread_scales(value_scales[...]) * np.float32(1.0 / cache_step)
    for j, plane in enumerate(unpack_planes(value_codes[...])):
        value_ref[:, j * 128 : (j + 1) * 128] = (plane * scales).astype(jnp.bfloat16)
    for copy in copies[5:10]:
        copy.wait()
    for r in range(rows):
        table_ref[pl.ds(r, 1), :] = query_table[pl.ds(lengths[r], 1), :]
    cosine, sine = table_ref[:, :128], table_ref[:, 128:]
    key_now = rotate_rows(pick_head(new_key[...], head), cosine, sine).astype(jnp.bfloat16)
    value_now = pick_head(new_value[...], head).astype(jnp.bfloat16)
    now_ref[0] = key_now
    now_ref[1] = value_now
    lane_row = iota((1, 128), 1) // 16
    for b in range(rows // chunk):
        line = jnp.full((1, 128), lengths[b * chunk], jnp.int32)
        for i in range(1, chunk):
            line = jnp.where(lane_row >= i, lengths[b * chunk + i], line)
        length_ref[pl.ds(b, 1), :] = line
    attend(
        half,
        length_ref,
        rotate_queries(queries[...], q_scratch, table_ref),
        key_now,
        value_now,
        select_ref,
        key_ref,
        value_ref,
        own_ref,
    )
    for copy in copies[10:]:
        copy.wait()


def partner_kernel(
    q_ref,
    table_ref,
    now_ref,
    length_ref,
    select_ref,
    key_ref,
    value_ref,
    own_ref,
    out_ref,
    q_scratch,
    out_scratch,
):
    attend(
        lax.rem(lax.axis_index("tensor"), 2),
        length_ref,
        rotate_queries(q_ref[...], q_scratch, table_ref),
        now_ref[0],
        now_ref[1],
        select_ref,
        key_ref,
        value_ref,
        out_scratch,
    )
    out_ref[:, :640] = own_ref[...].astype(jnp.bfloat16)
    out_ref[:, 640:] = out_scratch[...].astype(jnp.bfloat16)


def combine_kernel(mine_ref, theirs_ref, out_ref, scratch):
    half = lax.rem(lax.axis_index("tensor"), 2)
    lane_head = iota((rows, 128), 1) // 32
    for own in range(2):
        at, other = own * 640, 640 - own * 640
        logs = [mine_ref[:, at + 512 : at + 640], theirs_ref[:, other + 512 : other + 640]]
        logs = [log.astype(jnp.float32) for log in logs]
        for h in range(local_heads):
            mine, theirs = [
                jnp.sum(jnp.where(lane_head == h, log, 0.0), axis=1, keepdims=True) for log in logs
            ]
            joint = jnp.maximum(mine, theirs)
            mine_factor = jnp.exp(mine - joint)
            their_factor = jnp.exp(theirs - joint)
            scale = 1.0 / (mine_factor + their_factor)
            block = mine_ref[:, at + h * 128 : at + (h + 1) * 128].astype(jnp.float32)
            other_block = theirs_ref[:, other + h * 128 : other + (h + 1) * 128].astype(jnp.float32)
            scratch[own, :, h * 128 : (h + 1) * 128] = block * (
                mine_factor * scale
            ) + other_block * (their_factor * scale)
    first = scratch[half].astype(jnp.bfloat16)
    second = scratch[1 - half].astype(jnp.bfloat16)
    out_ref[:, :512] = first
    out_ref[:, 512:] = second


def weight_kernel(codes_ref, scales_ref, weight_ref, scale_scratch):
    scale_scratch[...] = scales_ref[...].astype(jnp.float32) * np.float32(1.0 / weight_step)

    @pl.loop(0, 4)
    def _(q):
        for b in range(8):
            words, scales = [], []
            for c in range(2):
                group = q * 16 + c * 8 + b
                words.append(codes_ref[pl.ds(group * 32, 32), :])
                scales.append(
                    jnp.broadcast_to(scale_scratch[pl.ds(group, 1), :], (32, 512)).astype(
                        jnp.bfloat16
                    )
                )
            for k in range(4):
                power = 16.0**k
                first, second = [
                    (
                        jnp.bitwise_and(word, 15 << 4 * k).astype(jnp.float32).astype(jnp.bfloat16)
                        - jnp.bfloat16(code_offset * power)
                    )
                    * (scale * jnp.bfloat16(1.0 / power))
                    for word, scale in zip(words, scales)
                ]
                start = q * 1024 + (b // 2) * 256 + k * 64 + (b % 2) * 32
                weight_ref[0, pl.ds(start, 32), :] = first + second
                weight_ref[1, pl.ds(start, 32), :] = first - second


def project_half(gathered_ref, hadamard_ref, weight_ref, pair_class):
    hadamard = hadamard_ref[...]
    turned = [
        jnp.dot(
            gathered_ref[:, q * 256 : (q + 1) * 256], hadamard, preferred_element_type=jnp.float32
        )
        for q in range(4)
    ]
    blocks = [turned[i % 4][i // 4 * rows : (i // 4 + 1) * rows] for i in range(16)]
    for bit in range(4):
        step = 1 << bit
        blocks = [
            blocks[i] + blocks[i ^ step] if i & step == 0 else blocks[i ^ step] - blocks[i]
            for i in range(16)
        ]
    total = None
    for i in range(16):
        term = jnp.dot(
            blocks[i].astype(jnp.bfloat16),
            weight_ref[pair_class, i * 256 : (i + 1) * 256, :],
            preferred_element_type=jnp.float32,
        )
        total = term if total is None else total + term
    return total


def project_kernel(gathered_ref, hadamard_ref, weight_ref, out_ref):
    parts = [
        project_half(gathered_ref.at[c * 128 : (c + 1) * 128], hadamard_ref, weight_ref, c)
        for c in range(2)
    ]
    out_ref[...] = ((parts[0] + parts[1]) * np.float32(8192.0**-0.5)).astype(jnp.bfloat16)


vmem = pl.BlockSpec(memory_space=pltpu.VMEM)
hbm = pl.BlockSpec(memory_space=pltpu.HBM)
params = pltpu.CompilerParams(vmem_limit_bytes=20 * 1024 * 1024)


def in_hbm(*arrays):
    return [pltpu.with_memory_space_constraint(array, pltpu.HBM) for array in arrays]


def per_device(
    queries,
    new_key,
    new_value,
    key_codes,
    key_scales,
    value_codes,
    value_scales,
    lengths,
    out_codes,
    out_scales,
):
    pairs = [(i, i ^ 1) for i in range(16)]
    f32, bf16, i32 = jnp.float32, jnp.bfloat16, jnp.int32
    shape = jax.ShapeDtypeStruct
    other_queries = lax.ppermute(queries, "tensor", pairs)
    outputs = pl.pallas_call(
        own_kernel,
        out_shape=(
            shape((512, 512), bf16),
            shape((512, 512), bf16),
            shape((rows, 256), f32),
            shape((2, rows, 128), bf16),
            shape((8, 128), i32),
            shape((128, 512), bf16),
            shape((256, 256), bf16),
            shape((rows, 640), f32),
            shape((2048, 512), i32),
            shape((64, 512), i32),
        ),
        in_specs=[hbm] * 12,
        out_specs=(vmem,) * 10,
        scratch_shapes=[
            pltpu.SMEM((rows,), i32),
            pltpu.VMEM((128, 128), bf16),
            pltpu.VMEM((rows, 8, 128), bf16),
            pltpu.VMEM((rows, 8, 128), bf16),
            pltpu.VMEM((512, 128), i32),
            pltpu.VMEM((rows, half_tokens), i32),
            pltpu.VMEM((512, 128), i32),
            pltpu.VMEM((rows, half_tokens), i32),
            pltpu.VMEM((2, 16, 512), f32),
            pltpu.VMEM((136, 256), f32),
            pltpu.VMEM((128, 128), f32),
            pltpu.SemaphoreType.DMA((12,)),
        ],
        compiler_params=params,
        cost_estimate=pl.CostEstimate(flops=400_000_000, bytes_accessed=14_000_000, transcendentals=0),
        name="own_heads",
    )(
        *in_hbm(
            lengths,
            queries.reshape(128, 128),
            new_key,
            new_value,
            key_codes.reshape(512, 128),
            key_scales.reshape(rows, half_tokens),
            value_codes.reshape(512, 128),
            value_scales.reshape(rows, half_tokens),
            jnp.asarray(key_tables()),
            jnp.asarray(query_table()),
            out_codes,
            out_scales,
        )
    )
    keys, values, table, now, length, select, hadamard, own, codes, scales = outputs
    sending = pl.pallas_call(
        partner_kernel,
        out_shape=shape((rows, 1280), bf16),
        in_specs=[vmem] * 8,
        out_specs=vmem,
        scratch_shapes=[pltpu.VMEM((128, 128), f32), pltpu.VMEM((rows, 640), f32)],
        compiler_params=params,
        name="other_heads",
    )(other_queries.reshape(128, 128), table, now, length, select, keys, values, own)
    received = lax.ppermute(sending, "tensor", pairs)
    scales, _ = lax.optimization_barrier((scales, sending))
    weight = pl.pallas_call(
        weight_kernel,
        out_shape=shape((2, 4096, 512), bf16),
        in_specs=[vmem] * 2,
        out_specs=vmem,
        scratch_shapes=[pltpu.VMEM((64, 512), f32)],
        compiler_params=params,
        cost_estimate=pl.CostEstimate(flops=20_000_000, bytes_accessed=12_000_000, transcendentals=0),
        name="unpack_weight",
    )(codes, scales)
    received, weight = lax.optimization_barrier((received, weight))
    attended = pl.pallas_call(
        combine_kernel,
        out_shape=shape((rows, 1024), bf16),
        in_specs=[vmem] * 2,
        out_specs=vmem,
        scratch_shapes=[pltpu.VMEM((2, rows, 512), f32)],
        compiler_params=params,
        name="combine_halves",
    )(sending, received)
    strided = [[4 * k + i for k in range(4)] for i in range(4)]
    gathered = lax.all_gather(attended, "tensor", axis=0, tiled=True, axis_index_groups=strided)
    edges = [[2 * a + 1, (2 * a + 2) % 16] for a in range(8)]
    edges = [edge if a % 2 == 0 else edge[::-1] for a, edge in enumerate(edges)]
    gathered = lax.all_gather(gathered, "tensor", axis=0, tiled=True, axis_index_groups=edges)
    return pl.pallas_call(
        project_kernel,
        out_shape=shape((rows, 512), bf16),
        in_specs=[vmem] * 3,
        out_specs=vmem,
        compiler_params=params,
        name="project",
    )(gathered, hadamard, weight)


def solution(mesh):
    return jax.shard_map(
        per_device,
        mesh=mesh,
        in_specs=(
            P("dp", "tensor", None),
            P("dp", None, None),
            P("dp", None, None),
            P("dp", "tensor", None),
            P("dp", "tensor", None),
            P("dp", "tensor", None),
            P("dp", "tensor", None),
            P("dp"),
            P(None, "tensor"),
            P(None, "tensor"),
        ),
        out_specs=P("dp", "tensor"),
        check_vma=False,
    )
```

```python
import functools

import jax
import jax.numpy as jnp
import numpy as np
from jax import lax
from jax.experimental import pallas as pl
from jax.experimental.pallas import tpu as pltpu
from jax.sharding import PartitionSpec as P

rope_base = 10000.0
neg_floor = -1e30
code_offset = 7.5
cache_step = 256.0
weight_step = 8192.0

rows = 32
head_width = 128
local_heads = 4
half_tokens = 64
chunk = 8
nt = (((1,), (1,)), ((), ()))


def rope_angles(positions):
    frequency = rope_base ** (-(np.arange(64) * 2.0 / head_width))
    return np.asarray(positions, np.float64)[..., None] * frequency


def key_tables():
    lane = np.arange(512)
    plane, low, word = lane // 128, lane % 128 // 32, lane % 32
    entry = 4 * word + plane
    position = 4 * np.arange(16)[:, None] + low[None, :]
    out = []
    for half in range(2):
        angle = rope_angles(np.arange(128))[half * half_tokens + position, (entry % 64)[None, :]]
        sign = np.where(entry < 64, -1.0, 1.0)
        scale = head_width**-0.5 / cache_step
        out.append(np.stack([np.cos(angle) * scale, np.sin(angle) * sign * scale]))
    return np.stack(out).astype(np.float32)


def query_table():
    angle = rope_angles(np.arange(136))
    return np.concatenate([np.cos(angle), np.cos(angle), -np.sin(angle), np.sin(angle)], -1).astype(
        np.float32
    )


def iota(shape, dim):
    return lax.broadcasted_iota(jnp.int32, shape, dim)


def one_hot(condition):
    return jnp.where(condition, 1.0, 0.0).astype(jnp.bfloat16)


def selector():
    shape = (128, 512)
    lane = iota(shape, 1)
    return one_hot(iota(shape, 0) == 4 * (lane % 32) + lane // 128)


def swap_words():
    shape = (128, 128)
    return one_hot(iota(shape, 0) == jnp.bitwise_xor(iota(shape, 1), 16))


def token_spread():
    return one_hot(iota((64, 128), 0) % 4 == iota((64, 128), 1) // 32)


def hadamard_pair():
    shape = (256, 256)
    column = iota(shape, 1)
    target = column // 32 % 2 * 128 + 4 * (column % 32) + column // 64
    both = jnp.bitwise_and(iota(shape, 0), target)
    for shift in (4, 2, 1):
        both = jnp.bitwise_xor(both, jnp.right_shift(both, shift))
    return (1.0 - 2.0 * jnp.bitwise_and(both, 1).astype(jnp.float32)).astype(jnp.bfloat16)


def unpack_planes(codes):
    return [
        jnp.bitwise_and(jnp.right_shift(codes, 4 * j), 15).astype(jnp.float32) - code_offset
        for j in range(4)
    ]


def spread_scales(scales):
    by_row = jnp.dot(
        one_hot(iota((512, rows), 0) // 16 == iota((512, rows), 1)),
        scales.astype(jnp.float32).astype(jnp.bfloat16),
        preferred_element_type=jnp.float32,
    )
    mine = iota((512, half_tokens), 1) // 4 == iota((512, half_tokens), 0) % 16
    kept = jnp.where(mine, by_row, 0.0).astype(jnp.bfloat16)
    return jnp.dot(kept, token_spread(), preferred_element_type=jnp.float32)


def rotate_rows(vectors, cosine, sine):
    return vectors * cosine + pltpu.roll(vectors, 64, 1) * sine


def rotate_queries(q, scratch, table_ref):
    scratch[...] = q.astype(jnp.float32)
    heads = [
        rotate_rows(
            scratch[pl.ds(h, rows, stride=local_heads), :], table_ref[:, :128], table_ref[:, 128:]
        )
        for h in range(local_heads)
    ]
    return jnp.concatenate(
        [
            heads[h][b * chunk : (b + 1) * chunk]
            for b in range(rows // chunk)
            for h in range(local_heads)
        ],
        axis=0,
    ).astype(jnp.bfloat16)


def attend(
    half, length_ref, q_rot, key_now, value_now, select_ref, key_ref, value_ref, target
):
    size = local_heads * chunk
    blocks = range(rows // chunk)
    select = select_ref[...]
    spread = jnp.dot(q_rot, select, preferred_element_type=jnp.float32)
    new_scores = lax.dot_general(
        q_rot, key_now, nt, preferred_element_type=jnp.float32
    ) * np.float32(head_width**-0.5)
    row = iota((128, rows), 0)
    mine = jnp.logical_and(iota((128, rows), 1) == row // size * chunk + row % chunk, half == 0)
    new_scores = jnp.where(mine, new_scores, neg_floor)
    lane_low = iota((1, 512), 1) % 128 // 32
    row = iota((4 * size, 128), 0)
    lane = iota((4 * size, 128), 1)
    position = jnp.where(
        row % chunk == lane // 16,
        half * half_tokens + 4 * (lane % 16) + row // size,
        1 << 20,
    )
    scores, live = [], []
    for b in blocks:
        part = spread[b * size : (b + 1) * size]
        left = jnp.concatenate(
            [jnp.where(lane_low == low, part, 0.0) for low in range(4)], axis=0
        ).astype(jnp.bfloat16)
        scores.append(
            lax.dot_general(
                left, key_ref[pl.ds(b * 128, 128), :], nt, preferred_element_type=jnp.float32
            )
        )
    for b in blocks:
        live.append(position < length_ref[pl.ds(b, 1), :])
        scores[b] = jnp.where(live[b], scores[b], neg_floor)
    quarter = lambda a, low: a[low * size : (low + 1) * size]
    widest = [
        jnp.maximum(
            jnp.maximum(quarter(a, 0), quarter(a, 1)), jnp.maximum(quarter(a, 2), quarter(a, 3))
        )
        for a in scores
    ]
    top = jnp.maximum(
        jnp.max(jnp.concatenate(widest, axis=0), axis=1, keepdims=True),
        jnp.max(new_scores, axis=1, keepdims=True),
    )
    weights = []
    for b in blocks:
        shift = jnp.broadcast_to(top[b * size : (b + 1) * size], (size, 128))
        shift = jnp.concatenate([shift] * 4, axis=0)
        weights.append(jnp.where(live[b], jnp.exp(scores[b] - shift), 0.0).astype(jnp.bfloat16))
    new_weight = jnp.where(mine, jnp.exp(new_scores - top), 0.0).astype(jnp.bfloat16)
    mixed = []
    for b in blocks:
        crossed = jnp.dot(
            weights[b], value_ref[pl.ds(b * 128, 128), :], preferred_element_type=jnp.float32
        )
        kept = quarter(crossed, 0)
        for low in range(1, 4):
            kept = jnp.where(lane_low == low, quarter(crossed, low), kept)
        mixed.append(kept)
    sums = []
    for b in blocks:
        wide = weights[b].astype(jnp.float32)
        sums.append((quarter(wide, 0) + quarter(wide, 1)) + (quarter(wide, 2) + quarter(wide, 3)))
    total = jnp.sum(jnp.concatenate(sums, axis=0), axis=1, keepdims=True) + jnp.sum(
        new_weight.astype(jnp.float32), axis=1, keepdims=True
    )
    mixed = jnp.concatenate(mixed, axis=0)
    high = mixed.astype(jnp.bfloat16)
    rest = (mixed - high.astype(jnp.float32)).astype(jnp.bfloat16)
    weighted = (
        lax.dot_general(high, select, nt, preferred_element_type=jnp.float32)
        + lax.dot_general(rest, select, nt, preferred_element_type=jnp.float32)
        + jnp.dot(new_weight, value_now, preferred_element_type=jnp.float32)
    )
    some = total > 0.0
    floor_total = jnp.where(some, total, 1.0)
    logsum = jnp.where(some, top + jnp.log(floor_total), neg_floor)
    result = weighted / floor_total
    pieces = stats_of(logsum)
    lane_head = iota((chunk, 128), 1) // 32
    for b in blocks:
        at = pl.ds(b * chunk, chunk)
        tail = None
        for h in range(local_heads):
            start = b * size + h * chunk
            target[at, h * 128 : (h + 1) * 128] = result[start : start + chunk]
            stat = pieces[start : start + chunk]
            tail = stat if tail is None else jnp.where(lane_head == h, stat, tail)
        target[at, 512:640] = tail


def stats_of(logsum):
    which = iota((128, 128), 1) % 32
    whole = jnp.broadcast_to(logsum, (128, 128))
    first = whole.astype(jnp.bfloat16).astype(jnp.float32)
    second = (whole - first).astype(jnp.bfloat16).astype(jnp.float32)
    third = whole - first - second
    return jnp.where(
        which == 0, first, jnp.where(which == 1, second, jnp.where(which == 2, third, 0.0))
    )


def pick_head(array, index):
    wide = array.astype(jnp.float32)
    return jnp.sum(jnp.where(iota(wide.shape, 1) == index, wide, 0.0), axis=1)


def own_kernel(
    lengths_hbm,
    queries_hbm,
    new_key_hbm,
    new_value_hbm,
    key_codes_hbm,
    key_scales_hbm,
    value_codes_hbm,
    value_scales_hbm,
    key_table_hbm,
    query_table_hbm,
    out_codes_hbm,
    out_scales_hbm,
    key_ref,
    value_ref,
    table_ref,
    now_ref,
    length_ref,
    select_ref,
    hadamard_ref,
    own_ref,
    out_codes_ref,
    out_scales_ref,
    lengths,
    queries,
    new_key,
    new_value,
    key_codes,
    key_scales,
    value_codes,
    value_scales,
    key_table,
    query_table,
    q_scratch,
    sems,
):
    rank = lax.axis_index("tensor")
    half = lax.rem(rank, 2)
    head = lax.div(rank, 2)
    pairs = [
        (key_codes_hbm, key_codes),
        (key_scales_hbm, key_scales),
        (key_table_hbm.at[half], key_table),
        (value_codes_hbm, value_codes),
        (value_scales_hbm, value_scales),
        (lengths_hbm, lengths),
        (query_table_hbm, query_table),
        (new_key_hbm, new_key),
        (new_value_hbm, new_value),
        (queries_hbm, queries),
        (out_codes_hbm, out_codes_ref),
        (out_scales_hbm, out_scales_ref),
    ]
    copies = [
        pltpu.make_async_copy(source, target, sems.at[i]) for i, (source, target) in enumerate(pairs)
    ]
    for copy in copies:
        copy.start()
    select_ref[...] = selector()
    hadamard_ref[...] = hadamard_pair()
    swap = swap_words()
    for copy in copies[:3]:
        copy.wait()
    scales = spread_scales(key_scales[...])
    for j, plane in enumerate(unpack_planes(key_codes[...])):
        partner = jnp.dot(plane.astype(jnp.bfloat16), swap, preferred_element_type=jnp.float32)
        lanes = slice(j * 128, (j + 1) * 128)
        shape = (rows, 16, 128)
        turned = (
            plane.reshape(shape) * key_table[0, :, lanes][None]
            + partner.reshape(shape) * key_table[1, :, lanes][None]
        ).reshape(512, 128)
        key_ref[:, lanes] = (turned * scales).astype(jnp.bfloat16)
    for copy in copies[3:5]:
        copy.wait()
    scales = spread_scales(value_scales[...]) * np.float32(1.0 / cache_step)
    for j, plane in enumerate(unpack_planes(value_codes[...])):
        value_ref[:, j * 128 : (j + 1) * 128] = (plane * scales).astype(jnp.bfloat16)
    for copy in copies[5:10]:
        copy.wait()
    for r in range(rows):
        table_ref[pl.ds(r, 1), :] = query_table[pl.ds(lengths[r], 1), :]
    cosine, sine = table_ref[:, :128], table_ref[:, 128:]
    key_now = rotate_rows(pick_head(new_key[...], head), cosine, sine).astype(jnp.bfloat16)
    value_now = pick_head(new_value[...], head).astype(jnp.bfloat16)
    now_ref[0] = key_now
    now_ref[1] = value_now
    lane_row = iota((1, 128), 1) // 16
    for b in range(rows // chunk):
        line = jnp.full((1, 128), lengths[b * chunk], jnp.int32)
        for i in range(1, chunk):
            line = jnp.where(lane_row >= i, lengths[b * chunk + i], line)
        length_ref[pl.ds(b, 1), :] = line
    attend(
        half,
        length_ref,
        rotate_queries(queries[...], q_scratch, table_ref),
        key_now,
        value_now,
        select_ref,
        key_ref,
        value_ref,
        own_ref,
    )
    for copy in copies[10:]:
        copy.wait()


def partner_kernel(
    q_ref,
    table_ref,
    now_ref,
    length_ref,
    select_ref,
    key_ref,
    value_ref,
    own_ref,
    out_ref,
    q_scratch,
    out_scratch,
):
    attend(
        lax.rem(lax.axis_index("tensor"), 2),
        length_ref,
        rotate_queries(q_ref[...], q_scratch, table_ref),
        now_ref[0],
        now_ref[1],
        select_ref,
        key_ref,
        value_ref,
        out_scratch,
    )
    out_ref[:, :640] = own_ref[...].astype(jnp.bfloat16)
    out_ref[:, 640:] = out_scratch[...].astype(jnp.bfloat16)


def combine_kernel(both_ref, out_ref, scratch):
    half = lax.rem(lax.axis_index("tensor"), 2)
    lane_head = iota((rows, 128), 1) // 32
    mine_ref, theirs_ref = both_ref.at[half], both_ref.at[1 - half]
    for own in range(2):
        at, other = own * 640, 640 - own * 640
        logs = [mine_ref[:, at + 512 : at + 640], theirs_ref[:, other + 512 : other + 640]]
        logs = [log.astype(jnp.float32) for log in logs]
        for h in range(local_heads):
            mine, theirs = [
                jnp.sum(jnp.where(lane_head == h, log, 0.0), axis=1, keepdims=True) for log in logs
            ]
            joint = jnp.maximum(mine, theirs)
            mine_factor = jnp.exp(mine - joint)
            their_factor = jnp.exp(theirs - joint)
            scale = 1.0 / (mine_factor + their_factor)
            block = mine_ref[:, at + h * 128 : at + (h + 1) * 128].astype(jnp.float32)
            other_block = theirs_ref[:, other + h * 128 : other + (h + 1) * 128].astype(jnp.float32)
            scratch[own, :, h * 128 : (h + 1) * 128] = block * (
                mine_factor * scale
            ) + other_block * (their_factor * scale)
    first = scratch[half].astype(jnp.bfloat16)
    second = scratch[1 - half].astype(jnp.bfloat16)
    out_ref[:, :512] = first
    out_ref[:, 512:] = second


def early_share():
    z = lax.axis_index("tensor")
    ring = lax.rem(z, 4)
    middle = jnp.logical_or(ring == 1, ring == 2)
    return jnp.where(z < 4, 8, jnp.where(middle, 2, 0))


def unpack_weight(first, last, codes_ref, scales_ref, weight_ref, scale_scratch):
    scale_scratch[...] = scales_ref[...].astype(jnp.float32) * np.float32(1.0 / weight_step)

    @pl.loop(first, last)
    def _(pair):
        for b in range(8):
            group = pair * 8 + b
            words = codes_ref[pl.ds(group * 32, 32), :]
            scale = jnp.broadcast_to(scale_scratch[pl.ds(group, 1), :], (32, 512)).astype(
                jnp.bfloat16
            )
            for k in range(4):
                power = 16.0**k
                plane = jnp.bitwise_and(words, 15 << 4 * k).astype(jnp.float32).astype(
                    jnp.bfloat16
                ) - jnp.bfloat16(code_offset * power)
                start = pair * 1024 + (b // 2) * 256 + k * 64 + (b % 2) * 32
                weight_ref[pl.ds(start, 32), :] = plane * (scale * jnp.bfloat16(1.0 / power))


def weight_kernel(codes_ref, scales_ref, weight_ref, scale_scratch):
    unpack_weight(0, early_share(), codes_ref, scales_ref, weight_ref, scale_scratch)


def project(gathered_ref, hadamard_ref, weight_ref, out_ref):
    hadamard = hadamard_ref[...]
    turned = [
        jnp.dot(
            gathered_ref[:, q * 256 : (q + 1) * 256], hadamard, preferred_element_type=jnp.float32
        )
        for q in range(4)
    ]
    start = [(i // 4 % 2 * 4 + i // 8) * rows for i in range(32)]
    blocks = [turned[i % 4][start[i] : start[i] + rows] for i in range(32)]
    for bit in range(5):
        step = 1 << bit
        blocks = [
            blocks[i] + blocks[i ^ step] if i & step == 0 else blocks[i ^ step] - blocks[i]
            for i in range(32)
        ]
    total = None
    for i in range(32):
        term = jnp.dot(
            blocks[i].astype(jnp.bfloat16),
            weight_ref[i * 256 : (i + 1) * 256, :],
            preferred_element_type=jnp.float32,
        )
        total = term if total is None else total + term
    out_ref[...] = (total * np.float32(8192.0**-0.5)).astype(jnp.bfloat16)


def project_kernel(
    gathered_ref, hadamard_ref, _, codes_ref, scales_ref, out_ref, weight_ref, scale_scratch
):
    unpack_weight(early_share(), 8, codes_ref, scales_ref, weight_ref, scale_scratch)
    project(gathered_ref, hadamard_ref, weight_ref, out_ref)


vmem = pl.BlockSpec(memory_space=pltpu.VMEM)
hbm = pl.BlockSpec(memory_space=pltpu.HBM)
params = pltpu.CompilerParams(vmem_limit_bytes=20 * 1024 * 1024)


def in_hbm(*arrays):
    return [pltpu.with_memory_space_constraint(array, pltpu.HBM) for array in arrays]


def per_device(
    queries,
    new_key,
    new_value,
    key_codes,
    key_scales,
    value_codes,
    value_scales,
    lengths,
    out_codes,
    out_scales,
):
    pairs = [(i, i ^ 1) for i in range(16)]
    f32, bf16, i32 = jnp.float32, jnp.bfloat16, jnp.int32
    shape = jax.ShapeDtypeStruct
    other_queries = lax.ppermute(queries, "tensor", pairs)
    outputs = pl.pallas_call(
        own_kernel,
        out_shape=(
            shape((512, 512), bf16),
            shape((512, 512), bf16),
            shape((rows, 256), f32),
            shape((2, rows, 128), bf16),
            shape((8, 128), i32),
            shape((128, 512), bf16),
            shape((256, 256), bf16),
            shape((rows, 640), f32),
            shape((2048, 512), i32),
            shape((64, 512), i32),
        ),
        in_specs=[hbm] * 12,
        out_specs=(vmem,) * 10,
        scratch_shapes=[
            pltpu.SMEM((rows,), i32),
            pltpu.VMEM((128, 128), bf16),
            pltpu.VMEM((rows, 8, 128), bf16),
            pltpu.VMEM((rows, 8, 128), bf16),
            pltpu.VMEM((512, 128), i32),
            pltpu.VMEM((rows, half_tokens), i32),
            pltpu.VMEM((512, 128), i32),
            pltpu.VMEM((rows, half_tokens), i32),
            pltpu.VMEM((2, 16, 512), f32),
            pltpu.VMEM((136, 256), f32),
            pltpu.VMEM((128, 128), f32),
            pltpu.SemaphoreType.DMA((12,)),
        ],
        compiler_params=params,
        cost_estimate=pl.CostEstimate(flops=400_000_000, bytes_accessed=14_000_000, transcendentals=0),
        name="own_heads",
    )(
        *in_hbm(
            lengths,
            queries.reshape(128, 128),
            new_key,
            new_value,
            key_codes.reshape(512, 128),
            key_scales.reshape(rows, half_tokens),
            value_codes.reshape(512, 128),
            value_scales.reshape(rows, half_tokens),
            jnp.asarray(key_tables()),
            jnp.asarray(query_table()),
            out_codes,
            out_scales,
        )
    )
    keys, values, table, now, length, select, hadamard, own, codes, scales = outputs
    sending = pl.pallas_call(
        partner_kernel,
        out_shape=shape((rows, 1280), bf16),
        in_specs=[vmem] * 8,
        out_specs=vmem,
        scratch_shapes=[pltpu.VMEM((128, 128), f32), pltpu.VMEM((rows, 640), f32)],
        compiler_params=params,
        name="other_heads",
    )(other_queries.reshape(128, 128), table, now, length, select, keys, values, own)
    both = lax.all_gather(
        sending, "tensor", axis=0, axis_index_groups=[[2 * a, 2 * a + 1] for a in range(8)]
    )
    scales, _ = lax.optimization_barrier((scales, both))
    weight = pl.pallas_call(
        weight_kernel,
        out_shape=shape((8192, 512), bf16),
        in_specs=[vmem] * 2,
        out_specs=vmem,
        scratch_shapes=[pltpu.VMEM((64, 512), f32)],
        compiler_params=params,
        cost_estimate=pl.CostEstimate(flops=20_000_000, bytes_accessed=12_000_000, transcendentals=0),
        name="unpack_weight",
    )(codes, scales)
    both, weight = lax.optimization_barrier((both, weight))
    attended = pl.pallas_call(
        combine_kernel,
        out_shape=shape((rows, 1024), bf16),
        in_specs=[vmem],
        out_specs=vmem,
        scratch_shapes=[pltpu.VMEM((2, rows, 512), f32)],
        compiler_params=params,
        name="combine_halves",
    )(both)
    strided = [[4 * k + i for k in range(4)] for i in range(4)]
    gathered = lax.all_gather(attended, "tensor", axis=0, tiled=True, axis_index_groups=strided)
    edges = [[2 * a + 1, (2 * a + 2) % 16] for a in range(8)]
    edges = [edge if a % 2 == 0 else edge[::-1] for a, edge in enumerate(edges)]
    gathered = lax.all_gather(gathered, "tensor", axis=0, tiled=True, axis_index_groups=edges)
    return pl.pallas_call(
        project_kernel,
        out_shape=(shape((rows, 512), bf16), shape((8192, 512), bf16)),
        in_specs=[vmem] * 5,
        out_specs=(vmem,) * 2,
        input_output_aliases={2: 1},
        scratch_shapes=[pltpu.VMEM((64, 512), f32)],
        compiler_params=params,
        name="project",
    )(gathered, hadamard, weight, codes, scales)[0]


def solution(mesh):
    return jax.shard_map(
        per_device,
        mesh=mesh,
        in_specs=(
            P("dp", "tensor", None),
            P("dp", None, None),
            P("dp", None, None),
            P("dp", "tensor", None),
            P("dp", "tensor", None),
            P("dp", "tensor", None),
            P("dp", "tensor", None),
            P("dp"),
            P(None, "tensor"),
            P(None, "tensor"),
        ),
        out_specs=P("dp", "tensor"),
        check_vma=False,
    )
```

```python
import functools

import jax
import jax.numpy as jnp
import numpy as np
from jax import lax
from jax.experimental import pallas as pl
from jax.experimental.pallas import tpu as pltpu
from jax.sharding import PartitionSpec as P

rope_base = 10000.0
neg_floor = -1e30
code_offset = 7.5
cache_step = 256.0
weight_step = 8192.0

rows = 32
head_width = 128
local_heads = 4
half_tokens = 64
chunk = 8
nt = (((1,), (1,)), ((), ()))


def rope_angles(positions):
    frequency = rope_base ** (-(np.arange(64) * 2.0 / head_width))
    return np.asarray(positions, np.float64)[..., None] * frequency


def key_tables():
    lane = np.arange(512)
    plane, low, word = lane // 128, lane % 128 // 32, lane % 32
    entry = 4 * word + plane
    position = 4 * np.arange(16)[:, None] + low[None, :]
    out = []
    for half in range(2):
        angle = rope_angles(np.arange(128))[half * half_tokens + position, (entry % 64)[None, :]]
        sign = np.where(entry < 64, -1.0, 1.0)
        scale = head_width**-0.5 / cache_step
        out.append(np.stack([np.cos(angle) * scale, np.sin(angle) * sign * scale]))
    return np.stack(out).astype(np.float32)


def query_table():
    angle = rope_angles(np.arange(136))
    return np.concatenate([np.cos(angle), np.cos(angle), -np.sin(angle), np.sin(angle)], -1).astype(
        np.float32
    )


def iota(shape, dim):
    return lax.broadcasted_iota(jnp.int32, shape, dim)


def one_hot(condition):
    return jnp.where(condition, 1.0, 0.0).astype(jnp.bfloat16)


def selector():
    shape = (128, 512)
    lane = iota(shape, 1)
    return one_hot(iota(shape, 0) == 4 * (lane % 32) + lane // 128)


def swap_words():
    shape = (128, 128)
    return one_hot(iota(shape, 0) == jnp.bitwise_xor(iota(shape, 1), 16))


def token_spread():
    return one_hot(iota((64, 128), 0) % 4 == iota((64, 128), 1) // 32)


def hadamard_pair():
    shape = (256, 256)
    column = iota(shape, 1)
    target = column // 32 % 2 * 128 + 4 * (column % 32) + column // 64
    both = jnp.bitwise_and(iota(shape, 0), target)
    for shift in (4, 2, 1):
        both = jnp.bitwise_xor(both, jnp.right_shift(both, shift))
    return (1.0 - 2.0 * jnp.bitwise_and(both, 1).astype(jnp.float32)).astype(jnp.bfloat16)


def unpack_planes(codes):
    return [
        jnp.bitwise_and(jnp.right_shift(codes, 4 * j), 15).astype(jnp.float32) - code_offset
        for j in range(4)
    ]


def spread_scales(scales):
    by_row = jnp.dot(
        one_hot(iota((512, rows), 0) // 16 == iota((512, rows), 1)),
        scales.astype(jnp.float32).astype(jnp.bfloat16),
        preferred_element_type=jnp.float32,
    )
    mine = iota((512, half_tokens), 1) // 4 == iota((512, half_tokens), 0) % 16
    kept = jnp.where(mine, by_row, 0.0).astype(jnp.bfloat16)
    return jnp.dot(kept, token_spread(), preferred_element_type=jnp.float32)


def rotate_rows(vectors, cosine, sine):
    return vectors * cosine + pltpu.roll(vectors, 64, 1) * sine


def rotate_queries(q, scratch, table_ref):
    scratch[...] = q.astype(jnp.float32)
    heads = [
        rotate_rows(
            scratch[pl.ds(h, rows, stride=local_heads), :], table_ref[:, :128], table_ref[:, 128:]
        )
        for h in range(local_heads)
    ]
    return jnp.concatenate(
        [
            heads[h][b * chunk : (b + 1) * chunk]
            for b in range(rows // chunk)
            for h in range(local_heads)
        ],
        axis=0,
    ).astype(jnp.bfloat16)


def attend(
    half, length_ref, q_rot, key_now, value_now, select_ref, key_ref, value_ref, target
):
    size = local_heads * chunk
    blocks = range(rows // chunk)
    select = select_ref[...]
    spread = jnp.dot(q_rot, select, preferred_element_type=jnp.float32)
    new_scores = lax.dot_general(
        q_rot, key_now, nt, preferred_element_type=jnp.float32
    ) * np.float32(head_width**-0.5)
    row = iota((128, rows), 0)
    mine = jnp.logical_and(iota((128, rows), 1) == row // size * chunk + row % chunk, half == 0)
    new_scores = jnp.where(mine, new_scores, neg_floor)
    lane_low = iota((1, 512), 1) % 128 // 32
    row = iota((4 * size, 128), 0)
    lane = iota((4 * size, 128), 1)
    position = jnp.where(
        row % chunk == lane // 16,
        half * half_tokens + 4 * (lane % 16) + row // size,
        1 << 20,
    )
    scores, live = [], []
    for b in blocks:
        part = spread[b * size : (b + 1) * size]
        left = jnp.concatenate(
            [jnp.where(lane_low == low, part, 0.0) for low in range(4)], axis=0
        ).astype(jnp.bfloat16)
        scores.append(
            lax.dot_general(
                left, key_ref[pl.ds(b * 128, 128), :], nt, preferred_element_type=jnp.float32
            )
        )
    for b in blocks:
        live.append(position < length_ref[pl.ds(b, 1), :])
        scores[b] = jnp.where(live[b], scores[b], neg_floor)
    quarter = lambda a, low: a[low * size : (low + 1) * size]
    widest = [
        jnp.maximum(
            jnp.maximum(quarter(a, 0), quarter(a, 1)), jnp.maximum(quarter(a, 2), quarter(a, 3))
        )
        for a in scores
    ]
    top = jnp.maximum(
        jnp.max(jnp.concatenate(widest, axis=0), axis=1, keepdims=True),
        jnp.max(new_scores, axis=1, keepdims=True),
    )
    weights = []
    for b in blocks:
        shift = jnp.broadcast_to(top[b * size : (b + 1) * size], (size, 128))
        shift = jnp.concatenate([shift] * 4, axis=0)
        weights.append(jnp.where(live[b], jnp.exp(scores[b] - shift), 0.0).astype(jnp.bfloat16))
    new_weight = jnp.where(mine, jnp.exp(new_scores - top), 0.0).astype(jnp.bfloat16)
    mixed = []
    for b in blocks:
        crossed = jnp.dot(
            weights[b], value_ref[pl.ds(b * 128, 128), :], preferred_element_type=jnp.float32
        )
        kept = quarter(crossed, 0)
        for low in range(1, 4):
            kept = jnp.where(lane_low == low, quarter(crossed, low), kept)
        mixed.append(kept)
    sums = []
    for b in blocks:
        wide = weights[b].astype(jnp.float32)
        sums.append((quarter(wide, 0) + quarter(wide, 1)) + (quarter(wide, 2) + quarter(wide, 3)))
    total = jnp.sum(jnp.concatenate(sums, axis=0), axis=1, keepdims=True) + jnp.sum(
        new_weight.astype(jnp.float32), axis=1, keepdims=True
    )
    mixed = jnp.concatenate(mixed, axis=0)
    high = mixed.astype(jnp.bfloat16)
    rest = (mixed - high.astype(jnp.float32)).astype(jnp.bfloat16)
    weighted = (
        lax.dot_general(high, select, nt, preferred_element_type=jnp.float32)
        + lax.dot_general(rest, select, nt, preferred_element_type=jnp.float32)
        + jnp.dot(new_weight, value_now, preferred_element_type=jnp.float32)
    )
    some = total > 0.0
    floor_total = jnp.where(some, total, 1.0)
    logsum = jnp.where(some, top + jnp.log(floor_total), neg_floor)
    result = weighted / floor_total
    pieces = stats_of(logsum)
    lane_head = iota((chunk, 128), 1) // 32
    for b in blocks:
        at = pl.ds(b * chunk, chunk)
        tail = None
        for h in range(local_heads):
            start = b * size + h * chunk
            target[at, h * 128 : (h + 1) * 128] = result[start : start + chunk]
            stat = pieces[start : start + chunk]
            tail = stat if tail is None else jnp.where(lane_head == h, stat, tail)
        target[at, 512:640] = tail


def stats_of(logsum):
    which = iota((128, 128), 1) % 32
    whole = jnp.broadcast_to(logsum, (128, 128))
    first = whole.astype(jnp.bfloat16).astype(jnp.float32)
    second = (whole - first).astype(jnp.bfloat16).astype(jnp.float32)
    third = whole - first - second
    return jnp.where(
        which == 0, first, jnp.where(which == 1, second, jnp.where(which == 2, third, 0.0))
    )


def pick_head(array, index):
    wide = array.astype(jnp.float32)
    return jnp.sum(jnp.where(iota(wide.shape, 1) == index, wide, 0.0), axis=1)


def own_kernel(
    lengths_hbm,
    queries_hbm,
    new_key_hbm,
    new_value_hbm,
    key_codes_hbm,
    key_scales_hbm,
    value_codes_hbm,
    value_scales_hbm,
    key_table_hbm,
    query_table_hbm,
    out_codes_hbm,
    out_scales_hbm,
    key_ref,
    value_ref,
    table_ref,
    now_ref,
    length_ref,
    select_ref,
    hadamard_ref,
    own_ref,
    out_codes_ref,
    out_scales_ref,
    lengths,
    queries,
    new_key,
    new_value,
    key_codes,
    key_scales,
    value_codes,
    value_scales,
    key_table,
    query_table,
    q_scratch,
    sems,
):
    rank = lax.axis_index("tensor")
    half = lax.rem(rank, 2)
    head = lax.div(rank, 2)
    pairs = [
        (key_codes_hbm, key_codes),
        (key_scales_hbm, key_scales),
        (key_table_hbm.at[half], key_table),
        (value_codes_hbm, value_codes),
        (value_scales_hbm, value_scales),
        (lengths_hbm, lengths),
        (query_table_hbm, query_table),
        (new_key_hbm, new_key),
        (new_value_hbm, new_value),
        (queries_hbm, queries),
        (out_codes_hbm, out_codes_ref),
        (out_scales_hbm, out_scales_ref),
    ]
    copies = [
        pltpu.make_async_copy(source, target, sems.at[i]) for i, (source, target) in enumerate(pairs)
    ]
    for copy in copies:
        copy.start()
    select_ref[...] = selector()
    hadamard_ref[...] = hadamard_pair()
    swap = swap_words()
    for copy in copies[:3]:
        copy.wait()
    scales = spread_scales(key_scales[...])
    for j, plane in enumerate(unpack_planes(key_codes[...])):
        partner = jnp.dot(plane.astype(jnp.bfloat16), swap, preferred_element_type=jnp.float32)
        lanes = slice(j * 128, (j + 1) * 128)
        shape = (rows, 16, 128)
        turned = (
            plane.reshape(shape) * key_table[0, :, lanes][None]
            + partner.reshape(shape) * key_table[1, :, lanes][None]
        ).reshape(512, 128)
        key_ref[:, lanes] = (turned * scales).astype(jnp.bfloat16)
    for copy in copies[3:5]:
        copy.wait()
    scales = spread_scales(value_scales[...]) * np.float32(1.0 / cache_step)
    for j, plane in enumerate(unpack_planes(value_codes[...])):
        value_ref[:, j * 128 : (j + 1) * 128] = (plane * scales).astype(jnp.bfloat16)
    for copy in copies[5:10]:
        copy.wait()
    for r in range(rows):
        table_ref[pl.ds(r, 1), :] = query_table[pl.ds(lengths[r], 1), :]
    cosine, sine = table_ref[:, :128], table_ref[:, 128:]
    key_now = rotate_rows(pick_head(new_key[...], head), cosine, sine).astype(jnp.bfloat16)
    value_now = pick_head(new_value[...], head).astype(jnp.bfloat16)
    now_ref[0] = key_now
    now_ref[1] = value_now
    lane_row = iota((1, 128), 1) // 16
    for b in range(rows // chunk):
        line = jnp.full((1, 128), lengths[b * chunk], jnp.int32)
        for i in range(1, chunk):
            line = jnp.where(lane_row >= i, lengths[b * chunk + i], line)
        length_ref[pl.ds(b, 1), :] = line
    attend(
        half,
        length_ref,
        rotate_queries(queries[...], q_scratch, table_ref),
        key_now,
        value_now,
        select_ref,
        key_ref,
        value_ref,
        own_ref,
    )
    for copy in copies[10:]:
        copy.wait()


def partner_kernel(
    q_ref,
    table_ref,
    now_ref,
    length_ref,
    select_ref,
    key_ref,
    value_ref,
    own_ref,
    out_ref,
    q_scratch,
    out_scratch,
):
    attend(
        lax.rem(lax.axis_index("tensor"), 2),
        length_ref,
        rotate_queries(q_ref[...], q_scratch, table_ref),
        now_ref[0],
        now_ref[1],
        select_ref,
        key_ref,
        value_ref,
        out_scratch,
    )
    out_ref[:, :640] = own_ref[...].astype(jnp.bfloat16)
    out_ref[:, 640:] = out_scratch[...].astype(jnp.bfloat16)


def combine_kernel(both_ref, out_ref, scratch):
    half = lax.rem(lax.axis_index("tensor"), 2)
    lane_head = iota((rows, 128), 1) // 32
    mine_ref, theirs_ref = both_ref.at[half], both_ref.at[1 - half]
    for own in range(2):
        at, other = own * 640, 640 - own * 640
        logs = [mine_ref[:, at + 512 : at + 640], theirs_ref[:, other + 512 : other + 640]]
        logs = [log.astype(jnp.float32) for log in logs]
        for h in range(local_heads):
            mine, theirs = [
                jnp.sum(jnp.where(lane_head == h, log, 0.0), axis=1, keepdims=True) for log in logs
            ]
            joint = jnp.maximum(mine, theirs)
            mine_factor = jnp.exp(mine - joint)
            their_factor = jnp.exp(theirs - joint)
            scale = 1.0 / (mine_factor + their_factor)
            block = mine_ref[:, at + h * 128 : at + (h + 1) * 128].astype(jnp.float32)
            other_block = theirs_ref[:, other + h * 128 : other + (h + 1) * 128].astype(jnp.float32)
            scratch[own, :, h * 128 : (h + 1) * 128] = block * (
                mine_factor * scale
            ) + other_block * (their_factor * scale)
    first = scratch[half].astype(jnp.bfloat16)
    second = scratch[1 - half].astype(jnp.bfloat16)
    out_ref[:, :512] = first
    out_ref[:, 512:] = second


def early_share():
    z = lax.axis_index("tensor")
    ring = lax.rem(z, 4)
    middle = jnp.logical_or(ring == 1, ring == 2)
    return jnp.where(z < 4, 8, jnp.where(middle, 2, 0))


def unpack_weight(first, last, codes_ref, scales_ref, weight_ref, scale_scratch):
    scale_scratch[...] = scales_ref[...].astype(jnp.float32) * np.float32(1.0 / weight_step)

    @pl.loop(first, last)
    def _(pair):
        for b in range(8):
            group = pair * 8 + b
            words = codes_ref[pl.ds(group * 32, 32), :]
            scale = jnp.broadcast_to(scale_scratch[pl.ds(group, 1), :], (32, 512)).astype(
                jnp.bfloat16
            )
            for k in range(4):
                power = 16.0**k
                plane = jnp.bitwise_and(words, 15 << 4 * k).astype(jnp.float32).astype(
                    jnp.bfloat16
                ) - jnp.bfloat16(code_offset * power)
                start = pair * 1024 + (b // 2) * 256 + k * 64 + (b % 2) * 32
                weight_ref[pl.ds(start, 32), :] = plane * (scale * jnp.bfloat16(1.0 / power))


def weight_kernel(codes_ref, scales_ref, weight_ref, scale_scratch):
    unpack_weight(0, early_share(), codes_ref, scales_ref, weight_ref, scale_scratch)


def project(gathered_ref, hadamard_ref, weight_ref, out_ref):
    hadamard = hadamard_ref[...]
    turned = [
        jnp.dot(
            gathered_ref[:, q * 256 : (q + 1) * 256], hadamard, preferred_element_type=jnp.float32
        )
        for q in range(4)
    ]
    start = [(i // 4 % 2 * 4 + i // 8) * rows for i in range(32)]
    blocks = [turned[i % 4][start[i] : start[i] + rows] for i in range(32)]
    for bit in range(5):
        step = 1 << bit
        blocks = [
            blocks[i] + blocks[i ^ step] if i & step == 0 else blocks[i ^ step] - blocks[i]
            for i in range(32)
        ]
    total = None
    for i in range(32):
        term = jnp.dot(
            blocks[i].astype(jnp.bfloat16),
            weight_ref[i * 256 : (i + 1) * 256, :],
            preferred_element_type=jnp.float32,
        )
        total = term if total is None else total + term
    out_ref[...] = (total * np.float32(8192.0**-0.5)).astype(jnp.bfloat16)


def project_kernel(
    gathered_ref, hadamard_ref, weight_ref, codes_ref, scales_ref, out_ref, late_weight, scale_scratch
):
    share = early_share()

    @pl.when(share == 8)
    def _():
        project(gathered_ref, hadamard_ref, weight_ref, out_ref)

    @pl.when(share < 8)
    def _():
        @pl.loop(0, share)
        def _(pair):
            part = pl.ds(pair * 1024, 1024)
            late_weight[part, :] = weight_ref[part, :]

        unpack_weight(share, 8, codes_ref, scales_ref, late_weight, scale_scratch)
        project(gathered_ref, hadamard_ref, late_weight, out_ref)


vmem = pl.BlockSpec(memory_space=pltpu.VMEM)
hbm = pl.BlockSpec(memory_space=pltpu.HBM)
params = pltpu.CompilerParams(vmem_limit_bytes=20 * 1024 * 1024)


def in_hbm(*arrays):
    return [pltpu.with_memory_space_constraint(array, pltpu.HBM) for array in arrays]


def per_device(
    queries,
    new_key,
    new_value,
    key_codes,
    key_scales,
    value_codes,
    value_scales,
    lengths,
    out_codes,
    out_scales,
):
    pairs = [(i, i ^ 1) for i in range(16)]
    f32, bf16, i32 = jnp.float32, jnp.bfloat16, jnp.int32
    shape = jax.ShapeDtypeStruct
    other_queries = lax.ppermute(queries, "tensor", pairs)
    outputs = pl.pallas_call(
        own_kernel,
        out_shape=(
            shape((512, 512), bf16),
            shape((512, 512), bf16),
            shape((rows, 256), f32),
            shape((2, rows, 128), bf16),
            shape((8, 128), i32),
            shape((128, 512), bf16),
            shape((256, 256), bf16),
            shape((rows, 640), f32),
            shape((2048, 512), i32),
            shape((64, 512), i32),
        ),
        in_specs=[hbm] * 12,
        out_specs=(vmem,) * 10,
        scratch_shapes=[
            pltpu.SMEM((rows,), i32),
            pltpu.VMEM((128, 128), bf16),
            pltpu.VMEM((rows, 8, 128), bf16),
            pltpu.VMEM((rows, 8, 128), bf16),
            pltpu.VMEM((512, 128), i32),
            pltpu.VMEM((rows, half_tokens), i32),
            pltpu.VMEM((512, 128), i32),
            pltpu.VMEM((rows, half_tokens), i32),
            pltpu.VMEM((2, 16, 512), f32),
            pltpu.VMEM((136, 256), f32),
            pltpu.VMEM((128, 128), f32),
            pltpu.SemaphoreType.DMA((12,)),
        ],
        compiler_params=params,
        cost_estimate=pl.CostEstimate(flops=400_000_000, bytes_accessed=14_000_000, transcendentals=0),
        name="own_heads",
    )(
        *in_hbm(
            lengths,
            queries.reshape(128, 128),
            new_key,
            new_value,
            key_codes.reshape(512, 128),
            key_scales.reshape(rows, half_tokens),
            value_codes.reshape(512, 128),
            value_scales.reshape(rows, half_tokens),
            jnp.asarray(key_tables()),
            jnp.asarray(query_table()),
            out_codes,
            out_scales,
        )
    )
    keys, values, table, now, length, select, hadamard, own, codes, scales = outputs
    sending = pl.pallas_call(
        partner_kernel,
        out_shape=shape((rows, 1280), bf16),
        in_specs=[vmem] * 8,
        out_specs=vmem,
        scratch_shapes=[pltpu.VMEM((128, 128), f32), pltpu.VMEM((rows, 640), f32)],
        compiler_params=params,
        name="other_heads",
    )(other_queries.reshape(128, 128), table, now, length, select, keys, values, own)
    both = lax.all_gather(
        sending, "tensor", axis=0, axis_index_groups=[[2 * a, 2 * a + 1] for a in range(8)]
    )
    scales, _ = lax.optimization_barrier((scales, both))
    weight = pl.pallas_call(
        weight_kernel,
        out_shape=shape((8192, 512), bf16),
        in_specs=[vmem] * 2,
        out_specs=vmem,
        scratch_shapes=[pltpu.VMEM((64, 512), f32)],
        compiler_params=params,
        cost_estimate=pl.CostEstimate(flops=20_000_000, bytes_accessed=12_000_000, transcendentals=0),
        name="unpack_weight",
    )(codes, scales)
    both, weight = lax.optimization_barrier((both, weight))
    attended = pl.pallas_call(
        combine_kernel,
        out_shape=shape((rows, 1024), bf16),
        in_specs=[vmem],
        out_specs=vmem,
        scratch_shapes=[pltpu.VMEM((2, rows, 512), f32)],
        compiler_params=params,
        name="combine_halves",
    )(both)
    strided = [[4 * k + i for k in range(4)] for i in range(4)]
    gathered = lax.all_gather(attended, "tensor", axis=0, tiled=True, axis_index_groups=strided)
    edges = [[2 * a + 1, (2 * a + 2) % 16] for a in range(8)]
    edges = [edge if a % 2 == 0 else edge[::-1] for a, edge in enumerate(edges)]
    gathered = lax.all_gather(gathered, "tensor", axis=0, tiled=True, axis_index_groups=edges)
    return pl.pallas_call(
        project_kernel,
        out_shape=shape((rows, 512), bf16),
        in_specs=[vmem] * 5,
        out_specs=vmem,
        scratch_shapes=[pltpu.VMEM((8192, 512), bf16), pltpu.VMEM((64, 512), f32)],
        compiler_params=params,
        name="project",
    )(gathered, hadamard, weight, codes, scales)


def solution(mesh):
    return jax.shard_map(
        per_device,
        mesh=mesh,
        in_specs=(
            P("dp", "tensor", None),
            P("dp", None, None),
            P("dp", None, None),
            P("dp", "tensor", None),
            P("dp", "tensor", None),
            P("dp", "tensor", None),
            P("dp", "tensor", None),
            P("dp"),
            P(None, "tensor"),
            P(None, "tensor"),
        ),
        out_specs=P("dp", "tensor"),
        check_vma=False,
    )
```

```python
import functools

import jax
import jax.numpy as jnp
import numpy as np
from jax import lax
from jax.experimental import pallas as pl
from jax.experimental.pallas import tpu as pltpu
from jax.sharding import PartitionSpec as P

rope_base = 10000.0
neg_floor = -1e30
code_offset = 7.5
cache_step = 256.0
weight_step = 8192.0

rows = 32
head_width = 128
local_heads = 4
half_tokens = 64
chunk = 8
nt = (((1,), (1,)), ((), ()))


def rope_angles(positions):
    frequency = rope_base ** (-(np.arange(64) * 2.0 / head_width))
    return np.asarray(positions, np.float64)[..., None] * frequency


def key_tables():
    lane = np.arange(512)
    plane, low, word = lane // 128, lane % 128 // 32, lane % 32
    entry = 4 * word + plane
    position = 4 * np.arange(16)[:, None] + low[None, :]
    out = []
    for half in range(2):
        angle = rope_angles(np.arange(128))[half * half_tokens + position, (entry % 64)[None, :]]
        sign = np.where(entry < 64, -1.0, 1.0)
        scale = head_width**-0.5 / cache_step
        out.append(np.stack([np.cos(angle) * scale, np.sin(angle) * sign * scale]))
    return np.stack(out).astype(np.float32)


def query_table():
    angle = rope_angles(np.arange(136))
    return np.concatenate([np.cos(angle), np.cos(angle), -np.sin(angle), np.sin(angle)], -1).astype(
        np.float32
    )


def iota(shape, dim):
    return lax.broadcasted_iota(jnp.int32, shape, dim)


def one_hot(condition):
    return jnp.where(condition, 1.0, 0.0).astype(jnp.bfloat16)


def selector():
    shape = (128, 512)
    lane = iota(shape, 1)
    return one_hot(iota(shape, 0) == 4 * (lane % 32) + lane // 128)


def swap_words():
    shape = (128, 128)
    return one_hot(iota(shape, 0) == jnp.bitwise_xor(iota(shape, 1), 16))


def token_spread():
    return one_hot(iota((64, 128), 0) % 4 == iota((64, 128), 1) // 32)


def hadamard_pair():
    shape = (256, 256)
    column = iota(shape, 1)
    target = column // 32 % 2 * 128 + 4 * (column % 32) + column // 64
    both = jnp.bitwise_and(iota(shape, 0), target)
    for shift in (4, 2, 1):
        both = jnp.bitwise_xor(both, jnp.right_shift(both, shift))
    return (1.0 - 2.0 * jnp.bitwise_and(both, 1).astype(jnp.float32)).astype(jnp.bfloat16)


def unpack_planes(codes):
    return [
        jnp.bitwise_and(jnp.right_shift(codes, 4 * j), 15).astype(jnp.float32) - code_offset
        for j in range(4)
    ]


def spread_scales(scales):
    by_row = jnp.dot(
        one_hot(iota((512, rows), 0) // 16 == iota((512, rows), 1)),
        scales.astype(jnp.float32).astype(jnp.bfloat16),
        preferred_element_type=jnp.float32,
    )
    mine = iota((512, half_tokens), 1) // 4 == iota((512, half_tokens), 0) % 16
    kept = jnp.where(mine, by_row, 0.0).astype(jnp.bfloat16)
    return jnp.dot(kept, token_spread(), preferred_element_type=jnp.float32)


def rotate_rows(vectors, cosine, sine):
    return vectors * cosine + pltpu.roll(vectors, 64, 1) * sine


def rotate_queries(q, scratch, table_ref):
    scratch[...] = q.astype(jnp.float32)
    heads = [
        rotate_rows(
            scratch[pl.ds(h, rows, stride=local_heads), :], table_ref[:, :128], table_ref[:, 128:]
        )
        for h in range(local_heads)
    ]
    return jnp.concatenate(
        [
            heads[h][b * chunk : (b + 1) * chunk]
            for b in range(rows // chunk)
            for h in range(local_heads)
        ],
        axis=0,
    ).astype(jnp.bfloat16)


def attend(
    half, length_ref, q_rot, key_now, value_now, select_ref, key_ref, value_ref, target
):
    size = local_heads * chunk
    blocks = range(rows // chunk)
    select = select_ref[...]
    spread = jnp.dot(q_rot, select, preferred_element_type=jnp.float32)
    new_scores = lax.dot_general(
        q_rot, key_now, nt, preferred_element_type=jnp.float32
    ) * np.float32(head_width**-0.5)
    row = iota((128, rows), 0)
    mine = jnp.logical_and(iota((128, rows), 1) == row // size * chunk + row % chunk, half == 0)
    new_scores = jnp.where(mine, new_scores, neg_floor)
    lane_low = iota((1, 512), 1) % 128 // 32
    row = iota((4 * size, 128), 0)
    lane = iota((4 * size, 128), 1)
    position = jnp.where(
        row % chunk == lane // 16,
        half * half_tokens + 4 * (lane % 16) + row // size,
        1 << 20,
    )
    scores, live = [], []
    for b in blocks:
        part = spread[b * size : (b + 1) * size]
        left = jnp.concatenate(
            [jnp.where(lane_low == low, part, 0.0) for low in range(4)], axis=0
        ).astype(jnp.bfloat16)
        scores.append(
            lax.dot_general(
                left, key_ref[pl.ds(b * 128, 128), :], nt, preferred_element_type=jnp.float32
            )
        )
    for b in blocks:
        live.append(position < length_ref[pl.ds(b, 1), :])
        scores[b] = jnp.where(live[b], scores[b], neg_floor)
    quarter = lambda a, low: a[low * size : (low + 1) * size]
    widest = [
        jnp.maximum(
            jnp.maximum(quarter(a, 0), quarter(a, 1)), jnp.maximum(quarter(a, 2), quarter(a, 3))
        )
        for a in scores
    ]
    top = jnp.maximum(
        jnp.max(jnp.concatenate(widest, axis=0), axis=1, keepdims=True),
        jnp.max(new_scores, axis=1, keepdims=True),
    )
    weights = []
    for b in blocks:
        shift = jnp.broadcast_to(top[b * size : (b + 1) * size], (size, 128))
        shift = jnp.concatenate([shift] * 4, axis=0)
        weights.append(jnp.where(live[b], jnp.exp(scores[b] - shift), 0.0).astype(jnp.bfloat16))
    new_weight = jnp.where(mine, jnp.exp(new_scores - top), 0.0).astype(jnp.bfloat16)
    mixed = []
    for b in blocks:
        crossed = jnp.dot(
            weights[b], value_ref[pl.ds(b * 128, 128), :], preferred_element_type=jnp.float32
        )
        kept = quarter(crossed, 0)
        for low in range(1, 4):
            kept = jnp.where(lane_low == low, quarter(crossed, low), kept)
        mixed.append(kept)
    sums = []
    for b in blocks:
        wide = weights[b].astype(jnp.float32)
        sums.append((quarter(wide, 0) + quarter(wide, 1)) + (quarter(wide, 2) + quarter(wide, 3)))
    total = jnp.sum(jnp.concatenate(sums, axis=0), axis=1, keepdims=True) + jnp.sum(
        new_weight.astype(jnp.float32), axis=1, keepdims=True
    )
    mixed = jnp.concatenate(mixed, axis=0)
    weighted = lax.dot_general(
        mixed.astype(jnp.bfloat16), select, nt, preferred_element_type=jnp.float32
    ) + jnp.dot(new_weight, value_now, preferred_element_type=jnp.float32)
    some = total > 0.0
    floor_total = jnp.where(some, total, 1.0)
    logsum = jnp.where(some, top + jnp.log(floor_total), neg_floor)
    result = weighted / floor_total
    pieces = stats_of(logsum)
    lane_head = iota((chunk, 128), 1) // 32
    for b in blocks:
        at = pl.ds(b * chunk, chunk)
        tail = None
        for h in range(local_heads):
            start = b * size + h * chunk
            target[at, h * 128 : (h + 1) * 128] = result[start : start + chunk]
            stat = pieces[start : start + chunk]
            tail = stat if tail is None else jnp.where(lane_head == h, stat, tail)
        target[at, 512:640] = tail


def stats_of(logsum):
    which = iota((128, 128), 1) % 32
    whole = jnp.broadcast_to(logsum, (128, 128))
    first = whole.astype(jnp.bfloat16).astype(jnp.float32)
    second = (whole - first).astype(jnp.bfloat16).astype(jnp.float32)
    third = whole - first - second
    return jnp.where(
        which == 0, first, jnp.where(which == 1, second, jnp.where(which == 2, third, 0.0))
    )


def pick_head(array, index):
    wide = array.astype(jnp.float32)
    return jnp.sum(jnp.where(iota(wide.shape, 1) == index, wide, 0.0), axis=1)


def own_kernel(
    lengths_hbm,
    queries_hbm,
    new_key_hbm,
    new_value_hbm,
    key_codes_hbm,
    key_scales_hbm,
    value_codes_hbm,
    value_scales_hbm,
    key_table_hbm,
    query_table_hbm,
    out_codes_hbm,
    out_scales_hbm,
    key_ref,
    value_ref,
    table_ref,
    now_ref,
    length_ref,
    select_ref,
    hadamard_ref,
    own_ref,
    out_codes_ref,
    out_scales_ref,
    lengths,
    queries,
    new_key,
    new_value,
    key_codes,
    key_scales,
    value_codes,
    value_scales,
    key_table,
    query_table,
    q_scratch,
    sems,
):
    rank = lax.axis_index("tensor")
    half = lax.rem(rank, 2)
    head = lax.div(rank, 2)
    pairs = [
        (key_codes_hbm, key_codes),
        (key_scales_hbm, key_scales),
        (key_table_hbm.at[half], key_table),
        (value_codes_hbm, value_codes),
        (value_scales_hbm, value_scales),
        (lengths_hbm, lengths),
        (query_table_hbm, query_table),
        (new_key_hbm, new_key),
        (new_value_hbm, new_value),
        (queries_hbm, queries),
        (out_codes_hbm, out_codes_ref),
        (out_scales_hbm, out_scales_ref),
    ]
    copies = [
        pltpu.make_async_copy(source, target, sems.at[i]) for i, (source, target) in enumerate(pairs)
    ]
    for copy in copies:
        copy.start()
    select_ref[...] = selector()
    hadamard_ref[...] = hadamard_pair()
    swap = swap_words()
    for copy in copies[:3]:
        copy.wait()
    scales = spread_scales(key_scales[...])
    for j, plane in enumerate(unpack_planes(key_codes[...])):
        partner = jnp.dot(plane.astype(jnp.bfloat16), swap, preferred_element_type=jnp.float32)
        lanes = slice(j * 128, (j + 1) * 128)
        shape = (rows, 16, 128)
        turned = (
            plane.reshape(shape) * key_table[0, :, lanes][None]
            + partner.reshape(shape) * key_table[1, :, lanes][None]
        ).reshape(512, 128)
        key_ref[:, lanes] = (turned * scales).astype(jnp.bfloat16)
    for copy in copies[3:5]:
        copy.wait()
    scales = spread_scales(value_scales[...]) * np.float32(1.0 / cache_step)
    for j, plane in enumerate(unpack_planes(value_codes[...])):
        value_ref[:, j * 128 : (j + 1) * 128] = (plane * scales).astype(jnp.bfloat16)
    for copy in copies[5:10]:
        copy.wait()
    for r in range(rows):
        table_ref[pl.ds(r, 1), :] = query_table[pl.ds(lengths[r], 1), :]
    cosine, sine = table_ref[:, :128], table_ref[:, 128:]
    key_now = rotate_rows(pick_head(new_key[...], head), cosine, sine).astype(jnp.bfloat16)
    value_now = pick_head(new_value[...], head).astype(jnp.bfloat16)
    now_ref[0] = key_now
    now_ref[1] = value_now
    lane_row = iota((1, 128), 1) // 16
    for b in range(rows // chunk):
        line = jnp.full((1, 128), lengths[b * chunk], jnp.int32)
        for i in range(1, chunk):
            line = jnp.where(lane_row >= i, lengths[b * chunk + i], line)
        length_ref[pl.ds(b, 1), :] = line
    attend(
        half,
        length_ref,
        rotate_queries(queries[...], q_scratch, table_ref),
        key_now,
        value_now,
        select_ref,
        key_ref,
        value_ref,
        own_ref,
    )
    for copy in copies[10:]:
        copy.wait()


def partner_kernel(
    q_ref,
    table_ref,
    now_ref,
    length_ref,
    select_ref,
    key_ref,
    value_ref,
    own_ref,
    out_ref,
    q_scratch,
    out_scratch,
):
    attend(
        lax.rem(lax.axis_index("tensor"), 2),
        length_ref,
        rotate_queries(q_ref[...], q_scratch, table_ref),
        now_ref[0],
        now_ref[1],
        select_ref,
        key_ref,
        value_ref,
        out_scratch,
    )
    out_ref[:, :640] = own_ref[...].astype(jnp.bfloat16)
    out_ref[:, 640:] = out_scratch[...].astype(jnp.bfloat16)


def combine_kernel(both_ref, out_ref, scratch):
    half = lax.rem(lax.axis_index("tensor"), 2)
    lane_head = iota((rows, 128), 1) // 32
    mine_ref, theirs_ref = both_ref.at[half], both_ref.at[1 - half]
    for own in range(2):
        at, other = own * 640, 640 - own * 640
        logs = [mine_ref[:, at + 512 : at + 640], theirs_ref[:, other + 512 : other + 640]]
        logs = [log.astype(jnp.float32) for log in logs]
        for h in range(local_heads):
            mine, theirs = [
                jnp.sum(jnp.where(lane_head == h, log, 0.0), axis=1, keepdims=True) for log in logs
            ]
            joint = jnp.maximum(mine, theirs)
            mine_factor = jnp.exp(mine - joint)
            their_factor = jnp.exp(theirs - joint)
            scale = 1.0 / (mine_factor + their_factor)
            block = mine_ref[:, at + h * 128 : at + (h + 1) * 128].astype(jnp.float32)
            other_block = theirs_ref[:, other + h * 128 : other + (h + 1) * 128].astype(jnp.float32)
            scratch[own, :, h * 128 : (h + 1) * 128] = block * (
                mine_factor * scale
            ) + other_block * (their_factor * scale)
    first = scratch[half].astype(jnp.bfloat16)
    second = scratch[1 - half].astype(jnp.bfloat16)
    out_ref[:, :512] = first
    out_ref[:, 512:] = second


def early_share():
    z = lax.axis_index("tensor")
    ring = lax.rem(z, 4)
    middle = jnp.logical_or(ring == 1, ring == 2)
    return jnp.where(z < 4, 8, jnp.where(middle, 2, 0))


def unpack_weight(first, last, codes_ref, scales_ref, weight_ref, scale_scratch):
    scale_scratch[...] = scales_ref[...].astype(jnp.float32) * np.float32(1.0 / weight_step)

    @pl.loop(first, last)
    def _(pair):
        for b in range(8):
            group = pair * 8 + b
            words = codes_ref[pl.ds(group * 32, 32), :]
            scale = jnp.broadcast_to(scale_scratch[pl.ds(group, 1), :], (32, 512)).astype(
                jnp.bfloat16
            )
            for k in range(4):
                power = 16.0**k
                plane = jnp.bitwise_and(words, 15 << 4 * k).astype(jnp.float32).astype(
                    jnp.bfloat16
                ) - jnp.bfloat16(code_offset * power)
                start = pair * 1024 + (b // 2) * 256 + k * 64 + (b % 2) * 32
                weight_ref[pl.ds(start, 32), :] = plane * (scale * jnp.bfloat16(1.0 / power))


def weight_kernel(codes_ref, scales_ref, weight_ref, scale_scratch):
    unpack_weight(0, early_share(), codes_ref, scales_ref, weight_ref, scale_scratch)


def project(gathered_ref, hadamard_ref, weight_ref, out_ref):
    hadamard = hadamard_ref[...]
    turned = [
        jnp.dot(
            gathered_ref[:, q * 256 : (q + 1) * 256], hadamard, preferred_element_type=jnp.float32
        )
        for q in range(4)
    ]
    start = [(i // 4 % 2 * 4 + i // 8) * rows for i in range(32)]
    blocks = [turned[i % 4][start[i] : start[i] + rows] for i in range(32)]
    for bit in range(5):
        step = 1 << bit
        blocks = [
            blocks[i] + blocks[i ^ step] if i & step == 0 else blocks[i ^ step] - blocks[i]
            for i in range(32)
        ]
    total = None
    for i in range(32):
        term = jnp.dot(
            blocks[i].astype(jnp.bfloat16),
            weight_ref[i * 256 : (i + 1) * 256, :],
            preferred_element_type=jnp.float32,
        )
        total = term if total is None else total + term
    out_ref[...] = (total * np.float32(8192.0**-0.5)).astype(jnp.bfloat16)


def project_kernel(
    gathered_ref, hadamard_ref, weight_ref, codes_ref, scales_ref, out_ref, late_weight, scale_scratch
):
    share = early_share()

    @pl.when(share == 8)
    def _():
        project(gathered_ref, hadamard_ref, weight_ref, out_ref)

    @pl.when(share < 8)
    def _():
        @pl.loop(0, share)
        def _(pair):
            part = pl.ds(pair * 1024, 1024)
            late_weight[part, :] = weight_ref[part, :]

        unpack_weight(share, 8, codes_ref, scales_ref, late_weight, scale_scratch)
        project(gathered_ref, hadamard_ref, late_weight, out_ref)


vmem = pl.BlockSpec(memory_space=pltpu.VMEM)
hbm = pl.BlockSpec(memory_space=pltpu.HBM)
params = pltpu.CompilerParams(vmem_limit_bytes=20 * 1024 * 1024)


def in_hbm(*arrays):
    return [pltpu.with_memory_space_constraint(array, pltpu.HBM) for array in arrays]


def per_device(
    queries,
    new_key,
    new_value,
    key_codes,
    key_scales,
    value_codes,
    value_scales,
    lengths,
    out_codes,
    out_scales,
):
    pairs = [(i, i ^ 1) for i in range(16)]
    f32, bf16, i32 = jnp.float32, jnp.bfloat16, jnp.int32
    shape = jax.ShapeDtypeStruct
    other_queries = lax.ppermute(queries, "tensor", pairs)
    outputs = pl.pallas_call(
        own_kernel,
        out_shape=(
            shape((512, 512), bf16),
            shape((512, 512), bf16),
            shape((rows, 256), f32),
            shape((2, rows, 128), bf16),
            shape((8, 128), i32),
            shape((128, 512), bf16),
            shape((256, 256), bf16),
            shape((rows, 640), f32),
            shape((2048, 512), i32),
            shape((64, 512), i32),
        ),
        in_specs=[hbm] * 12,
        out_specs=(vmem,) * 10,
        scratch_shapes=[
            pltpu.SMEM((rows,), i32),
            pltpu.VMEM((128, 128), bf16),
            pltpu.VMEM((rows, 8, 128), bf16),
            pltpu.VMEM((rows, 8, 128), bf16),
            pltpu.VMEM((512, 128), i32),
            pltpu.VMEM((rows, half_tokens), i32),
            pltpu.VMEM((512, 128), i32),
            pltpu.VMEM((rows, half_tokens), i32),
            pltpu.VMEM((2, 16, 512), f32),
            pltpu.VMEM((136, 256), f32),
            pltpu.VMEM((128, 128), f32),
            pltpu.SemaphoreType.DMA((12,)),
        ],
        compiler_params=params,
        cost_estimate=pl.CostEstimate(flops=400_000_000, bytes_accessed=14_000_000, transcendentals=0),
        name="own_heads",
    )(
        *in_hbm(
            lengths,
            queries.reshape(128, 128),
            new_key,
            new_value,
            key_codes.reshape(512, 128),
            key_scales.reshape(rows, half_tokens),
            value_codes.reshape(512, 128),
            value_scales.reshape(rows, half_tokens),
            jnp.asarray(key_tables()),
            jnp.asarray(query_table()),
            out_codes,
            out_scales,
        )
    )
    keys, values, table, now, length, select, hadamard, own, codes, scales = outputs
    sending = pl.pallas_call(
        partner_kernel,
        out_shape=shape((rows, 1280), bf16),
        in_specs=[vmem] * 8,
        out_specs=vmem,
        scratch_shapes=[pltpu.VMEM((128, 128), f32), pltpu.VMEM((rows, 640), f32)],
        compiler_params=params,
        name="other_heads",
    )(other_queries.reshape(128, 128), table, now, length, select, keys, values, own)
    both = lax.all_gather(
        sending, "tensor", axis=0, axis_index_groups=[[2 * a, 2 * a + 1] for a in range(8)]
    )
    scales, _ = lax.optimization_barrier((scales, both))
    weight = pl.pallas_call(
        weight_kernel,
        out_shape=shape((8192, 512), bf16),
        in_specs=[vmem] * 2,
        out_specs=vmem,
        scratch_shapes=[pltpu.VMEM((64, 512), f32)],
        compiler_params=params,
        cost_estimate=pl.CostEstimate(flops=20_000_000, bytes_accessed=12_000_000, transcendentals=0),
        name="unpack_weight",
    )(codes, scales)
    both, weight = lax.optimization_barrier((both, weight))
    attended = pl.pallas_call(
        combine_kernel,
        out_shape=shape((rows, 1024), bf16),
        in_specs=[vmem],
        out_specs=vmem,
        scratch_shapes=[pltpu.VMEM((2, rows, 512), f32)],
        compiler_params=params,
        name="combine_halves",
    )(both)
    strided = [[4 * k + i for k in range(4)] for i in range(4)]
    gathered = lax.all_gather(attended, "tensor", axis=0, tiled=True, axis_index_groups=strided)
    edges = [[2 * a + 1, (2 * a + 2) % 16] for a in range(8)]
    edges = [edge if a % 2 == 0 else edge[::-1] for a, edge in enumerate(edges)]
    gathered = lax.all_gather(gathered, "tensor", axis=0, tiled=True, axis_index_groups=edges)
    return pl.pallas_call(
        project_kernel,
        out_shape=shape((rows, 512), bf16),
        in_specs=[vmem] * 5,
        out_specs=vmem,
        scratch_shapes=[pltpu.VMEM((8192, 512), bf16), pltpu.VMEM((64, 512), f32)],
        compiler_params=params,
        name="project",
    )(gathered, hadamard, weight, codes, scales)


def solution(mesh):
    return jax.shard_map(
        per_device,
        mesh=mesh,
        in_specs=(
            P("dp", "tensor", None),
            P("dp", None, None),
            P("dp", None, None),
            P("dp", "tensor", None),
            P("dp", "tensor", None),
            P("dp", "tensor", None),
            P("dp", "tensor", None),
            P("dp"),
            P(None, "tensor"),
            P(None, "tensor"),
        ),
        out_specs=P("dp", "tensor"),
        check_vma=False,
    )
```
